128 devices in a mesh: dp: 8 (over z_lo, x), seq: 4 (over y), mp: 4 (over z_hi, core).
Axes of the slice: x: 4, y: 4, z: 4 (z_hi: 2, z_lo: 2; z = z_hi * 2 + z_lo), core: 2. Of those that a mesh axis runs over, the one named last changes fastest.
Arguments:
- hidden: bfloat16 [8, 1536, 8192], P('dp', 'seq', 'mp'), may hold values from -6 to 6
- gain: float32 [8192], replicated, may hold values from 0.5 to 1.5
- query_frozen_weight: bfloat16 [8192, 4096], P(('dp', 'seq'), 'mp'), may hold values from -1 to 1
- w_key: bfloat16 [8192, 512], P(('dp', 'seq'), 'mp'), may hold values from -1 to 1
- value_frozen_weight: bfloat16 [8192, 512], P(('dp', 'seq'), 'mp'), may hold values from -0.0625 to 0.0625
- a_query: bfloat16 [8192, 64], replicated, may hold values from -0.0625 to 0.0625
- query_up_weight: bfloat16 [64, 4096], P(None, 'mp'), may hold values from -0.75 to 0.75
- a_value: bfloat16 [8192, 64], replicated, may hold values from -0.0625 to 0.0625
- value_up_weight: bfloat16 [64, 512], P(None, 'mp'), may hold values from -0.75 to 0.75
- doc_ids: int32 [8, 1536], P('dp'), may hold values from 0 to 7, never falling along the last dimension, each value on 1 to 384 neighbouring positions
- d_out: bfloat16 [8, 1536, 4096], P('dp', 'seq', 'mp'), may hold values from -6 to 6
Outputs:
- attn_out: bfloat16 [8, 1536, 4096], P('dp', 'seq', 'mp')
- grad_a_query: float32 [8192, 64], P(('dp', 'seq', 'mp'))
- query_up_gradient: float32 [64, 4096], P(None, 'mp')
- grad_a_value: float32 [8192, 64], P(('dp', 'seq', 'mp'))
- value_up_gradient: float32 [64, 512], P(None, 'mp')
- grad_gain: float32 [8192], P('mp')
The draws below stay inside these ranges and needn't reach their ends.
Inputs may be any that keep to these rules, and one draw needn't show every extreme that they name: doc_ids never fall along a pack; each document has 1 to 384 tokens.
All inputs are finite; a program needn't handle non-finite values.
Results may differ from the reference program's by a relative error of at most 0.04.
Values may be sent and summed in bfloat16 or wider, within the bound.
No kernel may reach another device: no remote copies, remote signals or barrier semaphores. Data moves between devices by JAX's collectives and lax.ppermute only.
A program may use at most 192 MiB of HBM per device.

```python
import math
import jax
import jax.numpy as jnp
import numpy as np
from jax import lax

D = 8192
HD = 128
HEADS = 32
KV_HEADS = 4
RANK = 64
TOK_DEV = 384
GROUP = 384
PACKS = 8
SEQ_LEN = 1536
DOCS = 8


def draw_hidden(key, part):
    key = jax.random.fold_in(key, 11)
    noise_key = jax.random.fold_in(key, 0)
    values = jax.random.truncated_normal(noise_key, -6.0, 6.0, (PACKS, SEQ_LEN, D), jnp.float32)
    return values.astype(jnp.bfloat16)


def draw_query_frozen_weight(key, part):
    return projection_keyed(key, 12, HEADS * HD)


def draw_w_key(key, part):
    return projection_keyed(key, 13, KV_HEADS * HD)


def projection_keyed(key, salt, columns):
    own_key = jax.random.fold_in(key, salt)
    values = jax.random.truncated_normal(own_key, -6.0, 6.0, (D, columns), jnp.float32) * D ** (-0.5)
    return values.astype(jnp.bfloat16)


def block_levels(key, extent, cuts, least, top_value):
    level = 1.0
    for position, parts in cuts:
        heights = jax.random.uniform(jax.random.fold_in(jax.random.fold_in(key, 6), position), (parts,), jnp.float32, least / len(cuts), top_value / len(cuts))
        level = level * jnp.repeat(jnp.exp(heights), extent[position] // parts).reshape((-1,) + (1,) * (len(extent) - 1 - position))
    return level


def length_profile(number_of, total, reach, slope):
    portions = [(1 << 20) // math.isqrt(standing ** slope) + 1 for standing in range(2, number_of + 1)]
    rest, holding = total - reach - (number_of - 1), [1] * (number_of - 1)
    while rest > 0:
        movable = [i for i in range(number_of - 1) if holding[i] < reach]
        mass, remaining = sum([portions[i] for i in movable]), rest
        for i in movable:
            addition = min(reach - holding[i], max(1, remaining * portions[i] // mass), rest)
            holding[i] = holding[i] + addition
            rest = rest - addition
    return np.array([reach] + holding)


def ragged_sizes(key, number_of, total, limit, slope):
    if number_of == 2:
        one = jax.random.randint(key, (), max(1, total - limit), min(limit, total - 1) + 1)
        return jnp.stack([one, total - one])
    tallies = jnp.asarray(length_profile(number_of, total, limit, slope), jnp.int32)
    couples = (number_of - 1) // 2
    giver, taker = tallies[1:1 + 2 * couples:2], tallies[2:2 + 2 * couples:2]
    slack = jnp.minimum(giver - 1, limit - taker)
    moved = jax.random.randint(jax.random.fold_in(key, 1), (couples,), 0, 1 << 20) % (slack + 1)
    tallies = tallies.at[1:1 + 2 * couples:2].set(giver - moved).at[2:2 + 2 * couples:2].set(taker + moved)
    return tallies[jax.random.permutation(jax.random.fold_in(key, 2), number_of)]


def gaussian(key, dims, width, limit, cuts=(), kind=jnp.bfloat16):
    values = jax.random.normal(key, dims, jnp.float32) * width
    if len(cuts) > 0:
        values = block_levels(key, dims, cuts, -0.22, 0.18) * values
    return jnp.clip(values, min=-limit, max=limit).astype(kind)


def setup_inputs(seed: int = 0) -> dict:
    key_list = jax.random.split(jax.random.key(seed), 12)
    hidden = draw_hidden(jax.random.fold_in(key_list[11], 71), 0)
    gain = jnp.clip(1.0 + 0.1 * jax.random.normal(key_list[1], (D,), jnp.float32), 0.5, 1.5)
    query_frozen_weight = draw_query_frozen_weight(jax.random.fold_in(key_list[11], 71), 0)
    w_key = draw_w_key(jax.random.fold_in(key_list[11], 71), 0)
    value_frozen_weight = gaussian(key_list[4], (D, KV_HEADS * HD), D ** -0.5, 0.0625, ((0, 32), (1, 4)))
    a_query = gaussian(key_list[5], (D, RANK), D ** -0.5, 0.0625)
    query_up_weight = gaussian(key_list[6], (RANK, HEADS * HD), RANK ** -0.5, 0.75, ((1, 4),))
    a_value = gaussian(key_list[7], (D, RANK), D ** -0.5, 0.0625)
    value_up_weight = gaussian(key_list[8], (RANK, KV_HEADS * HD), RANK ** -0.5, 0.75, ((1, 4),))
    doc_ids = jax.vmap(lambda own: jnp.searchsorted(jnp.cumsum(ragged_sizes(own, DOCS, SEQ_LEN, TOK_DEV, 0)), jnp.arange(SEQ_LEN), side="right"))(jax.random.split(key_list[9], PACKS)).reshape((PACKS, SEQ_LEN)).astype(jnp.int32)
    d_out = gaussian(key_list[10], (PACKS, SEQ_LEN, HEADS * HD), 1.0, 6.0, ((0, 8), (1, 4), (2, 4)))
    return {"hidden": hidden, "gain": gain, "query_frozen_weight": query_frozen_weight, "w_key": w_key, "value_frozen_weight": value_frozen_weight, "a_query": a_query, "query_up_weight": query_up_weight, "a_value": a_value, "value_up_weight": value_up_weight, "doc_ids": doc_ids, "d_out": d_out}


EPS = 1e-05
ADAPTER_SCALE = 0.25
NEG_FILL = -1e+30

def attend_groups(queries, keys, values, grads, docs):
    widened_rows = jnp.float32
    scale = HD ** (-0.5)
    size = docs.shape[1]
    order = jnp.arange(size, dtype=jnp.int32)
    allowed = (docs[:, :, None] == docs[:, None, :]) & (order[:, None] >= order[None, :])
    allowed = allowed[:, None, None]
    scores = jnp.einsum('ngkqe,nske->nkqgs', queries.astype(widened_rows), keys.astype(widened_rows)) * scale
    scores = jnp.where(allowed, scores, NEG_FILL)
    peak = lax.optimization_barrier(jnp.max(scores, axis=-1, keepdims=True))
    expo = jnp.exp(scores - peak)
    probs = expo / lax.optimization_barrier(jnp.sum(expo, axis=-1, keepdims=True))
    probs_low = probs.astype(jnp.bfloat16)
    output = jnp.einsum('nkqgs,nske->ngkqe', probs_low.astype(widened_rows), values.astype(widened_rows)).astype(jnp.bfloat16)
    delta = lax.optimization_barrier(jnp.sum(grads.astype(widened_rows) * output.astype(widened_rows), axis=-1))
    dprob = jnp.einsum('ngkqe,nske->nkqgs', grads.astype(widened_rows), values.astype(widened_rows))
    dscore = probs * (dprob - jnp.transpose(delta, (0, 2, 3, 1))[..., None])
    dscore_low = dscore.astype(jnp.bfloat16)
    query_gradient = (jnp.einsum('nkqgs,nske->ngkqe', dscore_low.astype(widened_rows), keys.astype(widened_rows)) * scale).astype(jnp.bfloat16)
    dkey = jnp.einsum('nkqgs,ngkqe->nske', dscore_low.astype(widened_rows), queries.astype(widened_rows)) * scale
    value_gradient = jnp.einsum('nkqgs,ngkqe->nske', probs_low.astype(widened_rows), grads.astype(widened_rows))
    return (output, query_gradient, dkey, value_gradient)

def one_pack(items):
    query_rows_out, key, value_rows_out, grads, docs = items
    length = docs.shape[0]
    half = GROUP // 2
    per_kv = HEADS // KV_HEADS
    q_five = query_rows_out.reshape(length, KV_HEADS, per_kv, HD)
    g_five = grads.reshape(length, KV_HEADS, per_kv, HD)
    k_four = key.reshape(length, KV_HEADS, HD)
    v_four = value_rows_out.reshape(length, KV_HEADS, HD)
    groups = length // GROUP

    def split(array, count):
        return array.reshape((count, GROUP) + array.shape[1:])
    out_a, dq_a, dk_a, dv_a = attend_groups(split(q_five[:, :, 0::2], groups), split(k_four, groups), split(v_four, groups), split(g_five[:, :, 0::2], groups), split(docs, groups))
    out_a = out_a.reshape(length, KV_HEADS, per_kv // 2, HD)
    dq_a = dq_a.reshape(length, KV_HEADS, per_kv // 2, HD)
    dk_a = dk_a.reshape(length, KV_HEADS, HD)
    dv_a = dv_a.reshape(length, KV_HEADS, HD)
    pad_four = ((half, half), (0, 0), (0, 0), (0, 0))
    pad_three = ((half, half), (0, 0), (0, 0))
    q_pad = jnp.pad(q_five[:, :, 1::2], pad_four)
    g_pad = jnp.pad(g_five[:, :, 1::2], pad_four)
    k_pad = jnp.pad(k_four, pad_three)
    v_pad = jnp.pad(v_four, pad_three)
    d_pad = jnp.pad(docs, (half, half), constant_values=-1)
    out_b, dq_b, dk_b, dv_b = attend_groups(split(q_pad, groups + 1), split(k_pad, groups + 1), split(v_pad, groups + 1), split(g_pad, groups + 1), split(d_pad, groups + 1))
    out_b = out_b.reshape(length + GROUP, KV_HEADS, per_kv // 2, HD)[half:half + length]
    dq_b = dq_b.reshape(length + GROUP, KV_HEADS, per_kv // 2, HD)[half:half + length]
    dk_b = dk_b.reshape(length + GROUP, KV_HEADS, HD)[half:half + length]
    dv_b = dv_b.reshape(length + GROUP, KV_HEADS, HD)[half:half + length]
    output = jnp.stack([out_a, out_b], axis=3).reshape(length, HEADS * HD)
    query_gradient = jnp.stack([dq_a, dq_b], axis=3).reshape(length, HEADS * HD)
    dkey = (dk_a + dk_b).reshape(length, KV_HEADS * HD).astype(jnp.bfloat16)
    value_gradient = (dv_a + dv_b).reshape(length, KV_HEADS * HD).astype(jnp.bfloat16)
    return (output, query_gradient, dkey, value_gradient)

def reference(hidden, gain, query_frozen_weight, w_key, value_frozen_weight, a_query, query_up_weight, a_value, value_up_weight, doc_ids, d_out):
    widened_rows = jnp.float32
    raw = hidden.astype(widened_rows)
    scaled = raw * lax.rsqrt(lax.optimization_barrier(jnp.mean(raw * raw, axis=-1, keepdims=True)) + EPS)
    normed = (scaled * gain).astype(jnp.bfloat16)
    flattened_rows = normed.reshape(-1, D)
    query_low_rank = jnp.dot(flattened_rows, a_query, preferred_element_type=widened_rows).astype(jnp.bfloat16)
    value_low_rank = jnp.dot(flattened_rows, a_value, preferred_element_type=widened_rows).astype(jnp.bfloat16)
    query_rows_out = (jnp.dot(flattened_rows, query_frozen_weight, preferred_element_type=widened_rows) + ADAPTER_SCALE * jnp.dot(query_low_rank, query_up_weight, preferred_element_type=widened_rows)).astype(jnp.bfloat16)
    key = jnp.dot(flattened_rows, w_key, preferred_element_type=widened_rows).astype(jnp.bfloat16)
    value_rows_out = (jnp.dot(flattened_rows, value_frozen_weight, preferred_element_type=widened_rows) + ADAPTER_SCALE * jnp.dot(value_low_rank, value_up_weight, preferred_element_type=widened_rows)).astype(jnp.bfloat16)
    packs = hidden.shape[0]
    length = hidden.shape[1]
    output, query_gradient, dkey, value_gradient = lax.map(one_pack, (query_rows_out.reshape(packs, length, -1), key.reshape(packs, length, -1), value_rows_out.reshape(packs, length, -1), d_out, doc_ids))
    query_grad_matrix = query_gradient.reshape(-1, HEADS * HD)
    dk_flat = dkey.reshape(-1, KV_HEADS * HD)
    value_grad_matrix = value_gradient.reshape(-1, KV_HEADS * HD)
    query_up_gradient = ADAPTER_SCALE * jnp.dot(query_low_rank.T, query_grad_matrix, preferred_element_type=widened_rows)
    value_up_gradient = ADAPTER_SCALE * jnp.dot(value_low_rank.T, value_grad_matrix, preferred_element_type=widened_rows)
    query_rank_rows = (ADAPTER_SCALE * jnp.dot(query_grad_matrix, query_up_weight.T, preferred_element_type=widened_rows)).astype(jnp.bfloat16)
    value_rank_rows = (ADAPTER_SCALE * jnp.dot(value_grad_matrix, value_up_weight.T, preferred_element_type=widened_rows)).astype(jnp.bfloat16)
    grad_a_query = jnp.dot(flattened_rows.T, query_rank_rows, preferred_element_type=widened_rows)
    grad_a_value = jnp.dot(flattened_rows.T, value_rank_rows, preferred_element_type=widened_rows)
    d_normed = jnp.dot(query_grad_matrix, query_frozen_weight.T, preferred_element_type=widened_rows)
    d_normed = d_normed + jnp.dot(dk_flat, w_key.T, preferred_element_type=widened_rows)
    d_normed = d_normed + jnp.dot(value_grad_matrix, value_frozen_weight.T, preferred_element_type=widened_rows)
    d_normed = d_normed + jnp.dot(query_rank_rows, a_query.T, preferred_element_type=widened_rows)
    d_normed = d_normed + jnp.dot(value_rank_rows, a_value.T, preferred_element_type=widened_rows)
    grad_gain = lax.optimization_barrier(jnp.sum(d_normed * scaled.reshape(-1, D), axis=0))
    return (output, grad_a_query, query_up_gradient, grad_a_value, value_up_gradient, grad_gain)
```

```python
import jax
import jax.numpy as jnp
from jax import lax
from jax.experimental import pallas as pl
from jax.experimental.pallas import tpu as pltpu
from jax.sharding import PartitionSpec as P

HD = 128
EPS = 1e-05
ADAPTER_SCALE = 0.25
NEG_FILL = -1e30
BF = jnp.bfloat16
F32 = jnp.float32
VMEM_LIMIT = 56 * 1024 * 1024
REL = (0, -1, 1, 2)


def shift(value, axis, step):
    if axis == "x":
        route = [(z * 4 + i, z * 4 + (i + step) % 4) for z in range(2) for i in range(4)]
        return lax.ppermute(value, "dp", route)
    if axis == "zl":
        return lax.ppermute(value, "dp", [(i, (i + 4) % 8) for i in range(8)])
    if axis == "y":
        return lax.ppermute(value, "seq", [(i, (i + step) % 4) for i in range(4)])
    return lax.ppermute(value, "mp", [(i, i ^ step) for i in range(4)])


def ring(value, axis):
    half = value.shape[0] // 2
    before = shift(value, axis, 1)
    after = shift(value, axis, -1)
    return [
        value,
        before,
        after,
        shift(before[:half], axis, 1),
        shift(after[half:], axis, -1),
    ]


def gather_rows(shard, first, second):
    other = shift(shard, "zl", 1)
    inner = jnp.concatenate(ring(shard, first) + ring(other, first), axis=0)
    return ring(inner, second)


def shard_order(first, second, place):
    order = []
    for outer in REL:
        for flip in range(2):
            for inner in REL:
                at = dict(place)
                at[second] = (place[second] + outer) % 4
                at[first] = (place[first] + inner) % 4
                order.append((place["zl"] ^ flip) * 16 + at["x"] * 4 + at["y"])
    return jnp.stack(order).astype(jnp.int32)


def params(**kw):
    return pltpu.CompilerParams(vmem_limit_bytes=VMEM_LIMIT, **kw)


def normalise_kernel(
    loc1, loc2, id1, id2, h1, h2, inverse, gain1, gain2, a_rows, normed1, normed2, a_out
):
    inv = inverse[...]
    normed1[...] = (h1[...].astype(F32) * inv * gain1[0]).astype(BF)
    normed2[...] = (h2[...].astype(F32) * inv * gain2[0]).astype(BF)
    a_out[...] = a_rows[...]


def normalise(whole, inverse, gain, a_both, loc1, loc2, id1, id2):
    tokens, width = whole.shape
    shards = 32
    cols = width // shards
    gain3 = gain.reshape(shards, 1, cols)
    return pl.pallas_call(
        normalise_kernel,
        grid_spec=pltpu.PrefetchScalarGridSpec(
            num_scalar_prefetch=4,
            grid=(shards,),
            in_specs=[
                pl.BlockSpec((tokens, cols), lambda j, l1, l2, i1, i2: (0, l1[j])),
                pl.BlockSpec((tokens, cols), lambda j, l1, l2, i1, i2: (0, l2[j])),
                pl.BlockSpec((tokens, 1), lambda j, *_: (0, 0)),
                pl.BlockSpec((1, 1, cols), lambda j, l1, l2, i1, i2: (i1[j], 0, 0)),
                pl.BlockSpec((1, 1, cols), lambda j, l1, l2, i1, i2: (i2[j], 0, 0)),
                pl.BlockSpec((cols, 128), lambda j, l1, l2, i1, i2: (i1[j], 0)),
            ],
            out_specs=[
                pl.BlockSpec((tokens, cols), lambda j, *_: (0, j)),
                pl.BlockSpec((tokens, cols), lambda j, *_: (0, j)),
                pl.BlockSpec((cols, 128), lambda j, *_: (j, 0)),
            ],
        ),
        out_shape=[
            jax.ShapeDtypeStruct((tokens, width), BF),
            jax.ShapeDtypeStruct((tokens, width), BF),
            jax.ShapeDtypeStruct((width, 128), BF),
        ],
        compiler_params=params(),
        cost_estimate=pl.CostEstimate(
            flops=tokens * width * 4, bytes_accessed=tokens * width * 8, transcendentals=0
        ),
        name="normalise",
    )(loc1, loc2, id1, id2, whole, whole, inverse, gain3, gain3, a_both)


STARTS = (0, 2, 4, 6, 7)
COUNTS = (2, 2, 2, 1, 1)
STEP_ROWS = 1024


def block_specs(columns):
    def one(start, count):
        return pl.BlockSpec(
            (STEP_ROWS, columns), lambda j, *_: (jnp.clip(j - start, 0, count - 1), 0)
        )

    return [one(s, c) for s, c in zip(STARTS, COUNTS)]


def project_kernel(normed, low, up, b0, b1, b2, b3, b4, out, total):
    j = pl.program_id(0)

    @pl.when(j == 0)
    def _():
        total[...] = ADAPTER_SCALE * jnp.dot(low[...], up[...], preferred_element_type=F32)

    for block, start, count in zip((b0, b1, b2, b3, b4), STARTS, COUNTS):

        @pl.when((j >= start) & (j < start + count))
        def _():
            total[...] += jnp.dot(normed[...], block[...], preferred_element_type=F32)

    @pl.when(j == pl.num_programs(0) - 1)
    def _():
        out[...] = total[...].astype(BF)


def project(normed, low, up, blocks):
    tokens, width = normed.shape
    columns = up.shape[1]
    return pl.pallas_call(
        project_kernel,
        grid=(width // STEP_ROWS,),
        in_specs=[
            pl.BlockSpec((tokens, STEP_ROWS), lambda j: (0, j)),
            pl.BlockSpec(low.shape, lambda j: (0, 0)),
            pl.BlockSpec(up.shape, lambda j: (0, 0)),
        ]
        + block_specs(columns),
        out_specs=pl.BlockSpec((tokens, columns), lambda j: (0, 0)),
        out_shape=jax.ShapeDtypeStruct((tokens, columns), BF),
        scratch_shapes=[pltpu.VMEM((tokens, columns), F32)],
        compiler_params=params(),
        cost_estimate=pl.CostEstimate(
            flops=2 * tokens * width * columns,
            bytes_accessed=2 * width * (tokens + columns),
            transcendentals=0,
        ),
        name="project",
    )(normed, low, up, *blocks)


def gain_kernel(ids, normed, grads, b0, b1, b2, b3, b4, *rest):
    extra = rest[:-1]
    out = rest[-1]
    j = pl.program_id(0)
    per = STEP_ROWS // 256
    for block, start, count in zip((b0, b1, b2, b3, b4), STARTS, COUNTS):

        @pl.when((j >= start) & (j < start + count))
        def _():
            term = lax.dot_general(
                grads[...], block[...], (((1,), (1,)), ((), ())), preferred_element_type=F32
            )
            if extra:
                rank, a_rows = extra
                term = term + lax.dot_general(
                    rank[...], a_rows[...], (((1,), (1,)), ((), ())), preferred_element_type=F32
                )
            sums = jnp.sum(term * normed[...].astype(F32), axis=0, keepdims=True)
            for s in range(per):
                out[pl.ds(ids[j * per + s], 1), :] = sums[:, s * 256 : (s + 1) * 256]


def gain_part(ids, normed, grads, blocks, extra=()):
    tokens, width = normed.shape
    columns = grads.shape[1]
    specs = [
        pl.BlockSpec((tokens, STEP_ROWS), lambda j, *_: (0, j)),
        pl.BlockSpec(grads.shape, lambda j, *_: (0, 0)),
    ] + block_specs(columns)
    if extra:
        specs = specs + [
            pl.BlockSpec(extra[0].shape, lambda j, *_: (0, 0)),
            pl.BlockSpec((STEP_ROWS, 128), lambda j, *_: (j, 0)),
        ]
    return pl.pallas_call(
        gain_kernel,
        grid_spec=pltpu.PrefetchScalarGridSpec(
            num_scalar_prefetch=1,
            grid=(width // STEP_ROWS,),
            in_specs=specs,
            out_specs=pl.BlockSpec((32, 256), lambda j, *_: (0, 0)),
        ),
        out_shape=jax.ShapeDtypeStruct((32, 256), F32),
        compiler_params=params(),
        cost_estimate=pl.CostEstimate(
            flops=2 * tokens * width * columns,
            bytes_accessed=2 * width * (tokens + columns),
            transcendentals=0,
        ),
        name="gain_part",
    )(ids, normed, grads, *blocks, *extra)


def attend_kernel(
    q_head, q_tail, kv, prev, grads, docs_col, docs_row, out, dq, dkv, dprev, dk, dv, dkp, dvp
):
    tokens = kv.shape[0]
    half = tokens // 2
    scale = HD ** (-0.5)
    heads = grads.shape[1] // HD
    lead = q_head.shape[1] // HD - 2
    own_col = docs_col[...]
    ext_row = docs_row[...]

    def causal(rows, columns, ahead):
        row = lax.broadcasted_iota(jnp.int32, (rows, columns), 0)
        column = lax.broadcasted_iota(jnp.int32, (rows, columns), 1)
        return row + ahead >= column

    plain = (own_col == ext_row[:, half:]) & causal(tokens, tokens, 0)
    early = (own_col[:half] == ext_row[:, :tokens]) & causal(half, tokens, half)
    late = (own_col[half:] == ext_row[:, tokens:]) & causal(half, half, 0)
    k_own, v_own = kv[:, :HD], kv[:, HD:]
    k_early = jnp.concatenate([prev[:, :HD], k_own[:half]], axis=0)
    v_early = jnp.concatenate([prev[:, HD:], v_own[:half]], axis=0)
    k_late, v_late = k_own[half:], v_own[half:]

    def attend(queries, keys, values, cot, allowed):
        scores = (
            lax.dot_general(
                queries, keys, (((1,), (1,)), ((), ())), preferred_element_type=F32
            )
            * scale
        )
        scores = jnp.where(allowed, scores, NEG_FILL)
        expo = jnp.exp(scores - jnp.max(scores, axis=1, keepdims=True))
        probs = expo * (1.0 / jnp.sum(expo, axis=1, keepdims=True))
        probs_low = probs.astype(BF)
        output = jnp.dot(probs_low, values, preferred_element_type=F32).astype(BF)
        delta = jnp.sum(cot.astype(F32) * output.astype(F32), axis=1, keepdims=True)
        dprob = lax.dot_general(
            cot, values, (((1,), (1,)), ((), ())), preferred_element_type=F32
        )
        dscore = (probs * (dprob - delta)).astype(BF)
        dquery = (jnp.dot(dscore, keys, preferred_element_type=F32) * scale).astype(BF)
        dkey = lax.dot_general(
            dscore, queries, (((0,), (0,)), ((), ())), preferred_element_type=F32
        )
        dvalue = lax.dot_general(
            probs_low, cot, (((0,), (0,)), ((), ())), preferred_element_type=F32
        )
        return output, dquery, dkey, dvalue

    dk[...] = jnp.zeros_like(dk)
    dv[...] = jnp.zeros_like(dv)
    dkp[...] = jnp.zeros_like(dkp)
    dvp[...] = jnp.zeros_like(dvp)
    for h in range(heads):
        at = slice(h * HD, (h + 1) * HD)
        if h < lead:
            queries = q_head[:, (h + 2) * HD : (h + 3) * HD]
        else:
            queries = q_tail[:, (h - lead) * HD : (h - lead + 1) * HD]
        cot = grads[:, at]
        if h % 2 == 0:
            o, g, a, b = attend(queries, k_own, v_own, cot, plain)
            out[:, at] = o
            dq[:, at] = g
            dk[...] += a
            dv[...] += b
        else:
            o, g, a, b = attend(queries[:half], k_early, v_early, cot[:half], early)
            out[:half, at] = o
            dq[:half, at] = g
            dkp[...] += a[:half]
            dvp[...] += b[:half]
            dk[:half] += a[half:]
            dv[:half] += b[half:]
            o, g, a, b = attend(queries[half:], k_late, v_late, cot[half:], late)
            out[half:, at] = o
            dq[half:, at] = g
            dk[half:] += a
            dv[half:] += b
    dkv[:, :HD] = dk[...] * scale
    dkv[:, HD:] = dv[...]
    dprev[:, :HD] = (dkp[...] * scale).astype(BF)
    dprev[:, HD:] = dvp[...].astype(BF)


def attend(q_head, q_tail, kv, prev, grads, docs_col, docs_row):
    tokens, columns = grads.shape
    half = tokens // 2
    return pl.pallas_call(
        attend_kernel,
        out_shape=[
            jax.ShapeDtypeStruct((tokens, columns), BF),
            jax.ShapeDtypeStruct((tokens, columns), BF),
            jax.ShapeDtypeStruct((tokens, 2 * HD), F32),
            jax.ShapeDtypeStruct((half, 2 * HD), BF),
        ],
        scratch_shapes=[
            pltpu.VMEM((tokens, HD), F32),
            pltpu.VMEM((tokens, HD), F32),
            pltpu.VMEM((half, HD), F32),
            pltpu.VMEM((half, HD), F32),
        ],
        compiler_params=params(),
        cost_estimate=pl.CostEstimate(
            flops=2 * 5 * tokens * tokens * columns,
            bytes_accessed=2 * tokens * columns * 4,
            transcendentals=tokens * tokens * columns // HD,
        ),
        name="attend",
    )(q_head, q_tail, kv, prev, grads, docs_col, docs_row)


def dot_rows(left, right):
    return lax.dot_general(left, right, (((0,), (0,)), ((), ())), preferred_element_type=F32)


def dot_cols(left, right):
    return lax.dot_general(left, right, (((1,), (1,)), ((), ())), preferred_element_type=F32)


def ring_sum(value, axis):
    low = value.astype(BF)
    total = value
    for step in (1, -1, 2):
        total = total + shift(low, axis, step).astype(F32)
    return total


def sum_everywhere(value):
    value = ring_sum(value, "x")
    value = ring_sum(value, "y")
    return value + shift(value.astype(BF), "zl", 1).astype(F32)


def sum_heads(value):
    low = value.astype(BF)
    total = value
    for step in (1, 2, 3):
        total = total + shift(low, "mp", step).astype(F32)
    return total


def per_device(
    hidden,
    gain,
    query_frozen_weight,
    w_key,
    value_frozen_weight,
    a_query,
    query_up_weight,
    a_value,
    value_up_weight,
    doc_ids,
    d_out,
):
    tokens = hidden.shape[1]
    half = tokens // 2
    dp, seq, mp = lax.axis_index("dp"), lax.axis_index("seq"), lax.axis_index("mp")
    place = {"zl": dp // 4, "x": dp % 4, "y": seq}
    own = hidden[0]
    weights1 = jnp.concatenate(
        [w_key, value_frozen_weight, query_frozen_weight[:, : 3 * HD]], axis=1
    )
    weights2 = query_frozen_weight[:, 3 * HD :]
    h_zh = shift(own, "mp", 2)
    whole = jnp.concatenate([own, shift(own, "mp", 1), h_zh, shift(h_zh, "mp", 1)], axis=1)
    blocks1 = gather_rows(weights1, "x", "y")
    blocks2 = gather_rows(weights2, "y", "x")

    whole_wide = whole.astype(F32)
    inverse = lax.rsqrt(jnp.mean(whole_wide * whole_wide, axis=1, keepdims=True) + EPS)
    id1 = shard_order("x", "y", place)
    id2 = shard_order("y", "x", place)
    loc1 = ((id1 // 8) ^ mp) * 8 + id1 % 8
    loc2 = ((id2 // 8) ^ mp) * 8 + id2 % 8
    a_both = jnp.concatenate([a_query, a_value], axis=1)
    normed1, normed2, a_rows = normalise(whole, inverse, gain, a_both, loc1, loc2, id1, id2)
    low = jnp.dot(normed1, a_rows, preferred_element_type=F32).astype(BF)
    rank = query_up_weight.shape[0]
    up1 = jnp.concatenate(
        [
            jnp.concatenate(
                [jnp.zeros((rank, 2 * HD), BF), query_up_weight[:, : 3 * HD]], axis=1
            ),
            jnp.concatenate(
                [jnp.zeros((rank, HD), BF), value_up_weight, jnp.zeros((rank, 3 * HD), BF)], axis=1
            ),
        ],
        axis=0,
    )
    up2 = jnp.concatenate([query_up_weight[:, 3 * HD :], jnp.zeros((rank, 5 * HD), BF)], axis=0)
    part1 = project(normed1, low, up1, blocks1)
    kv = part1[:, : 2 * HD]
    prev = lax.ppermute(kv[half:], "seq", [(i, i + 1) for i in range(3)])
    part2 = project(normed2, low, up2, blocks2)

    docs = doc_ids[0]
    begin = seq * tokens
    own_docs = lax.dynamic_slice_in_dim(docs, begin, tokens)
    prev_docs = lax.dynamic_slice_in_dim(docs, jnp.maximum(begin - half, 0), half)
    prev_docs = jnp.where(seq > 0, prev_docs, -1)
    ext_docs = jnp.concatenate([prev_docs, own_docs])
    output, dq, dkv, dprev = attend(
        part1, part2, kv, prev, d_out[0], own_docs[:, None], ext_docs[None, :]
    )
    returned = lax.ppermute(dprev, "seq", [(i + 1, i) for i in range(3)]).astype(F32)
    dkv = jnp.concatenate([dkv[:half], dkv[half:] + returned], axis=0).astype(BF)
    dvalue = dkv[:, HD:]
    ranks = jnp.concatenate(
        [dot_cols(dq, query_up_weight), dot_cols(dvalue, value_up_weight)], axis=1
    )
    ranks = ADAPTER_SCALE * ranks
    rank_rows = sum_heads(ranks).astype(BF)
    grads1 = jnp.concatenate([dkv, dq[:, : 3 * HD]], axis=1)
    gain_sum = gain_part(id1, normed1, grads1, blocks1, (ranks.astype(BF), a_rows)) + gain_part(
        id2, normed2, dq[:, 3 * HD :], blocks2
    )

    up_grads = ADAPTER_SCALE * jnp.concatenate(
        [dot_rows(low[:, :rank], dq), dot_rows(low[:, rank:], dvalue)], axis=1
    )
    up_grads = sum_everywhere(up_grads)

    grad_a = dot_rows(normed1, rank_rows).reshape(32, 4, 64, 2 * rank)
    grad_a = lax.dynamic_index_in_dim(grad_a, mp, 1, keepdims=False)
    grad_a = grad_a.reshape(4, 8, 64, 2 * rank)
    total = grad_a[0]
    for i in (1, 2, 3):
        total = total + shift(grad_a[i].astype(BF), "y", REL[i]).astype(F32)
    grad_a = total.reshape(2, 4, 64, 2 * rank)
    total = grad_a[:, 0]
    for i in (1, 2, 3):
        total = total + shift(grad_a[:, i].astype(BF), "x", REL[i]).astype(F32)
    grad_a = total[0] + shift(total[1].astype(BF), "zl", 1).astype(F32)

    gain_sum = sum_heads(gain_sum)
    gain_sum = lax.dynamic_slice_in_dim(gain_sum, mp * 8, 8, 0)
    gain_sum = sum_everywhere(gain_sum).reshape(-1)
    gain_own = lax.dynamic_slice_in_dim(gain, mp * gain_sum.shape[0], gain_sum.shape[0])
    columns = query_up_weight.shape[1]
    return (
        output[None],
        grad_a[:, :rank],
        up_grads[:, :columns],
        grad_a[:, rank:],
        up_grads[:, columns:],
        gain_sum / gain_own,
    )


def solution(mesh):
    return jax.shard_map(
        per_device,
        mesh=mesh,
        in_specs=(
            P("dp", "seq", "mp"),
            P(),
            P(("dp", "seq"), "mp"),
            P(("dp", "seq"), "mp"),
            P(("dp", "seq"), "mp"),
            P(),
            P(None, "mp"),
            P(),
            P(None, "mp"),
            P("dp", None),
            P("dp", "seq", "mp"),
        ),
        out_specs=(
            P("dp", "seq", "mp"),
            P(("dp", "seq", "mp"), None),
            P(None, "mp"),
            P(("dp", "seq", "mp"), None),
            P(None, "mp"),
            P("mp"),
        ),
        check_vma=False,
    )
```

```python
import functools

import jax
import jax.numpy as jnp
from jax import lax
from jax.experimental import pallas as pl
from jax.experimental.pallas import tpu as pltpu
from jax.sharding import PartitionSpec as P

HD = 128
EPS = 1e-05
ADAPTER_SCALE = 0.25
NEG_FILL = -1e30
BF = jnp.bfloat16
F32 = jnp.float32
VMEM_LIMIT = 56 * 1024 * 1024
REL = (0, -1, 1, 2)
ROWS = 512


def shift(value, axis, step):
    if axis == "x":
        route = [(z * 4 + i, z * 4 + (i + step) % 4) for z in range(2) for i in range(4)]
        return lax.ppermute(value, "dp", route)
    if axis == "zl":
        return lax.ppermute(value, "dp", [(i, (i + 4) % 8) for i in range(8)])
    if axis == "y":
        return lax.ppermute(value, "seq", [(i, (i + step) % 4) for i in range(4)])
    return lax.ppermute(value, "mp", [(i, i ^ step) for i in range(4)])


def shift_plane(value, stage, step):
    route = []
    for z in range(2):
        for x in range(4):
            for y in range(4):
                for m in range(4):
                    to_x, to_y = x, y
                    if (m < 2) == (stage == 0):
                        to_y = (y + step) % 4
                    else:
                        to_x = (x + step) % 4
                    route.append(
                        (((z * 4 + x) * 4 + y) * 4 + m, ((z * 4 + to_x) * 4 + to_y) * 4 + m)
                    )
    return lax.ppermute(value, ("dp", "seq", "mp"), route)


def params(**kw):
    return pltpu.CompilerParams(vmem_limit_bytes=VMEM_LIMIT, **kw)


def any_specs(count):
    return [pl.BlockSpec(memory_space=pl.ANY)] * count


def vmem_specs(count):
    return [pl.BlockSpec(memory_space=pltpu.VMEM)] * count


def assemble_kernel(*refs):
    pieces, outs, sems = refs[:8], refs[8:10], refs[10]
    rows = pieces[0].shape[0]
    copies = [
        pltpu.make_async_copy(piece, outs[k // 4].at[pl.ds(k % 4 * rows, rows)], sems.at[k])
        for k, piece in enumerate(pieces)
    ]
    for copy in copies:
        copy.start()
    for copy in copies:
        copy.wait()


def assemble(pieces):
    rows, columns = pieces[0].shape
    return pl.pallas_call(
        assemble_kernel,
        in_specs=any_specs(8),
        out_specs=any_specs(2),
        out_shape=[jax.ShapeDtypeStruct((4 * rows, columns), BF)] * 2,
        scratch_shapes=[pltpu.SemaphoreType.DMA((8,))],
        compiler_params=params(),
        cost_estimate=pl.CostEstimate(
            flops=0, bytes_accessed=32 * rows * columns, transcendentals=0
        ),
        name="assemble",
    )(*pieces)


def gather_rows(shard):
    half = shard.shape[0] // 2
    pieces = []
    for part, axis in ((shard[:half], "x"), (shard[half:], "y")):
        pieces += [part] + [shift(part, axis, -step) for step in REL[1:]]
    blocks = []
    for inner, axis in zip(assemble(pieces), ("y", "x")):
        other = shift(inner, "zl", 1)
        before, after = shift(inner, axis, 1), shift(inner, axis, -1)
        before_other, after_other = shift(other, axis, 1), shift(other, axis, -1)
        blocks.append(
            [inner, other, before, before_other, after, after_other]
            + [shift(before, axis, 1), shift(after_other, axis, -1)]
        )
    return blocks


def block_places(dp, seq, mp):
    at = jnp.arange(64, dtype=jnp.int32)
    number = ((at // 16) ^ mp) * 16 + at % 16
    order, shard = number % 2, number // 2
    inverse = jnp.array([0, 2, 3, 1], jnp.int32)
    flip = (shard // 16) ^ (dp // 4)
    by_x = inverse[(shard // 4 % 4 - dp) % 4]
    by_y = inverse[(shard % 4 - seq) % 4]
    outer = jnp.where(order == 0, by_y, by_x)
    inner = jnp.where(order == 0, by_x, by_y)
    place = order * 32 + outer * 8 + flip * 4 + inner
    number_at = jnp.zeros((64,), jnp.int32).at[place].set(number)
    return number, place, number_at


def prepare_kernel(number, place, h0, h1, h2, h3, gain, a_both, normed, a_rows, low, square, inv):
    parts = (h0, h1, h2, h3)
    per = h0.shape[1] // 128
    square[...] = jnp.zeros_like(square)
    for part in parts:

        @pl.loop(0, per)
        def _(i):
            value = part[:, pl.ds(pl.multiple_of(i * 128, 128), 128)].astype(F32)
            square[...] += value * value

    width = normed.shape[1]
    mean = jnp.sum(square[...], axis=1, keepdims=True) * (1.0 / width)
    inv[...] = jnp.broadcast_to(lax.rsqrt(mean + EPS), inv.shape)
    for r, part in enumerate(parts):

        @pl.loop(0, per)
        def _(i):
            source = pl.multiple_of(number[r * per + i] * 128, 128)
            target = pl.multiple_of(place[r * per + i] * 128, 128)
            value = part[:, pl.ds(pl.multiple_of(i * 128, 128), 128)].astype(F32)
            scaled = value * inv[...]
            normed[:, pl.ds(target, 128)] = (scaled * gain[pl.ds(number[r * per + i], 1), :]).astype(BF)
            a_rows[pl.ds(target, 128), :] = a_both[pl.ds(source, 128), :]

    square[...] = jnp.zeros_like(square)

    @pl.loop(0, width // 1024)
    def _(i):
        at = pl.ds(pl.multiple_of(i * 1024, 1024), 1024)
        square[...] += jnp.dot(normed[:, at], a_rows[at, :], preferred_element_type=F32)

    low[...] = square[...].astype(BF)


def prepare(number, place, parts, gain, a_both):
    tokens, quarter = parts[0].shape
    width = 4 * quarter
    return pl.pallas_call(
        prepare_kernel,
        in_specs=[pl.BlockSpec(memory_space=pltpu.SMEM)] * 2 + vmem_specs(6),
        out_specs=vmem_specs(3),
        out_shape=[
            jax.ShapeDtypeStruct((tokens, width), BF),
            jax.ShapeDtypeStruct((width, 128), BF),
            jax.ShapeDtypeStruct((tokens, 128), BF),
        ],
        scratch_shapes=[pltpu.VMEM((tokens, 128), F32), pltpu.VMEM((tokens, 128), F32)],
        compiler_params=params(),
        cost_estimate=pl.CostEstimate(
            flops=2 * tokens * width * 128, bytes_accessed=tokens * width * 6, transcendentals=0
        ),
        name="prepare",
    )(number, place, *parts, gain.reshape(width // 128, 128), a_both)


def fetch(sources, held, sems):
    copies = [
        pltpu.make_async_copy(source, held.at[k], sems.at[k]) for k, source in enumerate(sources)
    ]
    for copy in copies:
        copy.start()
    return copies


def project_kernel(places, last, normed, *refs):
    count = len(places)
    sources, rest = refs[:count], refs[count:]
    if last:
        begin, low, up, kv, query, held, total, sems = rest
    else:
        total, held, sems = rest
    copies = fetch(sources, held, sems)
    if last:
        total[...] = begin[...] + ADAPTER_SCALE * jnp.dot(
            low[...], up[...], preferred_element_type=F32
        )
    for k, place in enumerate(places):
        copies[k].wait()
        block = jnp.dot(
            normed[:, place * ROWS : (place + 1) * ROWS], held[k], preferred_element_type=F32
        )
        if k == 0 and not last:
            total[...] = block
        else:
            total[...] += block
    if last:
        kv[...] = total[:, : 2 * HD].astype(BF)
        query[...] = total[:, 2 * HD :].astype(BF)


def project(normed, places, blocks, tail=()):
    tokens = normed.shape[0]
    columns = blocks[0].shape[1]
    count = len(blocks)
    last = len(tail) > 0
    total = jax.ShapeDtypeStruct((tokens, columns), F32)
    held = pltpu.VMEM((count, ROWS, columns), BF)
    sems = pltpu.SemaphoreType.DMA((count,))
    return pl.pallas_call(
        functools.partial(project_kernel, places, last),
        in_specs=vmem_specs(1) + any_specs(count) + vmem_specs(len(tail)),
        out_specs=vmem_specs(2) if last else vmem_specs(1)[0],
        out_shape=[
            jax.ShapeDtypeStruct((tokens, 2 * HD), BF),
            jax.ShapeDtypeStruct((tokens, columns - 2 * HD), BF),
        ]
        if last
        else total,
        scratch_shapes=[held] + ([pltpu.VMEM((tokens, columns), F32)] if last else []) + [sems],
        compiler_params=params(),
        cost_estimate=pl.CostEstimate(
            flops=2 * tokens * count * ROWS * columns,
            bytes_accessed=2 * count * ROWS * (tokens + columns),
            transcendentals=0,
        ),
        name="project",
    )(normed, *blocks, *tail)


def gain_kernel(count, numbers, normed, grads, ranks, a_rows, *refs):
    sources, (out, held, sems) = refs[:count], refs[count:]
    copies = fetch(sources, held, sems)
    grads_all, ranks_all = grads[...], ranks[...]
    for k in range(count):
        copies[k].wait()
        at = slice(k * ROWS, (k + 1) * ROWS)
        term = lax.dot_general(
            grads_all, held[k], (((1,), (1,)), ((), ())), preferred_element_type=F32
        ) + lax.dot_general(
            ranks_all, a_rows[at, :], (((1,), (1,)), ((), ())), preferred_element_type=F32
        )
        sums = jnp.sum(term * normed[:, at].astype(F32), axis=0, keepdims=True)
        for s in range(ROWS // 128):
            out[pl.ds(numbers[k * (ROWS // 128) + s], 1), :] = sums[:, s * 128 : (s + 1) * 128]


def gain_part(numbers, normed, grads, ranks, a_rows, blocks):
    tokens, width = normed.shape
    columns = grads.shape[1]
    count = len(blocks)
    return pl.pallas_call(
        functools.partial(gain_kernel, count),
        in_specs=[pl.BlockSpec(memory_space=pltpu.SMEM)] + vmem_specs(4) + any_specs(count),
        out_specs=vmem_specs(1)[0],
        out_shape=jax.ShapeDtypeStruct((width // 128, 128), F32),
        scratch_shapes=[
            pltpu.VMEM((count, ROWS, columns), BF),
            pltpu.SemaphoreType.DMA((count,)),
        ],
        compiler_params=params(),
        cost_estimate=pl.CostEstimate(
            flops=2 * tokens * width * columns,
            bytes_accessed=2 * width * (tokens + columns),
            transcendentals=0,
        ),
        name="gain_part",
    )(numbers, normed, grads, ranks, a_rows, *blocks)


def attend_kernel(
    query, kv, prev, grads, docs_col, docs_row, out, dq, dkv, dprev, dk, dv, dkp, dvp
):
    tokens = kv.shape[0]
    half = tokens // 2
    scale = HD ** (-0.5)
    heads = grads.shape[1] // HD
    own_col = docs_col[...]
    ext_row = docs_row[...]

    def causal(rows, columns, ahead):
        row = lax.broadcasted_iota(jnp.int32, (rows, columns), 0)
        column = lax.broadcasted_iota(jnp.int32, (rows, columns), 1)
        return row + ahead >= column

    plain = (own_col == ext_row[:, half:]) & causal(tokens, tokens, 0)
    early = (own_col[:half] == ext_row[:, :tokens]) & causal(half, tokens, half)
    late = (own_col[half:] == ext_row[:, tokens:]) & causal(half, half, 0)
    k_own, v_own = kv[:, :HD], kv[:, HD:]
    k_early = jnp.concatenate([prev[:, :HD], k_own[:half]], axis=0)
    v_early = jnp.concatenate([prev[:, HD:], v_own[:half]], axis=0)
    k_late, v_late = k_own[half:], v_own[half:]

    def attend(queries, keys, values, cot, allowed):
        scores = (
            lax.dot_general(
                queries, keys, (((1,), (1,)), ((), ())), preferred_element_type=F32
            )
            * scale
        )
        scores = jnp.where(allowed, scores, NEG_FILL)
        expo = jnp.exp(scores - jnp.max(scores, axis=1, keepdims=True))
        probs = expo * (1.0 / jnp.sum(expo, axis=1, keepdims=True))
        probs_low = probs.astype(BF)
        output = jnp.dot(probs_low, values, preferred_element_type=F32).astype(BF)
        delta = jnp.sum(cot.astype(F32) * output.astype(F32), axis=1, keepdims=True)
        dprob = lax.dot_general(
            cot, values, (((1,), (1,)), ((), ())), preferred_element_type=F32
        )
        dscore = (probs * (dprob - delta)).astype(BF)
        dquery = (jnp.dot(dscore, keys, preferred_element_type=F32) * scale).astype(BF)
        dkey = lax.dot_general(
            dscore, queries, (((0,), (0,)), ((), ())), preferred_element_type=F32
        )
        dvalue = lax.dot_general(
            probs_low, cot, (((0,), (0,)), ((), ())), preferred_element_type=F32
        )
        return output, dquery, dkey, dvalue

    dk[...] = jnp.zeros_like(dk)
    dv[...] = jnp.zeros_like(dv)
    dkp[...] = jnp.zeros_like(dkp)
    dvp[...] = jnp.zeros_like(dvp)
    for h in range(heads):
        at = slice(h * HD, (h + 1) * HD)
        queries = query[:, at]
        cot = grads[:, at]
        if h % 2 == 0:
            o, g, a, b = attend(queries, k_own, v_own, cot, plain)
            out[:, at] = o
            dq[:, at] = g
            dk[...] += a
            dv[...] += b
        else:
            o, g, a, b = attend(queries[:half], k_early, v_early, cot[:half], early)
            out[:half, at] = o
            dq[:half, at] = g
            dkp[...] += a[:half]
            dvp[...] += b[:half]
            dk[:half] += a[half:]
            dv[:half] += b[half:]
            o, g, a, b = attend(queries[half:], k_late, v_late, cot[half:], late)
            out[half:, at] = o
            dq[half:, at] = g
            dk[half:] += a
            dv[half:] += b
    dkv[:, :HD] = dk[...] * scale
    dkv[:, HD:] = dv[...]
    dprev[:, :HD] = (dkp[...] * scale).astype(BF)
    dprev[:, HD:] = dvp[...].astype(BF)


def attend(query, kv, prev, grads, docs_col, docs_row):
    tokens, columns = grads.shape
    half = tokens // 2
    return pl.pallas_call(
        attend_kernel,
        out_shape=[
            jax.ShapeDtypeStruct((tokens, columns), BF),
            jax.ShapeDtypeStruct((tokens, columns), BF),
            jax.ShapeDtypeStruct((tokens, 2 * HD), F32),
            jax.ShapeDtypeStruct((half, 2 * HD), BF),
        ],
        scratch_shapes=[
            pltpu.VMEM((tokens, HD), F32),
            pltpu.VMEM((tokens, HD), F32),
            pltpu.VMEM((half, HD), F32),
            pltpu.VMEM((half, HD), F32),
        ],
        compiler_params=params(),
        cost_estimate=pl.CostEstimate(
            flops=2 * 5 * tokens * tokens * columns,
            bytes_accessed=2 * tokens * columns * 4,
            transcendentals=tokens * tokens * columns // HD,
        ),
        name="attend",
    )(query, kv, prev, grads, docs_col, docs_row)


def dot_rows(left, right):
    return lax.dot_general(left, right, (((0,), (0,)), ((), ())), preferred_element_type=F32)


def dot_cols(left, right):
    return lax.dot_general(left, right, (((1,), (1,)), ((), ())), preferred_element_type=F32)


def sum_heads(value):
    low = value.astype(BF)
    total = value
    for step in (1, 2, 3):
        total = total + shift(low, "mp", step).astype(F32)
    return total


def reduce_stage(chunks, whole, move):
    count = whole.shape[0]
    total = jnp.concatenate([whole, chunks[0]], axis=0)
    low = whole.astype(BF)
    for i in (1, 2, 3):
        packed = jnp.concatenate([low, chunks[i].astype(BF)], axis=0)
        total = total + move(packed, REL[i]).astype(F32)
    return total[:count], total[count:]


def per_device(
    hidden,
    gain,
    query_frozen_weight,
    w_key,
    value_frozen_weight,
    a_query,
    query_up_weight,
    a_value,
    value_up_weight,
    doc_ids,
    d_out,
):
    tokens = hidden.shape[1]
    half = tokens // 2
    dp, seq, mp = lax.axis_index("dp"), lax.axis_index("seq"), lax.axis_index("mp")
    own = hidden[0]
    h_zh = shift(own, "mp", 2)
    parts = [own, shift(own, "mp", 1), h_zh, shift(h_zh, "mp", 1)]
    weights = jnp.concatenate([w_key, value_frozen_weight, query_frozen_weight], axis=1)
    first, second = gather_rows(weights)

    number, place, number_at = block_places(dp, seq, mp)
    a_both = jnp.concatenate([a_query, a_value], axis=1)
    normed, a_rows, low = prepare(number, place, parts, gain, a_both)
    rank = query_up_weight.shape[0]
    up = jnp.concatenate(
        [
            jnp.concatenate([jnp.zeros((rank, 2 * HD), BF), query_up_weight], axis=1),
            jnp.concatenate(
                [jnp.zeros((rank, HD), BF), value_up_weight, jnp.zeros_like(query_up_weight)], axis=1
            ),
        ],
        axis=0,
    )
    partial = project(
        normed, list(range(6)) + list(range(8, 14)), first[:6] + second[:6]
    )
    kv, query = project(normed, [6, 7, 14, 15], first[6:] + second[6:], (partial, low, up))
    prev = lax.ppermute(kv[half:], "seq", [(i, i + 1) for i in range(3)])

    docs = doc_ids[0]
    begin = seq * tokens
    own_docs = lax.dynamic_slice_in_dim(docs, begin, tokens)
    prev_docs = lax.dynamic_slice_in_dim(docs, jnp.maximum(begin - half, 0), half)
    prev_docs = jnp.where(seq > 0, prev_docs, -1)
    ext_docs = jnp.concatenate([prev_docs, own_docs])
    output, dq, dkv, dprev = attend(
        query, kv, prev, d_out[0], own_docs[:, None], ext_docs[None, :]
    )
    returned = lax.ppermute(dprev, "seq", [(i + 1, i) for i in range(3)]).astype(F32)
    dkv = jnp.concatenate([dkv[:half], dkv[half:] + returned], axis=0).astype(BF)
    dvalue = dkv[:, HD:]
    ranks = ADAPTER_SCALE * jnp.concatenate(
        [dot_cols(dq, query_up_weight), dot_cols(dvalue, value_up_weight)], axis=1
    )
    rank_rows = sum_heads(ranks).astype(BF)
    grads = jnp.concatenate([dkv, dq], axis=1)
    gains = gain_part(number_at, normed, grads, ranks.astype(BF), a_rows, first + second)

    up_rows = [dot_rows(low[:, rank:], dvalue)] + [
        dot_rows(low[:, :rank], dq[:, h * HD : (h + 1) * HD]) for h in range(dq.shape[1] // HD)
    ]
    up_rows = ADAPTER_SCALE * jnp.concatenate(up_rows, axis=0)
    whole = jnp.concatenate([up_rows, gains], axis=0)

    width = normed.shape[1]
    mine = lax.dynamic_slice_in_dim(normed, mp // 2 * (width // 2), width // 2, 1)
    grad_a = dot_rows(mine, rank_rows).reshape(32, 2, 64, 2 * rank)
    grad_a = lax.dynamic_index_in_dim(grad_a, mp % 2, 1, keepdims=False)
    grad_a = grad_a.reshape(4, 512, 2 * rank)
    whole, grad_a = reduce_stage(grad_a, whole, lambda v, step: shift_plane(v, 0, step))
    grad_a = grad_a.reshape(2, 4, 64, 2 * rank)
    chunks = [grad_a[:, i].reshape(128, 2 * rank) for i in range(4)]
    whole, grad_a = reduce_stage(chunks, whole, lambda v, step: shift_plane(v, 1, step))
    packed = jnp.concatenate([whole, grad_a[64:]], axis=0).astype(BF)
    total = jnp.concatenate([whole, grad_a[:64]], axis=0) + shift(packed, "zl", 1).astype(F32)
    count = up_rows.shape[0]
    gains = total[count : count + 64]
    grad_a = total[count + 64 :]
    low_gains = gains.astype(BF)
    gain_sum = lax.dynamic_slice_in_dim(gains, mp * 16, 16, 0)
    for step in (1, 2, 3):
        send = lax.dynamic_slice_in_dim(low_gains, (mp ^ step) * 16, 16, 0)
        gain_sum = gain_sum + shift(send, "mp", step).astype(F32)
    gain_sum = gain_sum.reshape(-1)
    gain_own = lax.dynamic_slice_in_dim(gain, mp * gain_sum.shape[0], gain_sum.shape[0])
    up_query = total[64:count].reshape(-1, 64, HD).transpose(1, 0, 2).reshape(64, -1)
    return (
        output[None],
        grad_a[:, :rank],
        up_query,
        grad_a[:, rank:],
        total[:64],
        gain_sum / gain_own,
    )


def solution(mesh):
    return jax.shard_map(
        per_device,
        mesh=mesh,
        in_specs=(
            P("dp", "seq", "mp"),
            P(),
            P(("dp", "seq"), "mp"),
            P(("dp", "seq"), "mp"),
            P(("dp", "seq"), "mp"),
            P(),
            P(None, "mp"),
            P(),
            P(None, "mp"),
            P("dp", None),
            P("dp", "seq", "mp"),
        ),
        out_specs=(
            P("dp", "seq", "mp"),
            P(("dp", "seq", "mp"), None),
            P(None, "mp"),
            P(("dp", "seq", "mp"), None),
            P(None, "mp"),
            P("mp"),
        ),
        check_vma=False,
    )
```

```python
import functools

import jax
import jax.numpy as jnp
from jax import lax
from jax.experimental import pallas as pl
from jax.experimental.pallas import tpu as pltpu
from jax.sharding import PartitionSpec as P

HD = 128
EPS = 1e-05
ADAPTER_SCALE = 0.25
NEG_FILL = -1e30
BF = jnp.bfloat16
F32 = jnp.float32
VMEM_LIMIT = 56 * 1024 * 1024
REL = (0, -1, 1, 2)
ROWS = 512


def shift(value, axis, step):
    if axis == "x":
        route = [(z * 4 + i, z * 4 + (i + step) % 4) for z in range(2) for i in range(4)]
        return lax.ppermute(value, "dp", route)
    if axis == "zl":
        return lax.ppermute(value, "dp", [(i, (i + 4) % 8) for i in range(8)])
    if axis == "y":
        return lax.ppermute(value, "seq", [(i, (i + step) % 4) for i in range(4)])
    return lax.ppermute(value, "mp", [(i, i ^ step) for i in range(4)])


def shift_plane(value, stage, step):
    route = []
    for z in range(2):
        for x in range(4):
            for y in range(4):
                for m in range(4):
                    to_x, to_y = x, y
                    if (m < 2) == (stage == 0):
                        to_y = (y + step) % 4
                    else:
                        to_x = (x + step) % 4
                    route.append(
                        (((z * 4 + x) * 4 + y) * 4 + m, ((z * 4 + to_x) * 4 + to_y) * 4 + m)
                    )
    return lax.ppermute(value, ("dp", "seq", "mp"), route)


def params(**kw):
    return pltpu.CompilerParams(vmem_limit_bytes=VMEM_LIMIT, **kw)


def any_specs(count):
    return [pl.BlockSpec(memory_space=pl.ANY)] * count


def vmem_specs(count):
    return [pl.BlockSpec(memory_space=pltpu.VMEM)] * count


def assemble_kernel(*refs):
    pieces, outs = refs[:8], refs[8:]
    rows = pieces[0].shape[0]
    for k, piece in enumerate(pieces):
        outs[k // 4][k % 4 * rows : (k % 4 + 1) * rows, :] = piece[...]


def assemble(pieces):
    rows, columns = pieces[0].shape
    return pl.pallas_call(
        assemble_kernel,
        in_specs=vmem_specs(8),
        out_specs=vmem_specs(2),
        out_shape=[jax.ShapeDtypeStruct((4 * rows, columns), BF)] * 2,
        compiler_params=params(),
        cost_estimate=pl.CostEstimate(
            flops=0, bytes_accessed=32 * rows * columns, transcendentals=0
        ),
        name="assemble",
    )(*pieces)


def gather_rows(shard):
    half = shard.shape[0] // 2
    pieces = []
    for part, axis in ((shard[:half], "x"), (shard[half:], "y")):
        pieces += [part] + [shift(part, axis, -step) for step in REL[1:]]
    blocks = []
    for inner, axis in zip(assemble(pieces), ("y", "x")):
        other = shift(inner, "zl", 1)
        before, after = shift(inner, axis, 1), shift(inner, axis, -1)
        before_other, after_other = shift(other, axis, 1), shift(other, axis, -1)
        blocks.append(
            [inner, other, before, before_other, after, after_other]
            + [shift(before, axis, 1), shift(after_other, axis, -1)]
        )
    return blocks


def block_places(dp, seq):
    number = jnp.arange(64, dtype=jnp.int32)
    order, shard = number % 2, number // 2
    inverse = jnp.array([0, 2, 3, 1], jnp.int32)
    flip = (shard // 16) ^ (dp // 4)
    by_x = inverse[(shard // 4 % 4 - dp) % 4]
    by_y = inverse[(shard % 4 - seq) % 4]
    outer = jnp.where(order == 0, by_y, by_x)
    inner = jnp.where(order == 0, by_x, by_y)
    place = order * 32 + outer * 8 + flip * 4 + inner
    number_at = jnp.zeros((64,), jnp.int32).at[place].set(number)
    return number, place, number_at


def prepare_kernel(number, place, gathered, gain, a_both, normed, a_rows, low, square, inv):
    tokens = normed.shape[0]
    parts = [gathered.at[k * tokens : (k + 1) * tokens] for k in range(4)]
    per = gathered.shape[1] // 128
    square[...] = jnp.zeros_like(square)
    for part in parts:

        @pl.loop(0, per)
        def _(i):
            value = part[:, pl.ds(pl.multiple_of(i * 128, 128), 128)].astype(F32)
            square[...] += value * value

    width = normed.shape[1]
    mean = jnp.sum(square[...], axis=1, keepdims=True) * (1.0 / width)
    inv[...] = jnp.broadcast_to(lax.rsqrt(mean + EPS), inv.shape)
    for r, part in enumerate(parts):

        @pl.loop(0, per)
        def _(i):
            source = pl.multiple_of(number[r * per + i] * 128, 128)
            target = pl.multiple_of(place[r * per + i] * 128, 128)
            value = part[:, pl.ds(pl.multiple_of(i * 128, 128), 128)].astype(F32)
            scaled = value * inv[...]
            normed[:, pl.ds(target, 128)] = (scaled * gain[pl.ds(number[r * per + i], 1), :]).astype(BF)
            a_rows[pl.ds(target, 128), :] = a_both[pl.ds(source, 128), :]

    square[...] = jnp.zeros_like(square)

    @pl.loop(0, width // 1024)
    def _(i):
        at = pl.ds(pl.multiple_of(i * 1024, 1024), 1024)
        square[...] += jnp.dot(normed[:, at], a_rows[at, :], preferred_element_type=F32)

    low[...] = square[...].astype(BF)


def prepare(number, place, parts, gain, a_both):
    tokens, quarter = parts[0].shape[0] // 4, parts[0].shape[1]
    width = 4 * quarter
    return pl.pallas_call(
        prepare_kernel,
        in_specs=[pl.BlockSpec(memory_space=pltpu.SMEM)] * 2 + vmem_specs(3),
        out_specs=vmem_specs(3),
        out_shape=[
            jax.ShapeDtypeStruct((tokens, width), BF),
            jax.ShapeDtypeStruct((width, 128), BF),
            jax.ShapeDtypeStruct((tokens, 128), BF),
        ],
        scratch_shapes=[pltpu.VMEM((tokens, 128), F32), pltpu.VMEM((tokens, 128), F32)],
        compiler_params=params(),
        cost_estimate=pl.CostEstimate(
            flops=2 * tokens * width * 128, bytes_accessed=tokens * width * 6, transcendentals=0
        ),
        name="prepare",
    )(number, place, *parts, gain.reshape(width // 128, 128), a_both)


def fetch(sources, held, sems):
    copies = [
        pltpu.make_async_copy(source, held.at[k], sems.at[k]) for k, source in enumerate(sources)
    ]
    for copy in copies:
        copy.start()
    return copies


def project_kernel(places, last, normed, *refs):
    count = len(places)
    sources, rest = refs[:count], refs[count:]
    if last:
        begin, low, up, kv, query, held, total, sems = rest
    else:
        total, held, sems = rest
    copies = fetch(sources, held, sems)
    if last:
        total[...] = begin[...] + ADAPTER_SCALE * jnp.dot(
            low[...], up[...], preferred_element_type=F32
        )
    for k, place in enumerate(places):
        copies[k].wait()
        block = jnp.dot(
            normed[:, place * ROWS : (place + 1) * ROWS], held[k], preferred_element_type=F32
        )
        if k == 0 and not last:
            total[...] = block
        else:
            total[...] += block
    if last:
        kv[...] = total[:, : 2 * HD].astype(BF)
        query[...] = total[:, 2 * HD :].astype(BF)


def project(normed, places, blocks, tail=()):
    tokens = normed.shape[0]
    columns = blocks[0].shape[1]
    count = len(blocks)
    last = len(tail) > 0
    total = jax.ShapeDtypeStruct((tokens, columns), F32)
    held = pltpu.VMEM((count, ROWS, columns), BF)
    sems = pltpu.SemaphoreType.DMA((count,))
    return pl.pallas_call(
        functools.partial(project_kernel, places, last),
        in_specs=vmem_specs(1) + any_specs(count) + vmem_specs(len(tail)),
        out_specs=vmem_specs(2) if last else vmem_specs(1)[0],
        out_shape=[
            jax.ShapeDtypeStruct((tokens, 2 * HD), BF),
            jax.ShapeDtypeStruct((tokens, columns - 2 * HD), BF),
        ]
        if last
        else total,
        scratch_shapes=[held] + ([pltpu.VMEM((tokens, columns), F32)] if last else []) + [sems],
        compiler_params=params(),
        cost_estimate=pl.CostEstimate(
            flops=2 * tokens * count * ROWS * columns,
            bytes_accessed=2 * count * ROWS * (tokens + columns),
            transcendentals=0,
        ),
        name="project",
    )(normed, *blocks, *tail)


def gain_kernel(count, numbers, normed, grads, ranks, a_rows, *refs):
    sources, (out, held, sems) = refs[:count], refs[count:]
    copies = fetch(sources, held, sems)
    grads_all, ranks_all = grads[...], ranks[...]
    for k in range(count):
        copies[k].wait()
        at = slice(k * ROWS, (k + 1) * ROWS)
        term = lax.dot_general(
            grads_all, held[k], (((1,), (1,)), ((), ())), preferred_element_type=F32
        ) + lax.dot_general(
            ranks_all, a_rows[at, :], (((1,), (1,)), ((), ())), preferred_element_type=F32
        )
        sums = jnp.sum(term * normed[:, at].astype(F32), axis=0, keepdims=True)
        for s in range(ROWS // 128):
            out[pl.ds(numbers[k * (ROWS // 128) + s], 1), :] = sums[:, s * 128 : (s + 1) * 128]


def gain_part(numbers, normed, grads, ranks, a_rows, blocks):
    tokens, width = normed.shape
    columns = grads.shape[1]
    count = len(blocks)
    return pl.pallas_call(
        functools.partial(gain_kernel, count),
        in_specs=[pl.BlockSpec(memory_space=pltpu.SMEM)] + vmem_specs(4) + any_specs(count),
        out_specs=vmem_specs(1)[0],
        out_shape=jax.ShapeDtypeStruct((width // 128, 128), F32),
        scratch_shapes=[
            pltpu.VMEM((count, ROWS, columns), BF),
            pltpu.SemaphoreType.DMA((count,)),
        ],
        compiler_params=params(),
        cost_estimate=pl.CostEstimate(
            flops=2 * tokens * width * columns,
            bytes_accessed=2 * width * (tokens + columns),
            transcendentals=0,
        ),
        name="gain_part",
    )(numbers, normed, grads, ranks, a_rows, *blocks)


def attend_kernel(
    query, kv, prev, grads, docs_col, docs_row, out, dq, dkv, dprev, dk, dv, dkp, dvp
):
    tokens = kv.shape[0]
    half = tokens // 2
    scale = HD ** (-0.5)
    heads = grads.shape[1] // HD
    own_col = docs_col[...]
    ext_row = docs_row[...]

    def causal(rows, columns, ahead):
        row = lax.broadcasted_iota(jnp.int32, (rows, columns), 0)
        column = lax.broadcasted_iota(jnp.int32, (rows, columns), 1)
        return row + ahead >= column

    plain = (own_col == ext_row[:, half:]) & causal(tokens, tokens, 0)
    early = (own_col[:half] == ext_row[:, :tokens]) & causal(half, tokens, half)
    late = (own_col[half:] == ext_row[:, tokens:]) & causal(half, half, 0)
    k_own, v_own = kv[:, :HD], kv[:, HD:]
    k_early = jnp.concatenate([prev[:, :HD], k_own[:half]], axis=0)
    v_early = jnp.concatenate([prev[:, HD:], v_own[:half]], axis=0)
    k_late, v_late = k_own[half:], v_own[half:]

    def attend(queries, keys, values, cot, allowed):
        scores = (
            lax.dot_general(
                queries, keys, (((1,), (1,)), ((), ())), preferred_element_type=F32
            )
            * scale
        )
        scores = jnp.where(allowed, scores, NEG_FILL)
        expo = jnp.exp(scores - jnp.max(scores, axis=1, keepdims=True))
        probs = expo * (1.0 / jnp.sum(expo, axis=1, keepdims=True))
        probs_low = probs.astype(BF)
        output = jnp.dot(probs_low, values, preferred_element_type=F32).astype(BF)
        delta = jnp.sum(cot.astype(F32) * output.astype(F32), axis=1, keepdims=True)
        dprob = lax.dot_general(
            cot, values, (((1,), (1,)), ((), ())), preferred_element_type=F32
        )
        dscore = (probs * (dprob - delta)).astype(BF)
        dquery = (jnp.dot(dscore, keys, preferred_element_type=F32) * scale).astype(BF)
        dkey = lax.dot_general(
            dscore, queries, (((0,), (0,)), ((), ())), preferred_element_type=F32
        )
        dvalue = lax.dot_general(
            probs_low, cot, (((0,), (0,)), ((), ())), preferred_element_type=F32
        )
        return output, dquery, dkey, dvalue

    dk[...] = jnp.zeros_like(dk)
    dv[...] = jnp.zeros_like(dv)
    dkp[...] = jnp.zeros_like(dkp)
    dvp[...] = jnp.zeros_like(dvp)
    for h in range(heads):
        at = slice(h * HD, (h + 1) * HD)
        queries = query[:, at]
        cot = grads[:, at]
        if h % 2 == 0:
            o, g, a, b = attend(queries, k_own, v_own, cot, plain)
            out[:, at] = o
            dq[:, at] = g
            dk[...] += a
            dv[...] += b
        else:
            o, g, a, b = attend(queries[:half], k_early, v_early, cot[:half], early)
            out[:half, at] = o
            dq[:half, at] = g
            dkp[...] += a[:half]
            dvp[...] += b[:half]
            dk[:half] += a[half:]
            dv[:half] += b[half:]
            o, g, a, b = attend(queries[half:], k_late, v_late, cot[half:], late)
            out[half:, at] = o
            dq[half:, at] = g
            dk[half:] += a
            dv[half:] += b
    dkv[:, :HD] = dk[...] * scale
    dkv[:, HD:] = dv[...]
    dprev[:, :HD] = (dkp[...] * scale).astype(BF)
    dprev[:, HD:] = dvp[...].astype(BF)


def attend(query, kv, prev, grads, docs_col, docs_row):
    tokens, columns = grads.shape
    half = tokens // 2
    return pl.pallas_call(
        attend_kernel,
        out_shape=[
            jax.ShapeDtypeStruct((tokens, columns), BF),
            jax.ShapeDtypeStruct((tokens, columns), BF),
            jax.ShapeDtypeStruct((tokens, 2 * HD), F32),
            jax.ShapeDtypeStruct((half, 2 * HD), BF),
        ],
        scratch_shapes=[
            pltpu.VMEM((tokens, HD), F32),
            pltpu.VMEM((tokens, HD), F32),
            pltpu.VMEM((half, HD), F32),
            pltpu.VMEM((half, HD), F32),
        ],
        compiler_params=params(),
        cost_estimate=pl.CostEstimate(
            flops=2 * 5 * tokens * tokens * columns,
            bytes_accessed=2 * tokens * columns * 4,
            transcendentals=tokens * tokens * columns // HD,
        ),
        name="attend",
    )(query, kv, prev, grads, docs_col, docs_row)


def dot_rows(left, right):
    return lax.dot_general(left, right, (((0,), (0,)), ((), ())), preferred_element_type=F32)


def dot_cols(left, right):
    return lax.dot_general(left, right, (((1,), (1,)), ((), ())), preferred_element_type=F32)


def sum_heads(value):
    low = value.astype(BF)
    total = value
    for step in (1, 2, 3):
        total = total + shift(low, "mp", step).astype(F32)
    return total


def reduce_stage(chunks, whole, move):
    count = whole.shape[0]
    total = jnp.concatenate([whole, chunks[0]], axis=0)
    low = whole.astype(BF)
    for i in (1, 2, 3):
        packed = jnp.concatenate([low, chunks[i].astype(BF)], axis=0)
        total = total + move(packed, REL[i]).astype(F32)
    return total[:count], total[count:]


def per_device(
    hidden,
    gain,
    query_frozen_weight,
    w_key,
    value_frozen_weight,
    a_query,
    query_up_weight,
    a_value,
    value_up_weight,
    doc_ids,
    d_out,
):
    tokens = hidden.shape[1]
    half = tokens // 2
    dp, seq, mp = lax.axis_index("dp"), lax.axis_index("seq"), lax.axis_index("mp")
    own = hidden[0]
    whole_hidden = lax.all_gather(own, "mp", axis=0, tiled=True)
    parts = [whole_hidden]
    weights = jnp.concatenate([w_key, value_frozen_weight, query_frozen_weight], axis=1)
    first, second = gather_rows(weights)

    number, place, number_at = block_places(dp, seq)
    a_both = jnp.concatenate([a_query, a_value], axis=1)
    normed, a_rows, low = prepare(number, place, parts, gain, a_both)
    rank = query_up_weight.shape[0]
    up = jnp.concatenate(
        [
            jnp.concatenate([jnp.zeros((rank, 2 * HD), BF), query_up_weight], axis=1),
            jnp.concatenate(
                [jnp.zeros((rank, HD), BF), value_up_weight, jnp.zeros_like(query_up_weight)], axis=1
            ),
        ],
        axis=0,
    )
    partial = project(
        normed, list(range(6)) + list(range(8, 14)), first[:6] + second[:6]
    )
    kv, query = project(normed, [6, 7, 14, 15], first[6:] + second[6:], (partial, low, up))
    prev = lax.ppermute(kv[half:], "seq", [(i, i + 1) for i in range(3)])

    docs = doc_ids[0]
    begin = seq * tokens
    own_docs = lax.dynamic_slice_in_dim(docs, begin, tokens)
    prev_docs = lax.dynamic_slice_in_dim(docs, jnp.maximum(begin - half, 0), half)
    prev_docs = jnp.where(seq > 0, prev_docs, -1)
    ext_docs = jnp.concatenate([prev_docs, own_docs])
    output, dq, dkv, dprev = attend(
        query, kv, prev, d_out[0], own_docs[:, None], ext_docs[None, :]
    )
    returned = lax.ppermute(dprev, "seq", [(i + 1, i) for i in range(3)]).astype(F32)
    dkv = jnp.concatenate([dkv[:half], dkv[half:] + returned], axis=0).astype(BF)
    dvalue = dkv[:, HD:]
    ranks = ADAPTER_SCALE * jnp.concatenate(
        [dot_cols(dq, query_up_weight), dot_cols(dvalue, value_up_weight)], axis=1
    )
    rank_rows = sum_heads(ranks).astype(BF)
    grads = jnp.concatenate([dkv, dq], axis=1)
    gains = gain_part(number_at, normed, grads, ranks.astype(BF), a_rows, first + second)

    up_rows = [dot_rows(low[:, rank:], dvalue)] + [
        dot_rows(low[:, :rank], dq[:, h * HD : (h + 1) * HD]) for h in range(dq.shape[1] // HD)
    ]
    up_rows = ADAPTER_SCALE * jnp.concatenate(up_rows, axis=0)
    whole = jnp.concatenate([up_rows, gains], axis=0)

    width = normed.shape[1]
    mine = lax.dynamic_slice_in_dim(normed, mp // 2 * (width // 2), width // 2, 1)
    grad_a = dot_rows(mine, rank_rows).reshape(32, 2, 64, 2 * rank)
    grad_a = lax.dynamic_index_in_dim(grad_a, mp % 2, 1, keepdims=False)
    grad_a = grad_a.reshape(4, 512, 2 * rank)
    whole, grad_a = reduce_stage(grad_a, whole, lambda v, step: shift_plane(v, 0, step))
    grad_a = grad_a.reshape(2, 4, 64, 2 * rank)
    chunks = [grad_a[:, i].reshape(128, 2 * rank) for i in range(4)]
    whole, grad_a = reduce_stage(chunks, whole, lambda v, step: shift_plane(v, 1, step))
    packed = jnp.concatenate([whole, grad_a[64:]], axis=0).astype(BF)
    total = jnp.concatenate([whole, grad_a[:64]], axis=0) + shift(packed, "zl", 1).astype(F32)
    count = up_rows.shape[0]
    gains = total[count : count + 64]
    grad_a = total[count + 64 :]
    low_gains = gains.astype(BF)
    gain_sum = lax.dynamic_slice_in_dim(gains, mp * 16, 16, 0)
    for step in (1, 2, 3):
        send = lax.dynamic_slice_in_dim(low_gains, (mp ^ step) * 16, 16, 0)
        gain_sum = gain_sum + shift(send, "mp", step).astype(F32)
    gain_sum = gain_sum.reshape(-1)
    gain_own = lax.dynamic_slice_in_dim(gain, mp * gain_sum.shape[0], gain_sum.shape[0])
    up_query = total[64:count].reshape(-1, 64, HD).transpose(1, 0, 2).reshape(64, -1)
    return (
        output[None],
        grad_a[:, :rank],
        up_query,
        grad_a[:, rank:],
        total[:64],
        gain_sum / gain_own,
    )


def solution(mesh):
    return jax.shard_map(
        per_device,
        mesh=mesh,
        in_specs=(
            P("dp", "seq", "mp"),
            P(),
            P(("dp", "seq"), "mp"),
            P(("dp", "seq"), "mp"),
            P(("dp", "seq"), "mp"),
            P(),
            P(None, "mp"),
            P(),
            P(None, "mp"),
            P("dp", None),
            P("dp", "seq", "mp"),
        ),
        out_specs=(
            P("dp", "seq", "mp"),
            P(("dp", "seq", "mp"), None),
            P(None, "mp"),
            P(("dp", "seq", "mp"), None),
            P(None, "mp"),
            P("mp"),
        ),
        check_vma=False,
    )
```

```python
import functools

import jax
import jax.numpy as jnp
from jax import lax
from jax.experimental import pallas as pl
from jax.experimental.pallas import tpu as pltpu
from jax.sharding import PartitionSpec as P

HD = 128
EPS = 1e-05
ADAPTER_SCALE = 0.25
NEG_FILL = -1e30
BF = jnp.bfloat16
F32 = jnp.float32
VMEM_LIMIT = 56 * 1024 * 1024
REL = (0, -1, 1, 2)
ROWS = 512


def shift(value, axis, step):
    if axis == "x":
        route = [(z * 4 + i, z * 4 + (i + step) % 4) for z in range(2) for i in range(4)]
        return lax.ppermute(value, "dp", route)
    if axis == "zl":
        return lax.ppermute(value, "dp", [(i, (i + 4) % 8) for i in range(8)])
    if axis == "y":
        return lax.ppermute(value, "seq", [(i, (i + step) % 4) for i in range(4)])
    return lax.ppermute(value, "mp", [(i, i ^ step) for i in range(4)])


def shift_plane(value, stage, step):
    route = []
    for z in range(2):
        for x in range(4):
            for y in range(4):
                for m in range(4):
                    to_x, to_y = x, y
                    if (m < 2) == (stage == 0):
                        to_y = (y + step) % 4
                    else:
                        to_x = (x + step) % 4
                    route.append(
                        (((z * 4 + x) * 4 + y) * 4 + m, ((z * 4 + to_x) * 4 + to_y) * 4 + m)
                    )
    return lax.ppermute(value, ("dp", "seq", "mp"), route)


def params(**kw):
    return pltpu.CompilerParams(vmem_limit_bytes=VMEM_LIMIT, **kw)


def any_specs(count):
    return [pl.BlockSpec(memory_space=pl.ANY)] * count


def vmem_specs(count):
    return [pl.BlockSpec(memory_space=pltpu.VMEM)] * count


def assemble_kernel(*refs):
    pieces, outs = refs[:8], refs[8:]
    rows = pieces[0].shape[0]
    for k, piece in enumerate(pieces):
        outs[k // 4][k % 4 * rows : (k % 4 + 1) * rows, :] = piece[...]


def assemble(pieces):
    rows, columns = pieces[0].shape
    return pl.pallas_call(
        assemble_kernel,
        in_specs=vmem_specs(8),
        out_specs=vmem_specs(2),
        out_shape=[jax.ShapeDtypeStruct((4 * rows, columns), BF)] * 2,
        compiler_params=params(),
        cost_estimate=pl.CostEstimate(
            flops=0, bytes_accessed=32 * rows * columns, transcendentals=0
        ),
        name="assemble",
    )(*pieces)


def gather_rows(shard):
    half = shard.shape[0] // 2
    pieces = []
    for part, axis in ((shard[:half], "x"), (shard[half:], "y")):
        pieces += [part] + [shift(part, axis, -step) for step in REL[1:]]
    blocks = []
    for inner, axis in zip(assemble(pieces), ("y", "x")):
        before, after = shift(inner, axis, 1), shift(inner, axis, -1)
        blocks.append(
            [inner, before, after]
            + [shift(before[: ROWS // 2], axis, 1), shift(after[ROWS // 2 :], axis, -1)]
        )
    return blocks


def gather_hidden(own):
    taken = []
    for turn in (0, 1):
        route = []
        for zl in range(2):
            for x in range(4):
                for zh in range(2):
                    for c in range(2):
                        to_zl, to_zh = zh, zl ^ turn
                        route.append(
                            ((zl * 4 + x) * 4 + zh * 2 + c, (to_zl * 4 + x) * 4 + to_zh * 2 + c)
                        )
        taken.append(lax.ppermute(own, ("dp", "mp"), route))
    return [(part, shift(part, "mp", 1)) for part in taken]


def block_places(x, y, core):
    at = jnp.arange(32, dtype=jnp.int32)
    number = ((at // 16) ^ core) * 16 + at % 16
    order, shard = number % 2, number // 2
    inverse = jnp.array([0, 2, 3, 1], jnp.int32)
    by_x = inverse[(shard // 4 - x) % 4]
    by_y = inverse[(shard % 4 - y) % 4]
    outer = jnp.where(order == 0, by_y, by_x)
    inner = jnp.where(order == 0, by_x, by_y)
    place = order * 16 + outer * 4 + inner
    number_at = jnp.sum(jnp.where(place[None, :] == at[:, None], number[None, :], 0), axis=1)
    return number, place, number_at.astype(jnp.int32)


def prepare_kernel(
    number, place, where, p0, p1, p2, p3, sums0, sums1, gain, a_both, normed, a_rows, inv
):
    tokens = p0.shape[0]
    per = p0.shape[1] // 128
    width = gain.shape[0] * 128
    for pack, (sums, parts) in enumerate(((sums0, (p0, p1)), (sums1, (p2, p3)))):
        inv[...] = jnp.broadcast_to(lax.rsqrt(sums[...] * (1.0 / width) + EPS), inv.shape)
        rows = pl.ds(pl.multiple_of(where[pack], tokens), tokens)
        for r, part in enumerate(parts):

            @pl.loop(0, per)
            def _(i):
                block = where[2] + number[r * per + i]
                target = pl.ds(pl.multiple_of(place[r * per + i] * 128, 128), 128)
                value = part[:, pl.ds(pl.multiple_of(i * 128, 128), 128)].astype(F32)
                scaled = value * inv[...]
                normed[rows, target] = (scaled * gain[pl.ds(block, 1), :]).astype(BF)
                if pack == 0:
                    source = pl.ds(pl.multiple_of(block * 128, 128), 128)
                    a_rows[target, :] = a_both[source, :]


def prepare(number, place, where, parts, sums, gain, a_both):
    tokens, quarter = parts[0].shape
    return pl.pallas_call(
        prepare_kernel,
        in_specs=[pl.BlockSpec(memory_space=pltpu.SMEM)] * 3 + vmem_specs(8),
        out_specs=vmem_specs(2),
        out_shape=[
            jax.ShapeDtypeStruct((2 * tokens, 2 * quarter), BF),
            jax.ShapeDtypeStruct((2 * quarter, 128), BF),
        ],
        scratch_shapes=[pltpu.VMEM((tokens, 128), F32)],
        compiler_params=params(),
        cost_estimate=pl.CostEstimate(
            flops=16 * tokens * quarter, bytes_accessed=16 * tokens * quarter, transcendentals=0
        ),
        name="prepare",
    )(number, place, where, *parts, *sums, gain.reshape(-1, 128), a_both)


def fetch(sources, held, sems):
    copies = []
    begin = 0
    for k, source in enumerate(sources):
        rows = source.shape[0]
        copies.append(
            pltpu.make_async_copy(source, held.at[pl.ds(begin, rows)], sems.at[k])
        )
        begin += rows
    for copy in copies:
        copy.start()
    return copies


def project_kernel(starts, normed, a_rows, *refs):
    count = len(starts)
    sources, (total, low, held, sems) = refs[:count], refs[count:]
    copies = fetch(sources, held, sems)
    width = normed.shape[1]
    for k in range(0, width, 1024):
        block = jnp.dot(normed[:, k : k + 1024], a_rows[k : k + 1024, :], preferred_element_type=F32)
        if k == 0:
            low[...] = block
        else:
            low[...] += block
    for k, start in enumerate(starts):
        copies[k].wait()
        block = jnp.dot(
            normed[:, start : start + ROWS],
            held[k * ROWS : (k + 1) * ROWS, :],
            preferred_element_type=F32,
        )
        if k == 0:
            total[...] = block
        else:
            total[...] += block


def project(normed, a_rows, starts, blocks):
    tokens = normed.shape[0]
    columns = blocks[0].shape[1]
    count = len(blocks)
    return pl.pallas_call(
        functools.partial(project_kernel, starts),
        in_specs=vmem_specs(2) + any_specs(count),
        out_specs=vmem_specs(2),
        out_shape=[
            jax.ShapeDtypeStruct((tokens, columns), F32),
            jax.ShapeDtypeStruct((tokens, 128), F32),
        ],
        scratch_shapes=[
            pltpu.VMEM((count * ROWS, columns), BF),
            pltpu.SemaphoreType.DMA((count,)),
        ],
        compiler_params=params(),
        cost_estimate=pl.CostEstimate(
            flops=2 * tokens * count * ROWS * columns,
            bytes_accessed=2 * count * ROWS * (tokens + columns),
            transcendentals=0,
        ),
        name="project",
    )(normed, a_rows, *blocks)


def finish_kernel(starts, normed, begin, low, *refs):
    sources, (kept, sent, held, sems) = refs[:4], refs[4:]
    copies = fetch(sources, held, sems)
    tokens = kept.shape[0]
    columns = begin.shape[1]
    for copy in copies:
        copy.wait()
    for part in (1, 0):
        rows = slice(part * tokens, (part + 1) * tokens)
        total = begin[rows, :]
        for k, start in enumerate(starts):
            total += jnp.dot(
                normed[rows, start : start + ROWS],
                held[k * ROWS : (k + 1) * ROWS, :],
                preferred_element_type=F32,
            )
        if part == 0:
            kept[:, :columns] = total
            kept[:, columns:] = low[rows, :]
        else:
            sent[:, :columns] = total.astype(BF)
            sent[:, columns:] = low[rows, :].astype(BF)


def finish(normed, begin, low, starts, blocks):
    tokens = normed.shape[0] // 2
    columns = blocks[0].shape[1]
    return pl.pallas_call(
        functools.partial(finish_kernel, starts),
        in_specs=vmem_specs(3) + any_specs(4),
        out_specs=vmem_specs(2),
        out_shape=[
            jax.ShapeDtypeStruct((tokens, columns + 128), F32),
            jax.ShapeDtypeStruct((tokens, columns + 128), BF),
        ],
        scratch_shapes=[
            pltpu.VMEM((2 * ROWS, columns), BF),
            pltpu.SemaphoreType.DMA((4,)),
        ],
        compiler_params=params(),
        cost_estimate=pl.CostEstimate(
            flops=8 * tokens * ROWS * columns,
            bytes_accessed=20 * tokens * columns,
            transcendentals=0,
        ),
        name="finish",
    )(normed, begin, low, *blocks)


def combine_kernel(kept, received, up, kv, query, low):
    columns = kv.shape[1] + query.shape[1]
    low_sum = (kept[:, columns:] + received[:, columns:].astype(F32)).astype(BF)
    low[...] = low_sum
    total = kept[:, :columns] + received[:, :columns].astype(F32)
    total += ADAPTER_SCALE * jnp.dot(low_sum, up[...], preferred_element_type=F32)
    kv[...] = total[:, : 2 * HD].astype(BF)
    query[...] = total[:, 2 * HD :].astype(BF)


def combine(kept, received, up):
    tokens = kept.shape[0]
    columns = up.shape[1]
    return pl.pallas_call(
        combine_kernel,
        in_specs=vmem_specs(3),
        out_specs=vmem_specs(3),
        out_shape=[
            jax.ShapeDtypeStruct((tokens, 2 * HD), BF),
            jax.ShapeDtypeStruct((tokens, columns - 2 * HD), BF),
            jax.ShapeDtypeStruct((tokens, 128), BF),
        ],
        compiler_params=params(),
        cost_estimate=pl.CostEstimate(
            flops=2 * tokens * 128 * columns,
            bytes_accessed=8 * tokens * columns,
            transcendentals=0,
        ),
        name="combine",
    )(kept, received, up)


def gain_kernel(count, numbers, normed, dkv0, dkv1, dq0, dq1, ranks, a_rows, *refs):
    sources, (out, held, sems) = refs[:count], refs[count:]
    copies = fetch(sources, held, sems)
    tokens = dq0.shape[0]
    for copy in copies:
        copy.wait()
    for k in range(normed.shape[1] // ROWS):
        at = slice(k * ROWS, (k + 1) * ROWS)
        sums = jnp.zeros((1, ROWS), F32)
        for part, (dkv, dq) in enumerate(((dkv0, dq0), (dkv1, dq1))):
            rows = slice(part * tokens, (part + 1) * tokens)
            term = lax.dot_general(
                dkv[...], held[at, : 2 * HD], (((1,), (1,)), ((), ())), preferred_element_type=F32
            )
            term += lax.dot_general(
                dq[...], held[at, 2 * HD :], (((1,), (1,)), ((), ())), preferred_element_type=F32
            )
            term += lax.dot_general(
                ranks[rows, :], a_rows[at, :], (((1,), (1,)), ((), ())), preferred_element_type=F32
            )
            sums += jnp.sum(term * normed[rows, at].astype(F32), axis=0, keepdims=True)
        for s in range(ROWS // 128):
            out[pl.ds(numbers[k * (ROWS // 128) + s], 1), :] = sums[:, s * 128 : (s + 1) * 128]


def gain_part(numbers, normed, dkv, dq, ranks, a_rows, blocks):
    tokens, width = normed.shape
    columns = blocks[0].shape[1]
    count = len(blocks)
    return pl.pallas_call(
        functools.partial(gain_kernel, count),
        in_specs=[pl.BlockSpec(memory_space=pltpu.SMEM)] + vmem_specs(7) + any_specs(count),
        out_specs=vmem_specs(1)[0],
        out_shape=jax.ShapeDtypeStruct((width // 128, 128), F32),
        scratch_shapes=[
            pltpu.VMEM((width, columns), BF),
            pltpu.SemaphoreType.DMA((count,)),
        ],
        compiler_params=params(),
        cost_estimate=pl.CostEstimate(
            flops=2 * tokens * width * columns,
            bytes_accessed=2 * width * (tokens + columns),
            transcendentals=0,
        ),
        name="gain_part",
    )(numbers, normed, *dkv, *dq, ranks, a_rows, *blocks)


def attend_kernel(
    query, kv, prev, grads, docs_col, docs_row, out, dq, dkv, dprev, dk, dv, dkp, dvp
):
    tokens = kv.shape[0]
    half = tokens // 2
    scale = HD ** (-0.5)
    heads = grads.shape[1] // HD
    own_col = docs_col[...]
    ext_row = docs_row[...]

    def causal(rows, columns, ahead):
        row = lax.broadcasted_iota(jnp.int32, (rows, columns), 0)
        column = lax.broadcasted_iota(jnp.int32, (rows, columns), 1)
        return row + ahead >= column

    plain = (own_col == ext_row[:, half:]) & causal(tokens, tokens, 0)
    early = (own_col[:half] == ext_row[:, :tokens]) & causal(half, tokens, half)
    late = (own_col[half:] == ext_row[:, tokens:]) & causal(half, half, 0)
    k_own, v_own = kv[:, :HD], kv[:, HD:]
    k_early = jnp.concatenate([prev[:, :HD], k_own[:half]], axis=0)
    v_early = jnp.concatenate([prev[:, HD:], v_own[:half]], axis=0)
    k_late, v_late = k_own[half:], v_own[half:]

    def attend(queries, keys, values, cot, allowed):
        scores = (
            lax.dot_general(
                queries, keys, (((1,), (1,)), ((), ())), preferred_element_type=F32
            )
            * scale
        )
        scores = jnp.where(allowed, scores, NEG_FILL)
        expo = jnp.exp(scores - jnp.max(scores, axis=1, keepdims=True))
        probs = expo * (1.0 / jnp.sum(expo, axis=1, keepdims=True))
        probs_low = probs.astype(BF)
        output = jnp.dot(probs_low, values, preferred_element_type=F32).astype(BF)
        delta = jnp.sum(cot.astype(F32) * output.astype(F32), axis=1, keepdims=True)
        dprob = lax.dot_general(
            cot, values, (((1,), (1,)), ((), ())), preferred_element_type=F32
        )
        dscore = (probs * (dprob - delta)).astype(BF)
        dquery = (jnp.dot(dscore, keys, preferred_element_type=F32) * scale).astype(BF)
        dkey = lax.dot_general(
            dscore, queries, (((0,), (0,)), ((), ())), preferred_element_type=F32
        )
        dvalue = lax.dot_general(
            probs_low, cot, (((0,), (0,)), ((), ())), preferred_element_type=F32
        )
        return output, dquery, dkey, dvalue

    dk[...] = jnp.zeros_like(dk)
    dv[...] = jnp.zeros_like(dv)
    dkp[...] = jnp.zeros_like(dkp)
    dvp[...] = jnp.zeros_like(dvp)
    for h in range(heads):
        at = slice(h * HD, (h + 1) * HD)
        queries = query[:, at]
        cot = grads[:, at]
        if h % 2 == 0:
            o, g, a, b = attend(queries, k_own, v_own, cot, plain)
            out[:, at] = o
            dq[:, at] = g
            dk[...] += a
            dv[...] += b
        else:
            o, g, a, b = attend(queries[:half], k_early, v_early, cot[:half], early)
            out[:half, at] = o
            dq[:half, at] = g
            dkp[...] += a[:half]
            dvp[...] += b[:half]
            dk[:half] += a[half:]
            dv[:half] += b[half:]
            o, g, a, b = attend(queries[half:], k_late, v_late, cot[half:], late)
            out[half:, at] = o
            dq[half:, at] = g
            dk[half:] += a
            dv[half:] += b
    dkv[:, :HD] = dk[...] * scale
    dkv[:, HD:] = dv[...]
    dprev[:, :HD] = (dkp[...] * scale).astype(BF)
    dprev[:, HD:] = dvp[...].astype(BF)


def attend(query, kv, prev, grads, docs_col, docs_row):
    tokens, columns = grads.shape
    half = tokens // 2
    return pl.pallas_call(
        attend_kernel,
        out_shape=[
            jax.ShapeDtypeStruct((tokens, columns), BF),
            jax.ShapeDtypeStruct((tokens, columns), BF),
            jax.ShapeDtypeStruct((tokens, 2 * HD), F32),
            jax.ShapeDtypeStruct((half, 2 * HD), BF),
        ],
        scratch_shapes=[
            pltpu.VMEM((tokens, HD), F32),
            pltpu.VMEM((tokens, HD), F32),
            pltpu.VMEM((half, HD), F32),
            pltpu.VMEM((half, HD), F32),
        ],
        compiler_params=params(),
        cost_estimate=pl.CostEstimate(
            flops=2 * 5 * tokens * tokens * columns,
            bytes_accessed=2 * tokens * columns * 4,
            transcendentals=tokens * tokens * columns // HD,
        ),
        name="attend",
    )(query, kv, prev, grads, docs_col, docs_row)


def dot_rows(left, right):
    return lax.dot_general(left, right, (((0,), (0,)), ((), ())), preferred_element_type=F32)


def dot_cols(left, right):
    return lax.dot_general(left, right, (((1,), (1,)), ((), ())), preferred_element_type=F32)


def sum_heads(value):
    low = value.astype(BF)
    total = value
    for step in (1, 2, 3):
        total = total + shift(low, "mp", step).astype(F32)
    return total


def reduce_stage(chunks, whole, move):
    count = whole.shape[0]
    total = jnp.concatenate([whole, chunks[0]], axis=0)
    low = whole.astype(BF)
    for i in (1, 2, 3):
        packed = jnp.concatenate([low, chunks[i].astype(BF)], axis=0)
        total = total + move(packed, REL[i]).astype(F32)
    return total[:count], total[count:]


def per_device(
    hidden,
    gain,
    query_frozen_weight,
    w_key,
    value_frozen_weight,
    a_query,
    query_up_weight,
    a_value,
    value_up_weight,
    doc_ids,
    d_out,
):
    tokens = hidden.shape[1]
    half = tokens // 2
    dp, seq, mp = lax.axis_index("dp"), lax.axis_index("seq"), lax.axis_index("mp")
    pair, high = dp // 4, mp // 2
    hidden_parts = gather_hidden(hidden[0])
    weights = jnp.concatenate([w_key, value_frozen_weight, query_frozen_weight], axis=1)
    first, second = gather_rows(weights)

    squares = jnp.stack(
        [
            sum(jnp.sum(jnp.square(part.astype(F32)), axis=1) for part in parts)
            for parts in hidden_parts
        ]
    )
    squares = squares + shift(squares, "zl", 1)
    number, place, number_at = block_places(dp % 4, seq, mp % 2)
    own_row = jnp.where(pair == high, 0, tokens)
    where = jnp.stack([own_row, tokens - own_row, pair * 32]).astype(jnp.int32)
    a_both = jnp.concatenate([a_query, a_value], axis=1)
    normed, a_rows = prepare(
        number,
        place,
        where,
        [part for parts in hidden_parts for part in parts],
        [squares[0][:, None], squares[1][:, None]],
        gain,
        a_both,
    )
    rank = query_up_weight.shape[0]
    up = jnp.concatenate(
        [
            jnp.concatenate([jnp.zeros((rank, 2 * HD), BF), query_up_weight], axis=1),
            jnp.concatenate(
                [jnp.zeros((rank, HD), BF), value_up_weight, jnp.zeros_like(query_up_weight)], axis=1
            ),
        ],
        axis=0,
    )
    width = normed.shape[1]
    starts = [order * width // 2 + k * ROWS for order in range(2) for k in range(3)]
    partial, low_part = project(normed, a_rows, starts, first[:3] + second[:3])
    starts = [order * width // 2 + 3 * ROWS for order in range(2)]
    kept, sent = finish(normed, partial, low_part, starts, first[3:] + second[3:])
    kv, query, low = combine(kept, shift(sent, "zl", 1), up)
    prev = lax.ppermute(kv[half:], "seq", [(i, i + 1) for i in range(3)])

    docs = doc_ids[0]
    begin = seq * tokens
    own_docs = lax.dynamic_slice_in_dim(docs, begin, tokens)
    prev_docs = lax.dynamic_slice_in_dim(docs, jnp.maximum(begin - half, 0), half)
    prev_docs = jnp.where(seq > 0, prev_docs, -1)
    ext_docs = jnp.concatenate([prev_docs, own_docs])
    output, dq, dkv, dprev = attend(
        query, kv, prev, d_out[0], own_docs[:, None], ext_docs[None, :]
    )
    dq_other = shift(dq, "zl", 1)
    returned = lax.ppermute(dprev, "seq", [(i + 1, i) for i in range(3)]).astype(F32)
    dkv = jnp.concatenate([dkv[:half], dkv[half:] + returned], axis=0).astype(BF)
    dkv_other = shift(dkv, "zl", 1)
    dvalue = dkv[:, HD:]
    ranks = ADAPTER_SCALE * jnp.concatenate(
        [
            jnp.concatenate(
                [dot_cols(a, query_up_weight), dot_cols(b[:, HD:], value_up_weight)], axis=1
            )
            for a, b in ((dq, dkv), (dq_other, dkv_other))
        ],
        axis=0,
    )
    rank_rows = sum_heads(ranks).astype(BF)
    gains = gain_part(
        number_at, normed, (dkv, dkv_other), (dq, dq_other), ranks.astype(BF), a_rows, first + second
    )

    up_rows = [dot_rows(low[:, rank:], dvalue)] + [
        dot_rows(low[:, :rank], dq[:, h * HD : (h + 1) * HD]) for h in range(dq.shape[1] // HD)
    ]
    up_rows = ADAPTER_SCALE * jnp.concatenate(up_rows, axis=0)
    whole = jnp.concatenate([up_rows, gains], axis=0)

    mine = lax.dynamic_slice_in_dim(normed, high * (width // 2), width // 2, 1)
    grad_a = dot_rows(mine, rank_rows).reshape(16, 2, 64, 2 * rank)
    grad_a = lax.dynamic_index_in_dim(grad_a, mp % 2, 1, keepdims=False)
    grad_a = grad_a.reshape(4, 256, 2 * rank)
    whole, grad_a = reduce_stage(grad_a, whole, lambda v, step: shift_plane(v, 0, step))
    grad_a = grad_a.reshape(4, 64, 2 * rank)
    whole, grad_a = reduce_stage(grad_a, whole, lambda v, step: shift_plane(v, 1, step))
    count = up_rows.shape[0]
    other = shift(whole.astype(BF), "zl", 1).astype(F32)
    up_rows = whole[:count] + other[:count]
    gains, other = whole[count:], other[count:]
    gains = jnp.where(
        pair == 0,
        jnp.concatenate([gains, other], axis=0),
        jnp.concatenate([other, gains], axis=0),
    )
    low_gains = gains.astype(BF)
    gain_sum = lax.dynamic_slice_in_dim(gains, mp * 16, 16, 0)
    for step in (1, 2, 3):
        send = lax.dynamic_slice_in_dim(low_gains, (mp ^ step) * 16, 16, 0)
        gain_sum = gain_sum + shift(send, "mp", step).astype(F32)
    gain_sum = gain_sum.reshape(-1)
    gain_own = lax.dynamic_slice_in_dim(gain, mp * gain_sum.shape[0], gain_sum.shape[0])
    up_query = up_rows[64:].reshape(-1, 64, HD).transpose(1, 0, 2).reshape(64, -1)
    return (
        output[None],
        grad_a[:, :rank],
        up_query,
        grad_a[:, rank:],
        up_rows[:64],
        gain_sum / gain_own,
    )


def solution(mesh):
    return jax.shard_map(
        per_device,
        mesh=mesh,
        in_specs=(
            P("dp", "seq", "mp"),
            P(),
            P(("dp", "seq"), "mp"),
            P(("dp", "seq"), "mp"),
            P(("dp", "seq"), "mp"),
            P(),
            P(None, "mp"),
            P(),
            P(None, "mp"),
            P("dp", None),
            P("dp", "seq", "mp"),
        ),
        out_specs=(
            P("dp", "seq", "mp"),
            P(("dp", "seq", "mp"), None),
            P(None, "mp"),
            P(("dp", "seq", "mp"), None),
            P(None, "mp"),
            P("mp"),
        ),
        check_vma=False,
    )
```

```python
import functools

import jax
import jax.numpy as jnp
from jax import lax
from jax.experimental import pallas as pl
from jax.experimental.pallas import tpu as pltpu
from jax.sharding import PartitionSpec as P

HD = 128
EPS = 1e-05
ADAPTER_SCALE = 0.25
NEG_FILL = -1e30
BF = jnp.bfloat16
F32 = jnp.float32
VMEM_LIMIT = 56 * 1024 * 1024
REL = (0, -1, 1, 2)
ROWS = 512


def shift(value, axis, step):
    if axis == "x":
        route = [(z * 4 + i, z * 4 + (i + step) % 4) for z in range(2) for i in range(4)]
        return lax.ppermute(value, "dp", route)
    if axis == "zl":
        return lax.ppermute(value, "dp", [(i, (i + 4) % 8) for i in range(8)])
    if axis == "y":
        return lax.ppermute(value, "seq", [(i, (i + step) % 4) for i in range(4)])
    return lax.ppermute(value, "mp", [(i, i ^ step) for i in range(4)])


def shift_plane(value, stage, step):
    route = []
    for z in range(2):
        for x in range(4):
            for y in range(4):
                for m in range(4):
                    to_x, to_y = x, y
                    if (m < 2) == (stage == 0):
                        to_y = (y + step) % 4
                    else:
                        to_x = (x + step) % 4
                    route.append(
                        (((z * 4 + x) * 4 + y) * 4 + m, ((z * 4 + to_x) * 4 + to_y) * 4 + m)
                    )
    return lax.ppermute(value, ("dp", "seq", "mp"), route)


def params(**kw):
    return pltpu.CompilerParams(vmem_limit_bytes=VMEM_LIMIT, **kw)


def any_specs(count):
    return [pl.BlockSpec(memory_space=pl.ANY)] * count


def vmem_specs(count):
    return [pl.BlockSpec(memory_space=pltpu.VMEM)] * count


def assemble_kernel(*refs):
    pieces, outs = refs[:8], refs[8:]
    rows = pieces[0].shape[0]
    for k, piece in enumerate(pieces):
        outs[k // 4][k % 4 * rows : (k % 4 + 1) * rows, :] = piece[...]


def assemble(pieces):
    rows, columns = pieces[0].shape
    return pl.pallas_call(
        assemble_kernel,
        in_specs=vmem_specs(8),
        out_specs=vmem_specs(2),
        out_shape=[jax.ShapeDtypeStruct((4 * rows, columns), BF)] * 2,
        compiler_params=params(),
        cost_estimate=pl.CostEstimate(
            flops=0, bytes_accessed=32 * rows * columns, transcendentals=0
        ),
        name="assemble",
    )(*pieces)


def gather_rows(shard):
    half = shard.shape[0] // 2
    pieces = []
    for part, axis in ((shard[:half], "x"), (shard[half:], "y")):
        pieces += [part] + [shift(part, axis, -step) for step in REL[1:]]
    blocks = []
    for inner, axis in zip(assemble(pieces), ("y", "x")):
        before, after = shift(inner, axis, 1), shift(inner, axis, -1)
        blocks.append(
            [inner, before, after]
            + [shift(before[: ROWS // 2], axis, 1), shift(after[ROWS // 2 :], axis, -1)]
        )
    return blocks


def tie_kernel(value, other, out):
    del value, other, out


def tie(value, other):
    return pl.pallas_call(
        tie_kernel,
        in_specs=any_specs(2),
        out_specs=any_specs(1)[0],
        out_shape=jax.ShapeDtypeStruct(value.shape, value.dtype),
        input_output_aliases={0: 0},
        compiler_params=params(),
        name="tie",
    )(value, other)


def turn(value, flip_z, flip_core):
    route = []
    for zl in range(2):
        for x in range(4):
            for zh in range(2):
                for c in range(2):
                    target = ((zh ^ flip_z) * 4 + x) * 4 + zl * 2 + (c ^ flip_core)
                    route.append(((zl * 4 + x) * 4 + zh * 2 + c, target))
    return lax.ppermute(value, ("dp", "mp"), route)


def block_places(x, y, core):
    at = jnp.arange(32, dtype=jnp.int32)
    number = ((at // 16) ^ core) * 16 + at % 16
    order, shard = number % 2, number // 2
    inverse = jnp.array([0, 2, 3, 1], jnp.int32)
    by_x = inverse[(shard // 4 - x) % 4]
    by_y = inverse[(shard % 4 - y) % 4]
    outer = jnp.where(order == 0, by_y, by_x)
    inner = jnp.where(order == 0, by_x, by_y)
    place = order * 16 + outer * 4 + inner
    number_at = jnp.sum(jnp.where(place[None, :] == at[:, None], number[None, :], 0), axis=1)
    return number, place, number_at.astype(jnp.int32)


def fetch(sources, held, sems):
    copies = []
    begin = 0
    for k, source in enumerate(sources):
        rows = source.shape[0]
        copies.append(
            pltpu.make_async_copy(source, held.at[pl.ds(begin, rows)], sems.at[k])
        )
        begin += rows
    for copy in copies:
        copy.start()
    return copies


TILE = 256


def project_kernel(number, place, where, p0, p1, p2, p3, gain, a_both, *refs):
    sources, (raw, a_rows, kept, sent, held, sems) = refs[:-6], refs[-6:]
    copies = fetch(sources, held, sems)
    tokens = p0.shape[0]
    per = p0.shape[1] // 128
    for pack, parts in enumerate(((p0, p1), (p2, p3))):
        rows = pl.ds(pl.multiple_of(where[pack], tokens), tokens)
        for r, part in enumerate(parts):

            @pl.loop(0, per)
            def _(i):
                block = where[2] + number[r * per + i]
                target = pl.ds(pl.multiple_of(place[r * per + i] * 128, 128), 128)
                value = part[:, pl.ds(pl.multiple_of(i * 128, 128), 128)].astype(F32)
                raw[rows, target] = (value * gain[pl.ds(block, 1), :]).astype(BF)
                if pack == 0:
                    source = pl.ds(pl.multiple_of(block * 128, 128), 128)
                    a_rows[target, :] = a_both[source, :]

    columns = held.shape[1]
    low = jnp.dot(raw[tokens:, :], a_rows[...], preferred_element_type=F32)
    sent[:, columns:] = low.astype(BF)
    kept[:, columns:] = jnp.dot(raw[:tokens, :], a_rows[...], preferred_element_type=F32)
    for copy in copies:
        copy.wait()

    @pl.loop(0, columns // TILE)
    def _(n):
        at = pl.ds(pl.multiple_of(n * TILE, TILE), TILE)
        sent[:, at] = jnp.dot(raw[tokens:, :], held[:, at], preferred_element_type=F32).astype(BF)
        kept[:, at] = jnp.dot(raw[:tokens, :], held[:, at], preferred_element_type=F32)


def project(number, place, where, parts, gain, a_both, blocks):
    tokens, quarter = parts[0].shape
    columns = blocks[0].shape[1]
    count = len(blocks)
    return pl.pallas_call(
        project_kernel,
        in_specs=[pl.BlockSpec(memory_space=pltpu.SMEM)] * 3 + vmem_specs(6) + any_specs(count),
        out_specs=vmem_specs(4),
        out_shape=[
            jax.ShapeDtypeStruct((2 * tokens, 2 * quarter), BF),
            jax.ShapeDtypeStruct((2 * quarter, 128), BF),
            jax.ShapeDtypeStruct((tokens, columns + 128), F32),
            jax.ShapeDtypeStruct((tokens, columns + 128), BF),
        ],
        scratch_shapes=[
            pltpu.VMEM((2 * quarter, columns), BF),
            pltpu.SemaphoreType.DMA((count,)),
        ],
        compiler_params=params(),
        cost_estimate=pl.CostEstimate(
            flops=8 * tokens * quarter * columns,
            bytes_accessed=4 * quarter * (3 * tokens + columns),
            transcendentals=0,
        ),
        name="project",
    )(number, place, where, *parts, gain.reshape(-1, 128), a_both, *blocks)


def combine_kernel(kept, received, inverse, up, kv, query, low):
    columns = kv.shape[1] + query.shape[1]
    inv = inverse[...]
    low_sum = ((kept[:, columns:] + received[:, columns:].astype(F32)) * inv).astype(BF)
    low[...] = low_sum
    total = (kept[:, :columns] + received[:, :columns].astype(F32)) * inv
    total += ADAPTER_SCALE * jnp.dot(low_sum, up[...], preferred_element_type=F32)
    kv[...] = total[:, : 2 * HD].astype(BF)
    query[...] = total[:, 2 * HD :].astype(BF)


def combine(kept, received, inverse, up):
    tokens = kept.shape[0]
    columns = up.shape[1]
    return pl.pallas_call(
        combine_kernel,
        in_specs=vmem_specs(4),
        out_specs=vmem_specs(3),
        out_shape=[
            jax.ShapeDtypeStruct((tokens, 2 * HD), BF),
            jax.ShapeDtypeStruct((tokens, columns - 2 * HD), BF),
            jax.ShapeDtypeStruct((tokens, 128), BF),
        ],
        compiler_params=params(),
        cost_estimate=pl.CostEstimate(
            flops=2 * tokens * 128 * columns,
            bytes_accessed=8 * tokens * columns,
            transcendentals=0,
        ),
        name="combine",
    )(kept, received, inverse, up)


def gain_kernel(count, numbers, raw, dkv, dq, ranks, inverse, a_rows, *refs):
    sources, (out, held, sems) = refs[:count], refs[count:]
    copies = fetch(sources, held, sems)
    for copy in copies:
        copy.wait()
    per = ROWS // 128

    @pl.loop(0, raw.shape[1] // ROWS)
    def _(k):
        at = pl.ds(pl.multiple_of(k * ROWS, ROWS), ROWS)
        term = lax.dot_general(
            dkv[...], held[at, : 2 * HD], (((1,), (1,)), ((), ())), preferred_element_type=F32
        )
        term += lax.dot_general(
            dq[...], held[at, 2 * HD :], (((1,), (1,)), ((), ())), preferred_element_type=F32
        )
        term += lax.dot_general(
            ranks[...], a_rows[at, :], (((1,), (1,)), ((), ())), preferred_element_type=F32
        )
        sums = jnp.sum(term * inverse[...] * raw[:, at].astype(F32), axis=0, keepdims=True)
        for s in range(per):
            out[pl.ds(numbers[k * per + s], 1), :] = sums[:, s * 128 : (s + 1) * 128]


def gain_part(part, numbers, raw, dkv, dq, ranks, inverse, a_rows, blocks):
    tokens, width = dq.shape[0], raw.shape[1]
    columns = blocks[0].shape[1]
    count = len(blocks)
    return pl.pallas_call(
        functools.partial(gain_kernel, count),
        grid=(1,),
        in_specs=[
            pl.BlockSpec(memory_space=pltpu.SMEM),
            pl.BlockSpec((tokens, width), lambda j: (part, 0)),
        ]
        + vmem_specs(5)
        + any_specs(count),
        out_specs=vmem_specs(1)[0],
        out_shape=jax.ShapeDtypeStruct((width // 128, 128), F32),
        scratch_shapes=[
            pltpu.VMEM((width, columns), BF),
            pltpu.SemaphoreType.DMA((count,)),
        ],
        compiler_params=params(),
        cost_estimate=pl.CostEstimate(
            flops=2 * tokens * width * columns,
            bytes_accessed=2 * width * (tokens + columns),
            transcendentals=0,
        ),
        name="gain_part",
    )(numbers, raw, dkv, dq, ranks, inverse, a_rows, *blocks)


def attend_kernel(odd, query, kv, prev, grads, docs_row, docs_col, *refs):
    if odd:
        out, dq, dkv, dprev, dk, dv = refs
    else:
        out, dq, dkv, dk, dv = refs
    tokens = kv.shape[0]
    half = tokens // 2
    scale = HD ** (-0.5)
    if odd:
        keys = jnp.concatenate([prev[:, :HD], kv[:, :HD]], axis=0)
        values = jnp.concatenate([prev[:, HD:], kv[:, HD:]], axis=0)
        spans = ((0, tokens), (tokens, tokens + half))
        doc_keys = docs_col[...]
        before = half
    else:
        keys, values = kv[:, :HD], kv[:, HD:]
        spans = ((0, half), (0, tokens))
        doc_keys = docs_col[half:, :]
        before = 0
    dk[...] = jnp.zeros_like(dk)
    dv[...] = jnp.zeros_like(dv)
    for part, (low, high) in enumerate(spans):
        rows = slice(part * half, (part + 1) * half)
        key_at = lax.broadcasted_iota(jnp.int32, (high - low, half), 0) + (low - before)
        query_at = lax.broadcasted_iota(jnp.int32, (high - low, half), 1) + part * half
        allowed = (doc_keys[low:high, :] == docs_row[:, rows]) & (key_at <= query_at)
        key, value = keys[low:high], values[low:high]
        for h in range(dq.shape[1] // HD):
            source = slice((2 * h + odd) * HD, (2 * h + odd + 1) * HD)
            target = slice(h * HD, (h + 1) * HD)
            row_query, cot = query[rows, source], grads[rows, source]
            scores = (
                lax.dot_general(
                    key, row_query, (((1,), (1,)), ((), ())), preferred_element_type=F32
                )
                * scale
            )
            scores = jnp.where(allowed, scores, NEG_FILL)
            expo = jnp.exp(scores - jnp.max(scores, axis=0, keepdims=True))
            probs = expo * (1.0 / jnp.sum(expo, axis=0, keepdims=True))
            probs_low = probs.astype(BF)
            output = lax.dot_general(
                value, probs_low, (((0,), (0,)), ((), ())), preferred_element_type=F32
            )
            out[rows, target] = output.T.astype(BF)
            dprob = lax.dot_general(
                value, cot, (((1,), (1,)), ((), ())), preferred_element_type=F32
            )
            delta = jnp.sum(probs_low.astype(F32) * dprob, axis=0, keepdims=True)
            dscore = (probs * (dprob - delta)).astype(BF)
            dquery = lax.dot_general(
                key, dscore, (((0,), (0,)), ((), ())), preferred_element_type=F32
            )
            dq[rows, target] = (dquery * scale).T.astype(BF)
            dk[low:high, :] += jnp.dot(dscore, row_query, preferred_element_type=F32)
            dv[low:high, :] += jnp.dot(probs_low, cot, preferred_element_type=F32)
    dkv[:, :HD] = dk[before:, :] * scale
    dkv[:, HD:] = dv[before:, :]
    if odd:
        dprev[:, :HD] = (dk[:before, :] * scale).astype(BF)
        dprev[:, HD:] = dv[:before, :].astype(BF)


def attend(odd, query, kv, prev, grads, docs_row, docs_col):
    tokens, columns = grads.shape
    half = tokens // 2
    span = tokens + half if odd else tokens
    outs = [
        jax.ShapeDtypeStruct((tokens, columns // 2), BF),
        jax.ShapeDtypeStruct((tokens, columns // 2), BF),
        jax.ShapeDtypeStruct((tokens, 2 * HD), F32),
    ]
    if odd:
        outs.append(jax.ShapeDtypeStruct((half, 2 * HD), BF))
    return pl.pallas_call(
        functools.partial(attend_kernel, odd),
        in_specs=vmem_specs(6),
        out_specs=vmem_specs(len(outs)),
        out_shape=outs,
        scratch_shapes=[pltpu.VMEM((span, HD), F32)] * 2,
        compiler_params=params(),
        cost_estimate=pl.CostEstimate(
            flops=5 * tokens * tokens * columns,
            bytes_accessed=4 * tokens * columns,
            transcendentals=tokens * tokens * columns // (2 * HD),
        ),
        name="attend",
    )(query, kv, prev, grads, docs_row, docs_col)


def dot_rows(left, right):
    return lax.dot_general(left, right, (((0,), (0,)), ((), ())), preferred_element_type=F32)


def dot_cols(left, right):
    return lax.dot_general(left, right, (((1,), (1,)), ((), ())), preferred_element_type=F32)


def sum_heads(value):
    low = value.astype(BF)
    total = value
    for step in (1, 2, 3):
        total = total + shift(low, "mp", step).astype(F32)
    return total


def reduce_stage(chunks, whole, move):
    count = whole.shape[0]
    total = jnp.concatenate([whole, chunks[0]], axis=0)
    low = whole.astype(BF)
    for i in (1, 2, 3):
        packed = jnp.concatenate([low, chunks[i].astype(BF)], axis=0)
        total = total + move(packed, REL[i]).astype(F32)
    return total[:count], total[count:]


def per_device(
    hidden,
    gain,
    query_frozen_weight,
    w_key,
    value_frozen_weight,
    a_query,
    query_up_weight,
    a_value,
    value_up_weight,
    doc_ids,
    d_out,
):
    tokens = hidden.shape[1]
    half = tokens // 2
    dp, seq, mp = lax.axis_index("dp"), lax.axis_index("seq"), lax.axis_index("mp")
    pair, high = dp // 4, mp // 2
    own = hidden[0]
    turned = turn(own, 0, 0)
    weights = jnp.concatenate([w_key, value_frozen_weight, query_frozen_weight], axis=1)
    first, second = gather_rows(weights)
    turned = tie(turned, first[0])
    turned_high = shift(turned, "mp", 2)
    hidden_parts = [turned, shift(turned, "mp", 1), turned_high, shift(turned_high, "mp", 1)]

    square = jnp.sum(jnp.square(own.astype(F32)), axis=1).reshape(-1, 128)
    square = tie(square, first[1])
    square_sum = square
    for step in (1, 2, 3):
        square_sum = square_sum + shift(square, "mp", step)
    features = gain.shape[0]
    inverse = lax.rsqrt(square_sum * (1.0 / features) + EPS)
    inverses = (inverse.reshape(-1, 1), shift(inverse, "zl", 1).reshape(-1, 1))
    number, place, number_at = block_places(dp % 4, seq, mp % 2)
    own_row = jnp.where(pair == high, 0, tokens)
    where = jnp.stack([own_row, tokens - own_row, pair * 32]).astype(jnp.int32)
    a_both = jnp.concatenate([a_query, a_value], axis=1)
    raw, a_rows, kept, sent = project(
        number, place, where, hidden_parts, gain, a_both, first + second
    )
    rank = query_up_weight.shape[0]
    up = jnp.concatenate(
        [
            jnp.concatenate([jnp.zeros((rank, 2 * HD), BF), query_up_weight], axis=1),
            jnp.concatenate(
                [jnp.zeros((rank, HD), BF), value_up_weight, jnp.zeros_like(query_up_weight)], axis=1
            ),
        ],
        axis=0,
    )
    kv, query, low = combine(kept, shift(sent, "zl", 1), inverses[0], up)
    prev = lax.ppermute(kv[half:], "seq", [(i, i + 1) for i in range(3)])

    docs = doc_ids[0]
    begin = seq * tokens
    own_docs = lax.dynamic_slice_in_dim(docs, begin, tokens)
    prev_docs = lax.dynamic_slice_in_dim(docs, jnp.maximum(begin - half, 0), half)
    prev_docs = jnp.where(seq > 0, prev_docs, -1)
    ext_docs = jnp.concatenate([prev_docs, own_docs])
    masks = (own_docs[None, :], ext_docs[:, None])
    out_even, dq_even, dkv_even = attend(0, query, kv, kv[half:], d_out[0], *masks)
    dq_even_other = shift(dq_even, "zl", 1)
    out_odd, dq_odd, dkv_odd, dprev = attend(1, query, kv, prev, d_out[0], *masks)
    dq_odd_other = shift(dq_odd, "zl", 1)
    returned = lax.ppermute(dprev, "seq", [(i + 1, i) for i in range(3)]).astype(F32)
    dkv = dkv_even + dkv_odd
    dkv = jnp.concatenate([dkv[:half], dkv[half:] + returned], axis=0).astype(BF)
    dkv_other = shift(dkv, "zl", 1)
    dvalue = dkv[:, HD:]

    def interleave(even, odd):
        pieces = []
        for h in range(even.shape[1] // HD):
            at = slice(h * HD, (h + 1) * HD)
            pieces += [even[:, at], odd[:, at]]
        return jnp.concatenate(pieces, axis=1)

    output = interleave(out_even, out_odd)
    dq, dq_other = interleave(dq_even, dq_odd), interleave(dq_even_other, dq_odd_other)
    ranks, gains = [], 0.0
    for part, (a, b) in enumerate(((dq, dkv), (dq_other, dkv_other))):
        ranks.append(
            ADAPTER_SCALE
            * jnp.concatenate(
                [dot_cols(a, query_up_weight), dot_cols(b[:, HD:], value_up_weight)], axis=1
            )
        )
        gains = gains + gain_part(
            part,
            number_at,
            raw,
            b,
            a,
            ranks[part].astype(BF),
            inverses[part],
            a_rows,
            first + second,
        )
    rank_rows = sum_heads(jnp.concatenate(ranks, axis=0))
    rank_rows = (rank_rows * jnp.concatenate(inverses, axis=0)).astype(BF)

    up_rows = [dot_rows(low[:, rank:], dvalue)] + [
        dot_rows(low[:, :rank], dq[:, h * HD : (h + 1) * HD]) for h in range(dq.shape[1] // HD)
    ]
    up_rows = ADAPTER_SCALE * jnp.concatenate(up_rows, axis=0)
    whole = jnp.concatenate([up_rows, gains], axis=0)

    width = raw.shape[1]
    mine = lax.dynamic_slice_in_dim(raw, high * (width // 2), width // 2, 1)
    grad_a = dot_rows(mine, rank_rows).reshape(16, 2, 64, 2 * rank)
    grad_a = lax.dynamic_index_in_dim(grad_a, mp % 2, 1, keepdims=False)
    grad_a = grad_a.reshape(4, 256, 2 * rank)
    whole, grad_a = reduce_stage(grad_a, whole, lambda v, step: shift_plane(v, 0, step))
    grad_a = grad_a.reshape(4, 64, 2 * rank)
    whole, grad_a = reduce_stage(grad_a, whole, lambda v, step: shift_plane(v, 1, step))
    count = up_rows.shape[0]
    up_rows = whole[:count] + shift(whole[:count].astype(BF), "zl", 1).astype(F32)
    gains = whole[count:].astype(BF)
    gain_sum = jnp.zeros((16, 128), F32)
    for flip_core in range(2):
        send = lax.dynamic_slice_in_dim(gains, (mp % 2 ^ flip_core) * 16, 16, 0)
        for flip_z in range(2):
            gain_sum = gain_sum + turn(send, flip_z, flip_core).astype(F32)
    gain_sum = gain_sum.reshape(-1)
    gain_own = lax.dynamic_slice_in_dim(gain, mp * gain_sum.shape[0], gain_sum.shape[0])
    up_query = up_rows[64:].reshape(-1, 64, HD).transpose(1, 0, 2).reshape(64, -1)
    return (
        output[None],
        grad_a[:, :rank],
        up_query,
        grad_a[:, rank:],
        up_rows[:64],
        gain_sum / gain_own,
    )


def solution(mesh):
    return jax.shard_map(
        per_device,
        mesh=mesh,
        in_specs=(
            P("dp", "seq", "mp"),
            P(),
            P(("dp", "seq"), "mp"),
            P(("dp", "seq"), "mp"),
            P(("dp", "seq"), "mp"),
            P(),
            P(None, "mp"),
            P(),
            P(None, "mp"),
            P("dp", None),
            P("dp", "seq", "mp"),
        ),
        out_specs=(
            P("dp", "seq", "mp"),
            P(("dp", "seq", "mp"), None),
            P(None, "mp"),
            P(("dp", "seq", "mp"), None),
            P(None, "mp"),
            P("mp"),
        ),
        check_vma=False,
    )
```

```python
import functools

import jax
import jax.numpy as jnp
from jax import lax
from jax.experimental import pallas as pl
from jax.experimental.pallas import tpu as pltpu
from jax.sharding import PartitionSpec as P

HD = 128
EPS = 1e-05
ADAPTER_SCALE = 0.25
NEG_FILL = -1e30
BF = jnp.bfloat16
F32 = jnp.float32
VMEM_LIMIT = 34 * 1024 * 1024
REL = (0, -1, 1, 2)
ROWS = 512


def shift(value, axis, step):
    if axis == "x":
        route = [(z * 4 + i, z * 4 + (i + step) % 4) for z in range(2) for i in range(4)]
        return lax.ppermute(value, "dp", route)
    if axis == "dp":
        return lax.ppermute(value, "dp", [(i, i ^ step) for i in range(8)])
    if axis == "zl":
        return lax.ppermute(value, "dp", [(i, (i + 4) % 8) for i in range(8)])
    if axis == "seq":
        return lax.ppermute(value, "seq", [(i, i ^ step) for i in range(4)])
    if axis == "y":
        return lax.ppermute(value, "seq", [(i, (i + step) % 4) for i in range(4)])
    return lax.ppermute(value, "mp", [(i, i ^ step) for i in range(4)])


def shift_plane(value, stage, step):
    route = []
    for z in range(2):
        for x in range(4):
            for y in range(4):
                for m in range(4):
                    to_x, to_y = x, y
                    if (m < 2) == (stage == 0):
                        to_y = (y + step) % 4
                    else:
                        to_x = (x + step) % 4
                    route.append(
                        (((z * 4 + x) * 4 + y) * 4 + m, ((z * 4 + to_x) * 4 + to_y) * 4 + m)
                    )
    return lax.ppermute(value, ("dp", "seq", "mp"), route)


def params(**kw):
    return pltpu.CompilerParams(vmem_limit_bytes=VMEM_LIMIT, **kw)


def any_specs(count):
    return [pl.BlockSpec(memory_space=pl.ANY)] * count


def vmem_specs(count):
    return [pl.BlockSpec(memory_space=pltpu.VMEM)] * count


def assemble_kernel(*refs):
    pieces, outs = refs[:8], refs[-2:]
    rows = pieces[0].shape[0]
    for k, piece in enumerate(pieces):
        outs[k // 4][k % 4 * rows : (k % 4 + 1) * rows, :] = piece[...]


def assemble(pieces, *others):
    rows, columns = pieces[0].shape
    return pl.pallas_call(
        assemble_kernel,
        in_specs=vmem_specs(8) + any_specs(len(others)),
        out_specs=vmem_specs(2),
        out_shape=[jax.ShapeDtypeStruct((4 * rows, columns), BF)] * 2,
        compiler_params=params(),
        cost_estimate=pl.CostEstimate(
            flops=0, bytes_accessed=32 * rows * columns, transcendentals=0
        ),
        name="assemble",
    )(*pieces, *others)


def first_rings(shard):
    half = shard.shape[0] // 2
    pieces = []
    for part, axis in ((shard[:half], "x"), (shard[half:], "y")):
        pieces += [part] + [shift(part, axis, -step) for step in REL[1:]]
    return pieces


def second_rings(inners):
    blocks = []
    for inner, axis in zip(inners, ("y", "x")):
        before, after = shift(inner, axis, 1), shift(inner, axis, -1)
        blocks.append(
            [inner, before, after]
            + [shift(before[: ROWS // 2], axis, 1), shift(after[ROWS // 2 :], axis, -1)]
        )
    return blocks


def tie_kernel(*refs):
    del refs


def tie(value, *others):
    return pl.pallas_call(
        tie_kernel,
        in_specs=any_specs(1 + len(others)),
        out_specs=any_specs(1)[0],
        out_shape=jax.ShapeDtypeStruct(value.shape, value.dtype),
        input_output_aliases={0: 0},
        compiler_params=params(),
        name="tie",
    )(value, *others)


def turn(value, flip_z, flip_core):
    route = []
    for zl in range(2):
        for x in range(4):
            for zh in range(2):
                for c in range(2):
                    target = ((zh ^ flip_z) * 4 + x) * 4 + zl * 2 + (c ^ flip_core)
                    route.append(((zl * 4 + x) * 4 + zh * 2 + c, target))
    return lax.ppermute(value, ("dp", "mp"), route)


def block_places(x, y, core):
    at = jnp.arange(32, dtype=jnp.int32)
    number = ((at // 16) ^ core) * 16 + at % 16
    order, shard = number % 2, number // 2
    inverse = jnp.array([0, 2, 3, 1], jnp.int32)
    by_x = inverse[(shard // 4 - x) % 4]
    by_y = inverse[(shard % 4 - y) % 4]
    outer = jnp.where(order == 0, by_y, by_x)
    inner = jnp.where(order == 0, by_x, by_y)
    place = order * 16 + outer * 4 + inner
    number_at = jnp.sum(jnp.where(place[None, :] == at[:, None], number[None, :], 0), axis=1)
    return number, place, number_at.astype(jnp.int32)


def fetch(sources, held, sems):
    copies = []
    begin = 0
    for k, source in enumerate(sources):
        rows = source.shape[0]
        copies.append(
            pltpu.make_async_copy(source, held.at[pl.ds(begin, rows)], sems.at[k])
        )
        begin += rows
    for copy in copies:
        copy.start()
    return copies


TILE = 256


def project_kernel(own, number, place, where, p0, p1, p2, p3, gain, a_both, other, *refs):
    del other
    if own:
        sources, (raw, out, taken, held, sems, take_sems) = refs[:-6], refs[-6:]
        a_rows = a_both
    else:
        sources, (raw, out, a_rows, taken, held, sems, take_sems) = refs[:-7], refs[-7:]

    def take(parts):
        return [pltpu.make_async_copy(p, taken.at[k], take_sems.at[k]) for k, p in enumerate(parts)]

    @pl.when(where[0] == (0 if own else 1))
    def _():
        for copy in take((p0, p1)):
            copy.start()

    @pl.when(where[0] != (0 if own else 1))
    def _():
        for copy in take((p2, p3)):
            copy.start()

    copies = fetch(sources, held, sems)
    for copy in take((p0, p1)):
        copy.wait()
    per = taken.shape[2] // 128
    for r in range(2):

        @pl.loop(0, per)
        def _(i):
            block = where[1] + number[r * per + i]
            target = pl.ds(pl.multiple_of(place[r * per + i] * 128, 128), 128)
            value = taken[r, :, pl.ds(pl.multiple_of(i * 128, 128), 128)].astype(F32)
            raw[:, target] = (value * gain[pl.ds(block, 1), :]).astype(BF)
            if not own:
                source = pl.ds(pl.multiple_of(block * 128, 128), 128)
                a_rows[target, :] = a_both[source, :]

    columns = held.shape[1]
    low = jnp.dot(raw[...], a_rows[...], preferred_element_type=F32)
    out[:, columns:] = low.astype(out.dtype)
    for copy in copies:
        copy.wait()

    @pl.loop(0, columns // TILE)
    def _(n):
        at = pl.ds(pl.multiple_of(n * TILE, TILE), TILE)
        total = jnp.dot(raw[...], held[:, at], preferred_element_type=F32)
        out[:, at] = total.astype(out.dtype)


def project(own, number, place, where, parts, gain, a_both, other, blocks):
    tokens, quarter = parts[0].shape
    columns = blocks[0].shape[1]
    count = len(blocks)
    outs = [
        jax.ShapeDtypeStruct((tokens, 2 * quarter), BF),
        jax.ShapeDtypeStruct((tokens, columns + 128), F32 if own else BF),
    ]
    if not own:
        outs.append(jax.ShapeDtypeStruct((2 * quarter, 128), BF))
    return pl.pallas_call(
        functools.partial(project_kernel, own),
        in_specs=[pl.BlockSpec(memory_space=pltpu.SMEM)] * 3
        + any_specs(4)
        + vmem_specs(2)
        + any_specs(1 + count),
        out_specs=vmem_specs(len(outs)),
        out_shape=outs,
        scratch_shapes=[
            pltpu.VMEM((2, tokens, quarter), BF),
            pltpu.VMEM((2 * quarter, columns), BF),
            pltpu.SemaphoreType.DMA((count,)),
            pltpu.SemaphoreType.DMA((2,)),
        ],
        compiler_params=params(),
        cost_estimate=pl.CostEstimate(
            flops=4 * tokens * quarter * columns,
            bytes_accessed=4 * quarter * (2 * tokens + columns),
            transcendentals=0,
        ),
        name="project",
    )(number, place, where, *parts, gain.reshape(-1, 128), a_both, other, *blocks)


def combine_kernel(kept, received, inverse, up, kv, query, low):
    columns = kv.shape[1] + query.shape[1]
    inv = inverse[...]
    low_sum = ((kept[:, columns:] + received[:, columns:].astype(F32)) * inv).astype(BF)
    low[...] = low_sum
    total = (kept[:, :columns] + received[:, :columns].astype(F32)) * inv
    total += ADAPTER_SCALE * jnp.dot(low_sum, up[...], preferred_element_type=F32)
    kv[...] = total[:, : 2 * HD].astype(BF)
    query[...] = total[:, 2 * HD :].astype(BF)


def combine(kept, received, inverse, up):
    tokens = kept.shape[0]
    columns = up.shape[1]
    return pl.pallas_call(
        combine_kernel,
        in_specs=vmem_specs(4),
        out_specs=vmem_specs(3),
        out_shape=[
            jax.ShapeDtypeStruct((tokens, 2 * HD), BF),
            jax.ShapeDtypeStruct((tokens, columns - 2 * HD), BF),
            jax.ShapeDtypeStruct((tokens, 128), BF),
        ],
        compiler_params=params(),
        cost_estimate=pl.CostEstimate(
            flops=2 * tokens * 128 * columns,
            bytes_accessed=8 * tokens * columns,
            transcendentals=0,
        ),
        name="combine",
    )(kept, received, inverse, up)


def gain_kernel(count, numbers, raw, dkv, dq, ranks, inverse, a_rows, *refs):
    sources, (out, held, sems) = refs[:count], refs[count:]
    copies = fetch(sources, held, sems)
    for copy in copies:
        copy.wait()
    per = ROWS // 128

    @pl.loop(0, raw.shape[1] // ROWS)
    def _(k):
        at = pl.ds(pl.multiple_of(k * ROWS, ROWS), ROWS)
        term = lax.dot_general(
            dkv[...], held[at, : 2 * HD], (((1,), (1,)), ((), ())), preferred_element_type=F32
        )
        term += lax.dot_general(
            dq[...], held[at, 2 * HD :], (((1,), (1,)), ((), ())), preferred_element_type=F32
        )
        term += lax.dot_general(
            ranks[...], a_rows[at, :], (((1,), (1,)), ((), ())), preferred_element_type=F32
        )
        sums = jnp.sum(term * inverse[...] * raw[:, at].astype(F32), axis=0, keepdims=True)
        for s in range(per):
            out[pl.ds(numbers[k * per + s], 1), :] = sums[:, s * 128 : (s + 1) * 128]


def gain_part(numbers, raw, dkv, dq, ranks, inverse, a_rows, blocks):
    tokens, width = dq.shape[0], raw.shape[1]
    columns = blocks[0].shape[1]
    count = len(blocks)
    return pl.pallas_call(
        functools.partial(gain_kernel, count),
        in_specs=[
            pl.BlockSpec(memory_space=pltpu.SMEM),
        ]
        + vmem_specs(6)
        + any_specs(count),
        out_specs=vmem_specs(1)[0],
        out_shape=jax.ShapeDtypeStruct((width // 128, 128), F32),
        scratch_shapes=[
            pltpu.VMEM((width, columns), BF),
            pltpu.SemaphoreType.DMA((count,)),
        ],
        compiler_params=params(),
        cost_estimate=pl.CostEstimate(
            flops=2 * tokens * width * columns,
            bytes_accessed=2 * width * (tokens + columns),
            transcendentals=0,
        ),
        name="gain_part",
    )(numbers, raw, dkv, dq, ranks, inverse, a_rows, *blocks)


def unite_kernel(partner, dq0, dq1, dkv0, dkv1, returned, up_query, up_value, dq, dkv, ranks):
    rank = up_query.shape[0]
    half = returned.shape[0]
    for h in range(dq.shape[1] // HD):
        source = (dq0, dq1)[h % 2]
        dq[:, h * HD : (h + 1) * HD] = source[:, h // 2 * HD : (h // 2 + 1) * HD]
    if partner:
        dkv[...] = dkv0[...]
    else:
        dkv[:half, :] = (dkv0[:half, :] + dkv1[:half, :]).astype(BF)
        dkv[half:, :] = (dkv0[half:, :] + dkv1[half:, :] + returned[...].astype(F32)).astype(BF)
    nt = (((1,), (1,)), ((), ()))
    of_query = lax.dot_general(dq[...], up_query[...], nt, preferred_element_type=F32)
    of_value = lax.dot_general(dkv[:, HD:], up_value[...], nt, preferred_element_type=F32)
    ranks[:, :rank] = (ADAPTER_SCALE * of_query).astype(BF)
    ranks[:, rank:] = (ADAPTER_SCALE * of_value).astype(BF)


def unite(partner, dq0, dq1, dkv0, dkv1, returned, up_query, up_value):
    tokens, columns = dq0.shape
    return pl.pallas_call(
        functools.partial(unite_kernel, partner),
        in_specs=vmem_specs(7),
        out_specs=vmem_specs(3),
        out_shape=[
            jax.ShapeDtypeStruct((tokens, 2 * columns), BF),
            jax.ShapeDtypeStruct((tokens, 2 * HD), BF),
            jax.ShapeDtypeStruct((tokens, 128), BF),
        ],
        compiler_params=params(),
        cost_estimate=pl.CostEstimate(
            flops=4 * tokens * columns * 64, bytes_accessed=8 * tokens * columns, transcendentals=0
        ),
        name="unite",
    )(dq0, dq1, dkv0, dkv1, returned, up_query, up_value)


def attend_kernel(odd, query, kv, prev, grads, docs_row, docs_col, *refs):
    if odd:
        out, dq, dkv, dprev, dk, dv = refs
    else:
        out, dq, dkv, dk, dv = refs
    tokens = kv.shape[0]
    half = tokens // 2
    scale = HD ** (-0.5)
    if odd:
        keys = jnp.concatenate([prev[:, :HD], kv[:, :HD]], axis=0)
        values = jnp.concatenate([prev[:, HD:], kv[:, HD:]], axis=0)
        spans = ((0, tokens), (tokens, tokens + half))
        doc_keys = docs_col[...]
        before = half
    else:
        keys, values = kv[:, :HD], kv[:, HD:]
        spans = ((0, half), (0, tokens))
        doc_keys = docs_col[half:, :]
        before = 0
    dk[...] = jnp.zeros_like(dk)
    dv[...] = jnp.zeros_like(dv)
    for part, (low, high) in enumerate(spans):
        rows = slice(part * half, (part + 1) * half)
        key_at = lax.broadcasted_iota(jnp.int32, (high - low, half), 0) + (low - before)
        query_at = lax.broadcasted_iota(jnp.int32, (high - low, half), 1) + part * half
        allowed = (doc_keys[low:high, :] == docs_row[:, rows]) & (key_at <= query_at)
        key, value = keys[low:high], values[low:high]
        for h in range(dq.shape[1] // HD):
            source = slice((2 * h + odd) * HD, (2 * h + odd + 1) * HD)
            target = slice(h * HD, (h + 1) * HD)
            row_query, cot = query[rows, source], grads[rows, source]
            scores = (
                lax.dot_general(
                    key, row_query, (((1,), (1,)), ((), ())), preferred_element_type=F32
                )
                * scale
            )
            scores = jnp.where(allowed, scores, NEG_FILL)
            expo = jnp.exp(scores - jnp.max(scores, axis=0, keepdims=True))
            probs = expo * (1.0 / jnp.sum(expo, axis=0, keepdims=True))
            probs_low = probs.astype(BF)
            output = lax.dot_general(
                value, probs_low, (((0,), (0,)), ((), ())), preferred_element_type=F32
            )
            out[rows, target] = output.T.astype(BF)
            dprob = lax.dot_general(
                value, cot, (((1,), (1,)), ((), ())), preferred_element_type=F32
            )
            delta = jnp.sum(probs_low.astype(F32) * dprob, axis=0, keepdims=True)
            dscore = (probs * (dprob - delta)).astype(BF)
            dquery = lax.dot_general(
                key, dscore, (((0,), (0,)), ((), ())), preferred_element_type=F32
            )
            dq[rows, target] = (dquery * scale).T.astype(BF)
            dk[low:high, :] += jnp.dot(dscore, row_query, preferred_element_type=F32)
            dv[low:high, :] += jnp.dot(probs_low, cot, preferred_element_type=F32)
    dkv[:, :HD] = dk[before:, :] * scale
    dkv[:, HD:] = dv[before:, :]
    if odd:
        dprev[:, :HD] = (dk[:before, :] * scale).astype(BF)
        dprev[:, HD:] = dv[:before, :].astype(BF)


def attend(odd, query, kv, prev, grads, docs_row, docs_col):
    tokens, columns = grads.shape
    half = tokens // 2
    span = tokens + half if odd else tokens
    outs = [
        jax.ShapeDtypeStruct((tokens, columns // 2), BF),
        jax.ShapeDtypeStruct((tokens, columns // 2), BF),
        jax.ShapeDtypeStruct((tokens, 2 * HD), F32),
    ]
    if odd:
        outs.append(jax.ShapeDtypeStruct((half, 2 * HD), BF))
    return pl.pallas_call(
        functools.partial(attend_kernel, odd),
        in_specs=vmem_specs(6),
        out_specs=vmem_specs(len(outs)),
        out_shape=outs,
        scratch_shapes=[pltpu.VMEM((span, HD), F32)] * 2,
        compiler_params=params(),
        cost_estimate=pl.CostEstimate(
            flops=5 * tokens * tokens * columns,
            bytes_accessed=4 * tokens * columns,
            transcendentals=tokens * tokens * columns // (2 * HD),
        ),
        name="attend",
    )(query, kv, prev, grads, docs_row, docs_col)


def dot_rows(left, right):
    return lax.dot_general(left, right, (((0,), (0,)), ((), ())), preferred_element_type=F32)


def dot_cols(left, right):
    return lax.dot_general(left, right, (((1,), (1,)), ((), ())), preferred_element_type=F32)


def sum_heads(value):
    total = value.astype(F32)
    for step in (1, 2, 3):
        total = total + shift(value, "mp", step).astype(F32)
    return total


def reduce_stage(chunks, whole, move):
    count = whole.shape[0]
    total = jnp.concatenate([whole, chunks[0]], axis=0)
    low = whole.astype(BF)
    for i in (1, 2, 3):
        packed = jnp.concatenate([low, chunks[i].astype(BF)], axis=0)
        total = total + move(packed, REL[i]).astype(F32)
    return total[:count], total[count:]


def per_device(
    hidden,
    gain,
    query_frozen_weight,
    w_key,
    value_frozen_weight,
    a_query,
    query_up_weight,
    a_value,
    value_up_weight,
    doc_ids,
    d_out,
):
    tokens = hidden.shape[1]
    half = tokens // 2
    dp, seq, mp = lax.axis_index("dp"), lax.axis_index("seq"), lax.axis_index("mp")
    pair, high = dp // 4, mp // 2
    own = hidden[0]
    turned = turn(own, 0, 0)
    weights = jnp.concatenate([w_key, value_frozen_weight, query_frozen_weight], axis=1)
    pieces = first_rings(weights)
    turned = tie(turned, *pieces[1:4], *pieces[5:])
    turned_high = shift(turned, "mp", 2)
    hidden_parts = [turned, shift(turned, "mp", 1), turned_high, shift(turned_high, "mp", 1)]
    a_both = jnp.concatenate([a_query, a_value], axis=1)
    square = jnp.sum(jnp.square(own.astype(F32)).reshape(tokens, -1, 128), axis=1)
    square = lax.psum(square, "mp")
    first, second = second_rings(assemble(pieces, a_both))
    number, place, number_at = block_places(dp % 4, seq, mp % 2)
    where = jnp.stack([jnp.where(pair == high, 0, 1), pair * 32]).astype(jnp.int32)
    raw_other, sent, a_rows = project(
        False, number, place, where, hidden_parts, gain, a_both, a_both, first + second
    )
    received = shift(sent, "zl", 1)
    raw_own, kept = project(
        True, number, place, where, hidden_parts, gain, a_rows, sent, first + second
    )
    rank = query_up_weight.shape[0]
    up = jnp.concatenate(
        [
            jnp.concatenate([jnp.zeros((rank, 2 * HD), BF), query_up_weight], axis=1),
            jnp.concatenate(
                [jnp.zeros((rank, HD), BF), value_up_weight, jnp.zeros_like(query_up_weight)], axis=1
            ),
        ],
        axis=0,
    )
    square = jnp.sum(square, axis=1, keepdims=True)
    inverse = lax.rsqrt(square * (1.0 / gain.shape[0]) + EPS)
    kv, query, low = combine(kept, received, inverse, up)
    inverse_row = shift(tie(inverse.reshape(-1, 128), kv), "zl", 1)
    prev = lax.ppermute(kv[half:], "seq", [(i, i + 1) for i in range(3)])

    docs = doc_ids[0]
    begin = seq * tokens
    own_docs = lax.dynamic_slice_in_dim(docs, begin, tokens)
    prev_docs = lax.dynamic_slice_in_dim(docs, jnp.maximum(begin - half, 0), half)
    prev_docs = jnp.where(seq > 0, prev_docs, -1)
    ext_docs = jnp.concatenate([prev_docs, own_docs])
    masks = (own_docs[None, :], ext_docs[:, None])
    out_even, dq_even, dkv_even = attend(0, query, kv, kv[half:], d_out[0], *masks)
    dq_even_other = shift(dq_even, "zl", 1)
    out_odd, dq_odd, dkv_odd, dprev = attend(1, query, kv, prev, d_out[0], *masks)
    dq_odd_other = shift(dq_odd, "zl", 1)
    returned = lax.ppermute(dprev, "seq", [(i + 1, i) for i in range(3)])
    dq, dkv, ranks_own = unite(
        False, dq_even, dq_odd, dkv_even, dkv_odd, returned, query_up_weight, value_up_weight
    )
    dkv_other = shift(dkv, "zl", 1)
    dq_other, dkv_other, ranks_other = unite(
        True,
        dq_even_other,
        dq_odd_other,
        dkv_other,
        dkv_other,
        returned,
        query_up_weight,
        value_up_weight,
    )
    output = []
    for h in range(out_even.shape[1] // HD):
        at = slice(h * HD, (h + 1) * HD)
        output += [out_even[:, at], out_odd[:, at]]
    output = jnp.concatenate(output, axis=1)
    inverses = (inverse, tie(inverse_row, dq_other).reshape(-1, 1))
    rank_rows = sum_heads(jnp.concatenate([ranks_own, ranks_other], axis=0))
    rank_rows = (rank_rows * jnp.concatenate(inverses, axis=0)).astype(BF)

    up_rows = ADAPTER_SCALE * jnp.concatenate(
        [dot_rows(low[:, rank:], dkv[:, HD:]), dot_rows(low[:, :rank], dq)], axis=1
    )
    up_rows = tie(up_rows, dkv)
    turns = iter((("dp", 1), ("dp", 2), ("seq", 1), ("seq", 2), ("dp", 4)))

    def add_next(rows, *others):
        axis, step = next(turns)
        moved = shift(rows.astype(BF), axis, step)
        if others:
            moved = tie(moved, *others)
        return rows + moved.astype(F32)

    blocks = first + second
    gains = gain_part(number_at, raw_own, dkv, dq, ranks_own, inverses[0], a_rows, blocks)
    up_rows = add_next(up_rows, gains)
    gains_other = gain_part(
        number_at, raw_other, dkv_other, dq_other, ranks_other, inverses[1], a_rows, blocks
    )
    up_rows = add_next(up_rows, gains_other)
    gains = gains + gains_other

    def row_products(raw, rows):
        width = raw.shape[1]
        mine = lax.dynamic_slice_in_dim(raw, high * (width // 2), width // 2, 1)
        return dot_rows(mine, rows)

    grad_a = row_products(raw_own, rank_rows[:tokens]) + row_products(
        raw_other, rank_rows[tokens:]
    )
    grad_a = grad_a.reshape(16, 2, 64, 2 * rank)
    grad_a = lax.dynamic_index_in_dim(grad_a, mp % 2, 1, keepdims=False)
    grad_a = grad_a.reshape(4, 256, 2 * rank)
    whole, grad_a = reduce_stage(grad_a, gains, lambda v, step: shift_plane(v, 0, step))
    up_rows = add_next(up_rows, whole)
    grad_a = grad_a.reshape(4, 64, 2 * rank)
    whole, grad_a = reduce_stage(grad_a, whole, lambda v, step: shift_plane(v, 1, step))
    up_rows = add_next(up_rows, whole)
    gains = whole.astype(BF)
    gain_sum = jnp.zeros((16, 128), F32)
    for flip_core in range(2):
        send = lax.dynamic_slice_in_dim(gains, (mp % 2 ^ flip_core) * 16, 16, 0)
        for flip_z in range(2):
            gain_sum = gain_sum + turn(send, flip_z, flip_core).astype(F32)
    up_rows = add_next(up_rows)
    gain_sum = gain_sum.reshape(-1)
    gain_own = lax.dynamic_slice_in_dim(gain, mp * gain_sum.shape[0], gain_sum.shape[0])
    return (
        output[None],
        grad_a[:, :rank],
        up_rows[:, HD:],
        grad_a[:, rank:],
        up_rows[:, :HD],
        gain_sum / gain_own,
    )


def solution(mesh):
    return jax.shard_map(
        per_device,
        mesh=mesh,
        in_specs=(
            P("dp", "seq", "mp"),
            P(),
            P(("dp", "seq"), "mp"),
            P(("dp", "seq"), "mp"),
            P(("dp", "seq"), "mp"),
            P(),
            P(None, "mp"),
            P(),
            P(None, "mp"),
            P("dp", None),
            P("dp", "seq", "mp"),
        ),
        out_specs=(
            P("dp", "seq", "mp"),
            P(("dp", "seq", "mp"), None),
            P(None, "mp"),
            P(("dp", "seq", "mp"), None),
            P(None, "mp"),
            P("mp"),
        ),
        check_vma=False,
    )
```

```python
import functools

import jax
import jax.numpy as jnp
from jax import lax
from jax.experimental import pallas as pl
from jax.experimental.pallas import tpu as pltpu
from jax.sharding import PartitionSpec as P

HD = 128
EPS = 1e-05
ADAPTER_SCALE = 0.25
NEG_FILL = -1e30
BF = jnp.bfloat16
F32 = jnp.float32
VMEM_LIMIT = 56 * 1024 * 1024
VMEM_SMALL = 24 * 1024 * 1024
REL = (0, -1, 1, 2)
ROWS = 512


def shift(value, axis, step):
    if axis == "x":
        route = [(z * 4 + i, z * 4 + (i + step) % 4) for z in range(2) for i in range(4)]
        return lax.ppermute(value, "dp", route)
    if axis == "dp":
        return lax.ppermute(value, "dp", [(i, i ^ step) for i in range(8)])
    if axis == "zl":
        return lax.ppermute(value, "dp", [(i, (i + 4) % 8) for i in range(8)])
    if axis == "seq":
        return lax.ppermute(value, "seq", [(i, i ^ step) for i in range(4)])
    if axis == "y":
        return lax.ppermute(value, "seq", [(i, (i + step) % 4) for i in range(4)])
    return lax.ppermute(value, "mp", [(i, i ^ step) for i in range(4)])


def shift_plane(value, stage, step):
    route = []
    for z in range(2):
        for x in range(4):
            for y in range(4):
                for m in range(4):
                    to_x, to_y = x, y
                    if (m < 2) == (stage == 0):
                        to_y = (y + step) % 4
                    else:
                        to_x = (x + step) % 4
                    route.append(
                        (((z * 4 + x) * 4 + y) * 4 + m, ((z * 4 + to_x) * 4 + to_y) * 4 + m)
                    )
    return lax.ppermute(value, ("dp", "seq", "mp"), route)


def params(limit=VMEM_SMALL):
    return pltpu.CompilerParams(vmem_limit_bytes=limit)


def any_specs(count):
    return [pl.BlockSpec(memory_space=pl.ANY)] * count


def vmem_specs(count):
    return [pl.BlockSpec(memory_space=pltpu.VMEM)] * count


def assemble_kernel(*refs):
    pieces, outs = refs[:8], refs[-2:]
    rows = pieces[0].shape[0]
    for k, piece in enumerate(pieces):
        outs[k // 4][k % 4 * rows : (k % 4 + 1) * rows, :] = piece[...]


def assemble(pieces, *others):
    rows, columns = pieces[0].shape
    return pl.pallas_call(
        assemble_kernel,
        in_specs=vmem_specs(8) + any_specs(len(others)),
        out_specs=vmem_specs(2),
        out_shape=[jax.ShapeDtypeStruct((4 * rows, columns), BF)] * 2,
        compiler_params=params(),
        cost_estimate=pl.CostEstimate(
            flops=0, bytes_accessed=32 * rows * columns, transcendentals=0
        ),
        name="assemble",
    )(*pieces, *others)


def first_rings(shard):
    half = shard.shape[0] // 2
    pieces = []
    for part, axis in ((shard[:half], "x"), (shard[half:], "y")):
        pieces += [part] + [shift(part, axis, -step) for step in REL[1:]]
    return pieces


def second_rings(inners):
    blocks = []
    for inner, axis in zip(inners, ("y", "x")):
        before, after = shift(inner, axis, 1), shift(inner, axis, -1)
        blocks.append(
            [inner, before, after]
            + [shift(before[: ROWS // 2], axis, 1), shift(after[ROWS // 2 :], axis, -1)]
        )
    return blocks


def tie_kernel(*refs):
    del refs


def tie(value, *others):
    return pl.pallas_call(
        tie_kernel,
        in_specs=any_specs(1 + len(others)),
        out_specs=any_specs(1)[0],
        out_shape=jax.ShapeDtypeStruct(value.shape, value.dtype),
        input_output_aliases={0: 0},
        compiler_params=params(VMEM_LIMIT),
        name="tie",
    )(value, *others)


def corners(values):
    return jnp.concatenate([value[:16, :128] for value in values], axis=0)


def turn(value, flip_z, flip_core):
    route = []
    for zl in range(2):
        for x in range(4):
            for zh in range(2):
                for c in range(2):
                    target = ((zh ^ flip_z) * 4 + x) * 4 + zl * 2 + (c ^ flip_core)
                    route.append(((zl * 4 + x) * 4 + zh * 2 + c, target))
    return lax.ppermute(value, ("dp", "mp"), route)


def block_places(x, y, core):
    at = jnp.arange(32, dtype=jnp.int32)
    number = ((at // 16) ^ core) * 16 + at % 16
    order, shard = number % 2, number // 2
    inverse = jnp.array([0, 2, 3, 1], jnp.int32)
    by_x = inverse[(shard // 4 - x) % 4]
    by_y = inverse[(shard % 4 - y) % 4]
    outer = jnp.where(order == 0, by_y, by_x)
    inner = jnp.where(order == 0, by_x, by_y)
    place = order * 16 + outer * 4 + inner
    number_at = jnp.sum(jnp.where(place[None, :] == at[:, None], number[None, :], 0), axis=1)
    return number, place, number_at.astype(jnp.int32)


def fetch(sources, held, sems):
    copies = []
    begin = 0
    for k, source in enumerate(sources):
        rows = source.shape[0]
        copies.append(
            pltpu.make_async_copy(source, held.at[pl.ds(begin, rows)], sems.at[k])
        )
        begin += rows
    for copy in copies:
        copy.start()
    return copies


TILE = 256


def project_kernel(own, number, place, where, p0, p1, swapped, gain, a_both, other, *refs):
    del other
    if own:
        sources, (raw, out, taken, held, square, sems, take_sems) = refs[:-7], refs[-7:]
        a_rows = a_both
    else:
        sources, (raw, out, a_rows, taken, held, square, sems, take_sems) = refs[:-8], refs[-8:]

    tokens = p0.shape[0]

    def take(parts):
        return [pltpu.make_async_copy(p, taken.at[k], take_sems.at[k]) for k, p in enumerate(parts)]

    @pl.when(where[0] == (0 if own else 1))
    def _():
        for copy in take((p0, swapped.at[pl.ds(0, tokens)])):
            copy.start()

    @pl.when(where[0] != (0 if own else 1))
    def _():
        for copy in take((p1, swapped.at[pl.ds(tokens, tokens)])):
            copy.start()

    copies = fetch(sources, held, sems)
    for copy in take((p0, swapped.at[pl.ds(0, tokens)])):
        copy.wait()
    per = taken.shape[2] // 128
    square[...] = jnp.zeros_like(square)
    for r in range(2):

        @pl.loop(0, per)
        def _(i):
            block = where[1] + number[r * per + i]
            target = pl.ds(pl.multiple_of(place[r * per + i] * 128, 128), 128)
            value = taken[r, :, pl.ds(pl.multiple_of(i * 128, 128), 128)].astype(F32)
            square[...] += value * value
            raw[:, target] = (value * gain[pl.ds(block, 1), :]).astype(BF)
            if not own:
                source = pl.ds(pl.multiple_of(block * 128, 128), 128)
                a_rows[target, :] = a_both[source, :]

    columns = held.shape[1]
    low = jnp.dot(raw[...], a_rows[...], preferred_element_type=F32)
    out[:, columns : columns + 128] = low.astype(out.dtype)
    total = jnp.broadcast_to(jnp.sum(square[...], axis=1, keepdims=True), square.shape)
    if not own:
        lead = total.astype(BF)
        lane = lax.broadcasted_iota(jnp.int32, square.shape, 1)
        total = jnp.where(lane == 0, lead.astype(F32), total - lead.astype(F32))
    out[:, columns + 128 :] = total.astype(out.dtype)
    for copy in copies:
        copy.wait()

    @pl.loop(0, columns // TILE)
    def _(n):
        at = pl.ds(pl.multiple_of(n * TILE, TILE), TILE)
        total = jnp.dot(raw[...], held[:, at], preferred_element_type=F32)
        out[:, at] = total.astype(out.dtype)


def project(own, number, place, where, parts, gain, a_both, other, blocks):
    tokens, quarter = parts[0].shape
    columns = blocks[0].shape[1]
    count = len(blocks)
    outs = [
        jax.ShapeDtypeStruct((tokens, 2 * quarter), BF),
        jax.ShapeDtypeStruct((tokens, columns + 256), F32 if own else BF),
    ]
    if not own:
        outs.append(jax.ShapeDtypeStruct((2 * quarter, 128), BF))
    return pl.pallas_call(
        functools.partial(project_kernel, own),
        in_specs=[pl.BlockSpec(memory_space=pltpu.SMEM)] * 3
        + any_specs(3)
        + vmem_specs(2)
        + any_specs(1 + count),
        out_specs=vmem_specs(len(outs)),
        out_shape=outs,
        scratch_shapes=[
            pltpu.VMEM((2, tokens, quarter), BF),
            pltpu.VMEM((2 * quarter, columns), BF),
            pltpu.VMEM((tokens, 128), F32),
            pltpu.SemaphoreType.DMA((count,)),
            pltpu.SemaphoreType.DMA((2,)),
        ],
        compiler_params=params(VMEM_LIMIT),
        cost_estimate=pl.CostEstimate(
            flops=4 * tokens * quarter * columns,
            bytes_accessed=4 * quarter * (2 * tokens + columns),
            transcendentals=0,
        ),
        name="project",
    )(number, place, where, *parts, gain.reshape(-1, 128), a_both, other, *blocks)


def combine_kernel(features, kept, received, up, kv, query, low, inverse):
    columns = kv.shape[1] + query.shape[1]
    last = columns + 128
    square = kept[:, last : last + 1] + received[:, last : last + 1].astype(F32)
    square += received[:, last + 1 : last + 2].astype(F32)
    inv = lax.rsqrt(square * (1.0 / features) + EPS)
    inverse[...] = inv
    low_sum = kept[:, columns:last] + received[:, columns:last].astype(F32)
    low_sum = (low_sum * inv).astype(BF)
    low[...] = low_sum
    total = (kept[:, :columns] + received[:, :columns].astype(F32)) * inv
    total += ADAPTER_SCALE * jnp.dot(low_sum, up[...], preferred_element_type=F32)
    kv[...] = total[:, : 2 * HD].astype(BF)
    query[...] = total[:, 2 * HD :].astype(BF)


def combine(features, kept, received, up):
    tokens = kept.shape[0]
    columns = up.shape[1]
    return pl.pallas_call(
        functools.partial(combine_kernel, features),
        in_specs=vmem_specs(3),
        out_specs=vmem_specs(4),
        out_shape=[
            jax.ShapeDtypeStruct((tokens, 2 * HD), BF),
            jax.ShapeDtypeStruct((tokens, columns - 2 * HD), BF),
            jax.ShapeDtypeStruct((tokens, 128), BF),
            jax.ShapeDtypeStruct((tokens, 1), F32),
        ],
        compiler_params=params(),
        cost_estimate=pl.CostEstimate(
            flops=2 * tokens * 128 * columns,
            bytes_accessed=8 * tokens * columns,
            transcendentals=0,
        ),
        name="combine",
    )(kept, received, up)


def gain_kernel(count, numbers, dkv, dq, ranks, inverse, a_rows, raw, *refs):
    sources, (out, held, rows, sems, row_sems) = refs[:count], refs[count:]
    spans = []
    for source in sources:
        begin = spans[-1][1] if spans else 0
        spans.append((begin, begin + source.shape[0]))
    row_copies = [
        pltpu.make_async_copy(
            raw.at[:, pl.ds(begin, end - begin)], rows.at[:, pl.ds(begin, end - begin)], row_sems.at[k]
        )
        for k, (begin, end) in enumerate(spans)
    ]
    copies = fetch(sources, held, sems)
    for copy in row_copies:
        copy.start()
    nt = (((1,), (1,)), ((), ()))
    for k, (begin, end) in enumerate(spans):
        at = slice(begin, end)
        copies[k].wait()
        row_copies[k].wait()
        term = lax.dot_general(dkv[...], held[at, : 2 * HD], nt, preferred_element_type=F32)
        term += lax.dot_general(dq[...], held[at, 2 * HD :], nt, preferred_element_type=F32)
        term += lax.dot_general(ranks[...], a_rows[at, :], nt, preferred_element_type=F32)
        sums = jnp.sum(term * inverse[...] * rows[:, at].astype(F32), axis=0, keepdims=True)
        for s in range((end - begin) // 128):
            out[pl.ds(numbers[begin // 128 + s], 1), :] = sums[:, s * 128 : (s + 1) * 128]


def gain_part(numbers, raw, dkv, dq, ranks, inverse, a_rows, blocks):
    tokens, width = raw.shape
    columns = blocks[0].shape[1]
    count = len(blocks)
    return pl.pallas_call(
        functools.partial(gain_kernel, count),
        in_specs=[pl.BlockSpec(memory_space=pltpu.SMEM)] + vmem_specs(5) + any_specs(1 + count),
        out_specs=vmem_specs(1)[0],
        out_shape=jax.ShapeDtypeStruct((width // 128, 128), F32),
        scratch_shapes=[
            pltpu.VMEM((width, columns), BF),
            pltpu.VMEM((tokens, width), BF),
            pltpu.SemaphoreType.DMA((count,)),
            pltpu.SemaphoreType.DMA((count,)),
        ],
        compiler_params=params(VMEM_LIMIT),
        cost_estimate=pl.CostEstimate(
            flops=2 * tokens * width * columns,
            bytes_accessed=2 * width * (tokens + columns),
            transcendentals=0,
        ),
        name="gain_part",
    )(numbers, dkv, dq, ranks, inverse, a_rows, raw, *blocks)


def unite_kernel(partner, dq0, dq1, dkv0, dkv1, returned, up_query, up_value, dq, dkv, ranks):
    rank = up_query.shape[0]
    half = returned.shape[0]
    for h in range(dq.shape[1] // HD):
        source = (dq0, dq1)[h % 2]
        dq[:, h * HD : (h + 1) * HD] = source[:, h // 2 * HD : (h // 2 + 1) * HD]
    if partner:
        dkv[...] = dkv0[...]
    else:
        dkv[:half, :] = (dkv0[:half, :] + dkv1[:half, :]).astype(BF)
        dkv[half:, :] = (dkv0[half:, :] + dkv1[half:, :] + returned[...].astype(F32)).astype(BF)
    nt = (((1,), (1,)), ((), ()))
    of_query = lax.dot_general(dq[...], up_query[...], nt, preferred_element_type=F32)
    of_value = lax.dot_general(dkv[:, HD:], up_value[...], nt, preferred_element_type=F32)
    ranks[:, :rank] = (ADAPTER_SCALE * of_query).astype(BF)
    ranks[:, rank:] = (ADAPTER_SCALE * of_value).astype(BF)


def unite(partner, dq0, dq1, dkv0, dkv1, returned, up_query, up_value):
    tokens, columns = dq0.shape
    return pl.pallas_call(
        functools.partial(unite_kernel, partner),
        in_specs=vmem_specs(7),
        out_specs=vmem_specs(3),
        out_shape=[
            jax.ShapeDtypeStruct((tokens, 2 * columns), BF),
            jax.ShapeDtypeStruct((tokens, 2 * HD), BF),
            jax.ShapeDtypeStruct((tokens, 128), BF),
        ],
        compiler_params=params(),
        cost_estimate=pl.CostEstimate(
            flops=4 * tokens * columns * 64, bytes_accessed=8 * tokens * columns, transcendentals=0
        ),
        name="unite",
    )(dq0, dq1, dkv0, dkv1, returned, up_query, up_value)


def attend_kernel(odd, query, kv, prev, grads, docs_row, docs_col, *refs):
    if odd:
        out, dq, dkv, dprev, dk, dv = refs
    else:
        out, dq, dkv, dk, dv = refs
    tokens = kv.shape[0]
    half = tokens // 2
    scale = HD ** (-0.5)
    if odd:
        keys = jnp.concatenate([prev[:, :HD], kv[:, :HD]], axis=0)
        values = jnp.concatenate([prev[:, HD:], kv[:, HD:]], axis=0)
        spans = ((0, tokens), (tokens, tokens + half))
        doc_keys = docs_col[...]
        before = half
    else:
        keys, values = kv[:, :HD], kv[:, HD:]
        spans = ((0, half), (0, tokens))
        doc_keys = docs_col[half:, :]
        before = 0
    dk[...] = jnp.zeros_like(dk)
    dv[...] = jnp.zeros_like(dv)
    for part, (low, high) in enumerate(spans):
        rows = slice(part * half, (part + 1) * half)
        key_at = lax.broadcasted_iota(jnp.int32, (high - low, half), 0) + (low - before)
        query_at = lax.broadcasted_iota(jnp.int32, (high - low, half), 1) + part * half
        allowed = (doc_keys[low:high, :] == docs_row[:, rows]) & (key_at <= query_at)
        key, value = keys[low:high], values[low:high]
        for h in range(dq.shape[1] // HD):
            source = slice((2 * h + odd) * HD, (2 * h + odd + 1) * HD)
            target = slice(h * HD, (h + 1) * HD)
            row_query, cot = query[rows, source], grads[rows, source]
            scores = (
                lax.dot_general(
                    key, row_query, (((1,), (1,)), ((), ())), preferred_element_type=F32
                )
                * scale
            )
            scores = jnp.where(allowed, scores, NEG_FILL)
            expo = jnp.exp(scores - jnp.max(scores, axis=0, keepdims=True))
            probs = expo * (1.0 / jnp.sum(expo, axis=0, keepdims=True))
            probs_low = probs.astype(BF)
            output = lax.dot_general(
                value, probs_low, (((0,), (0,)), ((), ())), preferred_element_type=F32
            )
            out[rows, target] = output.T.astype(BF)
            dprob = lax.dot_general(
                value, cot, (((1,), (1,)), ((), ())), preferred_element_type=F32
            )
            delta = jnp.sum(probs_low.astype(F32) * dprob, axis=0, keepdims=True)
            dscore = (probs * (dprob - delta)).astype(BF)
            dquery = lax.dot_general(
                key, dscore, (((0,), (0,)), ((), ())), preferred_element_type=F32
            )
            dq[rows, target] = (dquery * scale).T.astype(BF)
            dk[low:high, :] += jnp.dot(dscore, row_query, preferred_element_type=F32)
            dv[low:high, :] += jnp.dot(probs_low, cot, preferred_element_type=F32)
    dkv[:, :HD] = dk[before:, :] * scale
    dkv[:, HD:] = dv[before:, :]
    if odd:
        dprev[:, :HD] = (dk[:before, :] * scale).astype(BF)
        dprev[:, HD:] = dv[:before, :].astype(BF)


def attend(odd, query, kv, prev, grads, docs_row, docs_col):
    tokens, columns = grads.shape
    half = tokens // 2
    span = tokens + half if odd else tokens
    outs = [
        jax.ShapeDtypeStruct((tokens, columns // 2), BF),
        jax.ShapeDtypeStruct((tokens, columns // 2), BF),
        jax.ShapeDtypeStruct((tokens, 2 * HD), F32),
    ]
    if odd:
        outs.append(jax.ShapeDtypeStruct((half, 2 * HD), BF))
    return pl.pallas_call(
        functools.partial(attend_kernel, odd),
        in_specs=vmem_specs(6),
        out_specs=vmem_specs(len(outs)),
        out_shape=outs,
        scratch_shapes=[pltpu.VMEM((span, HD), F32)] * 2,
        compiler_params=params(),
        cost_estimate=pl.CostEstimate(
            flops=5 * tokens * tokens * columns,
            bytes_accessed=4 * tokens * columns,
            transcendentals=tokens * tokens * columns // (2 * HD),
        ),
        name="attend",
    )(query, kv, prev, grads, docs_row, docs_col)


def dot_rows(left, right):
    return lax.dot_general(left, right, (((0,), (0,)), ((), ())), preferred_element_type=F32)


def dot_cols(left, right):
    return lax.dot_general(left, right, (((1,), (1,)), ((), ())), preferred_element_type=F32)


def sum_heads(value):
    total = value.astype(F32)
    for step in (1, 2, 3):
        total = total + shift(value, "mp", step).astype(F32)
    return total


def reduce_stage(chunks, whole, move):
    count = whole.shape[0]
    total = jnp.concatenate([whole, chunks[0]], axis=0)
    low = whole.astype(BF)
    for i in (1, 2, 3):
        packed = jnp.concatenate([low, chunks[i].astype(BF)], axis=0)
        total = total + move(packed, REL[i]).astype(F32)
    return total[:count], total[count:]


def per_device(
    hidden,
    gain,
    query_frozen_weight,
    w_key,
    value_frozen_weight,
    a_query,
    query_up_weight,
    a_value,
    value_up_weight,
    doc_ids,
    d_out,
):
    tokens = hidden.shape[1]
    half = tokens // 2
    dp, seq, mp = lax.axis_index("dp"), lax.axis_index("seq"), lax.axis_index("mp")
    pair, high = dp // 4, mp // 2
    own = hidden[0]
    turned = turn(own, 0, 0)
    weights = jnp.concatenate([w_key, value_frozen_weight, query_frozen_weight], axis=1)
    pieces = first_rings(weights)
    turned = tie(turned, corners(pieces[1:4] + pieces[5:]))
    turned_high = shift(turned, "mp", 2)
    a_both = jnp.concatenate([a_query, a_value], axis=1)
    first, second = second_rings(assemble(pieces, a_both))
    turned_high = tie(turned_high, corners(first[1:3] + second[1:3]))
    swapped = shift(jnp.concatenate([turned, turned_high], axis=0), "mp", 1)
    hidden_parts = [turned, turned_high, swapped]
    number, place, number_at = block_places(dp % 4, seq, mp % 2)
    where = jnp.stack([jnp.where(pair == high, 0, 1), pair * 32]).astype(jnp.int32)
    raw_other, sent, a_rows = project(
        False, number, place, where, hidden_parts, gain, a_both, a_both, first + second
    )
    received = shift(sent, "zl", 1)
    raw_own, kept = project(
        True, number, place, where, hidden_parts, gain, a_rows, sent, first + second
    )
    rank = query_up_weight.shape[0]
    up = jnp.concatenate(
        [
            jnp.concatenate([jnp.zeros((rank, 2 * HD), BF), query_up_weight], axis=1),
            jnp.concatenate(
                [jnp.zeros((rank, HD), BF), value_up_weight, jnp.zeros_like(query_up_weight)], axis=1
            ),
        ],
        axis=0,
    )
    kv, query, low, inverse = combine(gain.shape[0], kept, received, up)
    inverse_row = shift(tie(inverse.reshape(-1, 128), kv), "zl", 1)
    prev = lax.ppermute(kv[half:], "seq", [(i, i + 1) for i in range(3)])

    docs = doc_ids[0]
    begin = seq * tokens
    own_docs = lax.dynamic_slice_in_dim(docs, begin, tokens)
    prev_docs = lax.dynamic_slice_in_dim(docs, jnp.maximum(begin - half, 0), half)
    prev_docs = jnp.where(seq > 0, prev_docs, -1)
    ext_docs = jnp.concatenate([prev_docs, own_docs])
    masks = (own_docs[None, :], ext_docs[:, None])
    out_even, dq_even, dkv_even = attend(0, query, kv, kv[half:], d_out[0], *masks)
    dq_even_other = shift(dq_even, "zl", 1)
    out_odd, dq_odd, dkv_odd, dprev = attend(1, query, kv, prev, d_out[0], *masks)
    dq_odd_other = shift(dq_odd, "zl", 1)
    returned = lax.ppermute(dprev, "seq", [(i + 1, i) for i in range(3)])
    dq, dkv, ranks_own = unite(
        False, dq_even, dq_odd, dkv_even, dkv_odd, returned, query_up_weight, value_up_weight
    )
    dkv_other = shift(dkv, "zl", 1)
    dq_other, dkv_other, ranks_other = unite(
        True,
        dq_even_other,
        dq_odd_other,
        dkv_other,
        dkv_other,
        returned,
        query_up_weight,
        value_up_weight,
    )
    output = []
    for h in range(out_even.shape[1] // HD):
        at = slice(h * HD, (h + 1) * HD)
        output += [out_even[:, at], out_odd[:, at]]
    output = jnp.concatenate(output, axis=1)
    inverses = (inverse, tie(inverse_row, dq_other).reshape(-1, 1))
    rank_rows = sum_heads(jnp.concatenate([ranks_own, ranks_other], axis=0))
    rank_rows = (rank_rows * jnp.concatenate(inverses, axis=0)).astype(BF)

    up_rows = ADAPTER_SCALE * jnp.concatenate(
        [dot_rows(low[:, rank:], dkv[:, HD:]), dot_rows(low[:, :rank], dq)], axis=1
    )
    up_rows = tie(up_rows, dkv)
    turns = iter((("dp", 1), ("dp", 2), ("seq", 1), ("seq", 2), ("dp", 4)))

    def add_next(rows, *others):
        axis, step = next(turns)
        moved = shift(rows.astype(BF), axis, step)
        if others:
            moved = tie(moved, *others)
        return rows + moved.astype(F32)

    blocks = first + second
    gains = gain_part(number_at, raw_own, dkv, dq, ranks_own, inverses[0], a_rows, blocks)
    up_rows = add_next(up_rows, gains)
    gains_other = gain_part(
        number_at, raw_other, dkv_other, dq_other, ranks_other, inverses[1], a_rows, blocks
    )
    up_rows = add_next(up_rows, gains_other)
    gains = gains + gains_other

    def row_products(raw, rows):
        width = raw.shape[1]
        mine = lax.dynamic_slice_in_dim(raw, high * (width // 2), width // 2, 1)
        return dot_rows(mine, rows)

    grad_a = row_products(raw_own, rank_rows[:tokens]) + row_products(
        raw_other, rank_rows[tokens:]
    )
    grad_a = grad_a.reshape(16, 2, 64, 2 * rank)
    grad_a = lax.dynamic_index_in_dim(grad_a, mp % 2, 1, keepdims=False)
    grad_a = grad_a.reshape(4, 256, 2 * rank)
    whole, grad_a = reduce_stage(grad_a, gains, lambda v, step: shift_plane(v, 0, step))
    up_rows = add_next(up_rows, whole)
    grad_a = grad_a.reshape(4, 64, 2 * rank)
    whole, grad_a = reduce_stage(grad_a, whole, lambda v, step: shift_plane(v, 1, step))
    up_rows = add_next(up_rows, whole)
    gains = whole.astype(BF)
    gain_sum = jnp.zeros((16, 128), F32)
    for flip_core in range(2):
        send = lax.dynamic_slice_in_dim(gains, (mp % 2 ^ flip_core) * 16, 16, 0)
        for flip_z in range(2):
            gain_sum = gain_sum + turn(send, flip_z, flip_core).astype(F32)
    up_rows = add_next(up_rows)
    gain_sum = gain_sum.reshape(-1)
    gain_own = lax.dynamic_slice_in_dim(gain, mp * gain_sum.shape[0], gain_sum.shape[0])
    return (
        output[None],
        grad_a[:, :rank],
        up_rows[:, HD:],
        grad_a[:, rank:],
        up_rows[:, :HD],
        gain_sum / gain_own,
    )


def solution(mesh):
    return jax.shard_map(
        per_device,
        mesh=mesh,
        in_specs=(
            P("dp", "seq", "mp"),
            P(),
            P(("dp", "seq"), "mp"),
            P(("dp", "seq"), "mp"),
            P(("dp", "seq"), "mp"),
            P(),
            P(None, "mp"),
            P(),
            P(None, "mp"),
            P("dp", None),
            P("dp", "seq", "mp"),
        ),
        out_specs=(
            P("dp", "seq", "mp"),
            P(("dp", "seq", "mp"), None),
            P(None, "mp"),
            P(("dp", "seq", "mp"), None),
            P(None, "mp"),
            P("mp"),
        ),
        check_vma=False,
    )
```

```python
import functools

import jax
import jax.numpy as jnp
from jax import lax
from jax.experimental import pallas as pl
from jax.experimental.pallas import tpu as pltpu
from jax.sharding import PartitionSpec as P

HD = 128
EPS = 1e-05
ADAPTER_SCALE = 0.25
NEG_FILL = -1e30
BF = jnp.bfloat16
F32 = jnp.float32
VMEM_LIMIT = 56 * 1024 * 1024
VMEM_SMALL = 24 * 1024 * 1024
REL = (0, -1, 1, 2)
ROWS = 512


def shift(value, axis, step):
    if axis == "x":
        route = [(z * 4 + i, z * 4 + (i + step) % 4) for z in range(2) for i in range(4)]
        return lax.ppermute(value, "dp", route)
    if axis == "dp":
        return lax.ppermute(value, "dp", [(i, i ^ step) for i in range(8)])
    if axis == "zl":
        return lax.ppermute(value, "dp", [(i, (i + 4) % 8) for i in range(8)])
    if axis == "seq":
        return lax.ppermute(value, "seq", [(i, i ^ step) for i in range(4)])
    if axis == "y":
        return lax.ppermute(value, "seq", [(i, (i + step) % 4) for i in range(4)])
    return lax.ppermute(value, "mp", [(i, i ^ step) for i in range(4)])


def shift_plane(value, stage, step):
    route = []
    for z in range(2):
        for x in range(4):
            for y in range(4):
                for m in range(4):
                    to_x, to_y = x, y
                    if (m < 2) == (stage == 0):
                        to_y = (y + step) % 4
                    else:
                        to_x = (x + step) % 4
                    route.append(
                        (((z * 4 + x) * 4 + y) * 4 + m, ((z * 4 + to_x) * 4 + to_y) * 4 + m)
                    )
    return lax.ppermute(value, ("dp", "seq", "mp"), route)


def params(limit=VMEM_SMALL):
    return pltpu.CompilerParams(vmem_limit_bytes=limit)


def any_specs(count):
    return [pl.BlockSpec(memory_space=pl.ANY)] * count


def vmem_specs(count):
    return [pl.BlockSpec(memory_space=pltpu.VMEM)] * count


def assemble_kernel(*refs):
    pieces, outs = refs[:8], refs[-2:]
    rows = pieces[0].shape[0]
    for k, piece in enumerate(pieces):
        outs[k // 4][k % 4 * rows : (k % 4 + 1) * rows, :] = piece[...]


def assemble(pieces, *others):
    rows, columns = pieces[0].shape
    return pl.pallas_call(
        assemble_kernel,
        in_specs=vmem_specs(8) + any_specs(len(others)),
        out_specs=vmem_specs(2),
        out_shape=[jax.ShapeDtypeStruct((4 * rows, columns), BF)] * 2,
        compiler_params=params(),
        cost_estimate=pl.CostEstimate(
            flops=0, bytes_accessed=32 * rows * columns, transcendentals=0
        ),
        name="assemble",
    )(*pieces, *others)


def first_rings(shard):
    half = shard.shape[0] // 2
    pieces = []
    for part, axis in ((shard[:half], "x"), (shard[half:], "y")):
        pieces += [part] + [shift(part, axis, -step) for step in REL[1:]]
    return pieces


def second_rings(inners):
    blocks = []
    for inner, axis in zip(inners, ("y", "x")):
        before, after = shift(inner, axis, 1), shift(inner, axis, -1)
        blocks.append(
            [inner, before, after]
            + [shift(before[: ROWS // 2], axis, 1), shift(after[ROWS // 2 :], axis, -1)]
        )
    return blocks


def tie_kernel(*refs):
    del refs


def tie(value, *others):
    return pl.pallas_call(
        tie_kernel,
        in_specs=any_specs(1 + len(others)),
        out_specs=any_specs(1)[0],
        out_shape=jax.ShapeDtypeStruct(value.shape, value.dtype),
        input_output_aliases={0: 0},
        compiler_params=params(VMEM_LIMIT),
        name="tie",
    )(value, *others)


def corners(values):
    return jnp.concatenate([value[:16, :128] for value in values], axis=0)


def turn(value, flip_z, flip_core):
    route = []
    for zl in range(2):
        for x in range(4):
            for zh in range(2):
                for c in range(2):
                    target = ((zh ^ flip_z) * 4 + x) * 4 + zl * 2 + (c ^ flip_core)
                    route.append(((zl * 4 + x) * 4 + zh * 2 + c, target))
    return lax.ppermute(value, ("dp", "mp"), route)


def block_places(x, y, core):
    at = jnp.arange(32, dtype=jnp.int32)
    number = ((at // 16) ^ core) * 16 + at % 16
    order, shard = number % 2, number // 2
    inverse = jnp.array([0, 2, 3, 1], jnp.int32)
    by_x = inverse[(shard // 4 - x) % 4]
    by_y = inverse[(shard % 4 - y) % 4]
    outer = jnp.where(order == 0, by_y, by_x)
    inner = jnp.where(order == 0, by_x, by_y)
    place = order * 16 + outer * 4 + inner
    number_at = jnp.sum(jnp.where(place[None, :] == at[:, None], number[None, :], 0), axis=1)
    return number, place, number_at.astype(jnp.int32)


def fetch(sources, held, sems):
    copies = []
    begin = 0
    for k, source in enumerate(sources):
        rows = source.shape[0]
        copies.append(
            pltpu.make_async_copy(source, held.at[pl.ds(begin, rows)], sems.at[k])
        )
        begin += rows
    for copy in copies:
        copy.start()
    return copies


TILE = 256


def project_kernel(own, number, place, where, p0, p1, swapped, gain, a_both, other, *refs):
    del other
    if own:
        sources, (raw, out, taken, held, square, sems, take_sems) = refs[:-7], refs[-7:]
        a_rows = a_both
    else:
        sources, (raw, out, a_rows, taken, held, square, sems, take_sems) = refs[:-8], refs[-8:]

    tokens = p0.shape[0]

    def take(parts):
        return [pltpu.make_async_copy(p, taken.at[k], take_sems.at[k]) for k, p in enumerate(parts)]

    @pl.when(where[0] == (0 if own else 1))
    def _():
        for copy in take((p0, swapped.at[pl.ds(0, tokens)])):
            copy.start()

    @pl.when(where[0] != (0 if own else 1))
    def _():
        for copy in take((p1, swapped.at[pl.ds(tokens, tokens)])):
            copy.start()

    copies = fetch([source.at[:, pl.ds(0, held.shape[1])] for source in sources], held, sems)
    for copy in take((p0, swapped.at[pl.ds(0, tokens)])):
        copy.wait()
    per = taken.shape[2] // 128
    square[...] = jnp.zeros_like(square)
    for r in range(2):

        @pl.loop(0, per)
        def _(i):
            block = where[1] + number[r * per + i]
            target = pl.ds(pl.multiple_of(place[r * per + i] * 128, 128), 128)
            value = taken[r, :, pl.ds(pl.multiple_of(i * 128, 128), 128)].astype(F32)
            square[...] += value * value
            raw[:, target] = (value * gain[pl.ds(block, 1), :]).astype(BF)
            if not own:
                source = pl.ds(pl.multiple_of(block * 128, 128), 128)
                a_rows[target, :] = a_both[source, :]

    columns = held.shape[1]
    tile = TILE if columns % TILE == 0 else 128
    low = jnp.dot(raw[...], a_rows[...], preferred_element_type=F32)
    out[:, columns : columns + 128] = low.astype(out.dtype)
    total = jnp.broadcast_to(jnp.sum(square[...], axis=1, keepdims=True), square.shape)
    if not own:
        lead = total.astype(BF)
        lane = lax.broadcasted_iota(jnp.int32, square.shape, 1)
        total = jnp.where(lane == 0, lead.astype(F32), total - lead.astype(F32))
    out[:, columns + 128 :] = total.astype(out.dtype)
    for copy in copies:
        copy.wait()

    @pl.loop(0, columns // tile)
    def _(n):
        at = pl.ds(pl.multiple_of(n * tile, tile), tile)
        total = jnp.dot(raw[...], held[:, at], preferred_element_type=F32)
        out[:, at] = total.astype(out.dtype)


def project(own, columns, number, place, where, parts, gain, a_both, other, blocks):
    tokens, quarter = parts[0].shape
    count = len(blocks)
    outs = [
        jax.ShapeDtypeStruct((tokens, 2 * quarter), BF),
        jax.ShapeDtypeStruct((tokens, columns + 256), F32 if own else BF),
    ]
    if not own:
        outs.append(jax.ShapeDtypeStruct((2 * quarter, 128), BF))
    return pl.pallas_call(
        functools.partial(project_kernel, own),
        in_specs=[pl.BlockSpec(memory_space=pltpu.SMEM)] * 3
        + any_specs(3)
        + vmem_specs(2)
        + any_specs(1 + count),
        out_specs=vmem_specs(len(outs)),
        out_shape=outs,
        scratch_shapes=[
            pltpu.VMEM((2, tokens, quarter), BF),
            pltpu.VMEM((2 * quarter, columns), BF),
            pltpu.VMEM((tokens, 128), F32),
            pltpu.SemaphoreType.DMA((count,)),
            pltpu.SemaphoreType.DMA((2,)),
        ],
        compiler_params=params(VMEM_LIMIT),
        cost_estimate=pl.CostEstimate(
            flops=4 * tokens * quarter * columns,
            bytes_accessed=4 * quarter * (2 * tokens + columns),
            transcendentals=0,
        ),
        name="project",
    )(number, place, where, *parts, gain.reshape(-1, 128), a_both, other, *blocks)


def project_rest_kernel(raw, *refs):
    sources, (out, held, sems) = refs[:-3], refs[-3:]
    columns = held.shape[1]
    begin = sources[0].shape[1] - columns
    copies = fetch([source.at[:, pl.ds(begin, columns)] for source in sources], held, sems)
    for copy in copies:
        copy.wait()

    @pl.loop(0, columns // 128)
    def _(n):
        at = pl.ds(pl.multiple_of(n * 128, 128), 128)
        out[:, at] = jnp.dot(raw[...], held[:, at], preferred_element_type=F32).astype(BF)


def project_rest(columns, raw, blocks):
    tokens, width = raw.shape
    count = len(blocks)
    return pl.pallas_call(
        project_rest_kernel,
        in_specs=vmem_specs(1) + any_specs(count),
        out_specs=vmem_specs(1)[0],
        out_shape=jax.ShapeDtypeStruct((tokens, columns), BF),
        scratch_shapes=[pltpu.VMEM((width, columns), BF), pltpu.SemaphoreType.DMA((count,))],
        compiler_params=params(VMEM_LIMIT),
        cost_estimate=pl.CostEstimate(
            flops=2 * tokens * width * columns,
            bytes_accessed=2 * width * (tokens + columns),
            transcendentals=0,
        ),
        name="project_rest",
    )(raw, *blocks)


def combine_kernel(features, kept, received, rest, up, kv, query, low, inverse):
    columns = kv.shape[1] + query.shape[1]
    last = columns + 128
    begin = columns - rest.shape[1]
    lead = begin + 128
    square = kept[:, last : last + 1] + received[:, lead : lead + 1].astype(F32)
    square += received[:, lead + 1 : lead + 2].astype(F32)
    inv = lax.rsqrt(square * (1.0 / features) + EPS)
    inverse[...] = inv
    low_sum = kept[:, columns:last] + received[:, begin:lead].astype(F32)
    low_sum = (low_sum * inv).astype(BF)
    low[...] = low_sum
    both = jnp.concatenate([received[:, :begin], rest[...]], axis=1)
    total = (kept[:, :columns] + both.astype(F32)) * inv
    total += ADAPTER_SCALE * jnp.dot(low_sum, up[...], preferred_element_type=F32)
    kv[...] = total[:, : 2 * HD].astype(BF)
    query[...] = total[:, 2 * HD :].astype(BF)


def combine(features, kept, received, rest, up):
    tokens = kept.shape[0]
    columns = up.shape[1]
    return pl.pallas_call(
        functools.partial(combine_kernel, features),
        in_specs=vmem_specs(4),
        out_specs=vmem_specs(4),
        out_shape=[
            jax.ShapeDtypeStruct((tokens, 2 * HD), BF),
            jax.ShapeDtypeStruct((tokens, columns - 2 * HD), BF),
            jax.ShapeDtypeStruct((tokens, 128), BF),
            jax.ShapeDtypeStruct((tokens, 1), F32),
        ],
        compiler_params=params(),
        cost_estimate=pl.CostEstimate(
            flops=2 * tokens * 128 * columns,
            bytes_accessed=8 * tokens * columns,
            transcendentals=0,
        ),
        name="combine",
    )(kept, received, rest, up)


def gain_kernel(count, numbers, *refs):
    packs, raws, a_rows = (refs[:4], refs[4:8]), refs[8:10], refs[10]
    sources, (out, held, rows, sems, row_sems) = refs[11 : 11 + count], refs[11 + count :]
    spans = []
    for source in sources:
        begin = spans[-1][1] if spans else 0
        spans.append((begin, begin + source.shape[0]))
    copies = fetch(sources, held, sems)
    row_copies = []
    for k, (begin, end) in enumerate(spans):
        at = pl.ds(begin, end - begin)
        for pack in range(2):
            copy = pltpu.make_async_copy(
                raws[pack].at[:, at], rows.at[pack, :, at], row_sems.at[pack, k]
            )
            copy.start()
            row_copies.append(copy)
    nt = (((1,), (1,)), ((), ()))
    for k, (begin, end) in enumerate(spans):
        at = slice(begin, end)
        copies[k].wait()
        sums = jnp.zeros((1, end - begin), F32)
        for pack, (dkv, dq, ranks, inverse) in enumerate(packs):
            row_copies[2 * k + pack].wait()
            term = lax.dot_general(dkv[...], held[at, : 2 * HD], nt, preferred_element_type=F32)
            term += lax.dot_general(dq[...], held[at, 2 * HD :], nt, preferred_element_type=F32)
            term += lax.dot_general(ranks[...], a_rows[at, :], nt, preferred_element_type=F32)
            term *= inverse[...] * rows[pack, :, at].astype(F32)
            sums += jnp.sum(term, axis=0, keepdims=True)
        for s in range((end - begin) // 128):
            out[pl.ds(numbers[begin // 128 + s], 1), :] = sums[:, s * 128 : (s + 1) * 128]


def gain_part(numbers, packs, raws, a_rows, blocks):
    tokens, width = raws[0].shape
    columns = blocks[0].shape[1]
    count = len(blocks)
    return pl.pallas_call(
        functools.partial(gain_kernel, count),
        in_specs=[pl.BlockSpec(memory_space=pltpu.SMEM)]
        + vmem_specs(8)
        + any_specs(2)
        + vmem_specs(1)
        + any_specs(count),
        out_specs=vmem_specs(1)[0],
        out_shape=jax.ShapeDtypeStruct((width // 128, 128), F32),
        scratch_shapes=[
            pltpu.VMEM((width, columns), BF),
            pltpu.VMEM((2, tokens, width), BF),
            pltpu.SemaphoreType.DMA((count,)),
            pltpu.SemaphoreType.DMA((2, count)),
        ],
        compiler_params=params(VMEM_LIMIT),
        cost_estimate=pl.CostEstimate(
            flops=4 * tokens * width * columns,
            bytes_accessed=2 * width * (2 * tokens + columns),
            transcendentals=0,
        ),
        name="gain_part",
    )(numbers, *packs[0], *packs[1], *raws, a_rows, *blocks)


def unite_kernel(partner, dq0, dq1, dkv0, dkv1, returned, up_query, up_value, dq, dkv, ranks):
    rank = up_query.shape[0]
    half = returned.shape[0]
    for h in range(dq.shape[1] // HD):
        source = (dq0, dq1)[h % 2]
        dq[:, h * HD : (h + 1) * HD] = source[:, h // 2 * HD : (h // 2 + 1) * HD]
    if partner:
        dkv[...] = dkv0[...]
    else:
        dkv[:half, :] = (dkv0[:half, :] + dkv1[:half, :]).astype(BF)
        dkv[half:, :] = (dkv0[half:, :] + dkv1[half:, :] + returned[...].astype(F32)).astype(BF)
    nt = (((1,), (1,)), ((), ()))
    of_query = lax.dot_general(dq[...], up_query[...], nt, preferred_element_type=F32)
    of_value = lax.dot_general(dkv[:, HD:], up_value[...], nt, preferred_element_type=F32)
    ranks[:, :rank] = (ADAPTER_SCALE * of_query).astype(BF)
    ranks[:, rank:] = (ADAPTER_SCALE * of_value).astype(BF)


def unite(partner, dq0, dq1, dkv0, dkv1, returned, up_query, up_value):
    tokens, columns = dq0.shape
    return pl.pallas_call(
        functools.partial(unite_kernel, partner),
        in_specs=vmem_specs(7),
        out_specs=vmem_specs(3),
        out_shape=[
            jax.ShapeDtypeStruct((tokens, 2 * columns), BF),
            jax.ShapeDtypeStruct((tokens, 2 * HD), BF),
            jax.ShapeDtypeStruct((tokens, 128), BF),
        ],
        compiler_params=params(),
        cost_estimate=pl.CostEstimate(
            flops=4 * tokens * columns * 64, bytes_accessed=8 * tokens * columns, transcendentals=0
        ),
        name="unite",
    )(dq0, dq1, dkv0, dkv1, returned, up_query, up_value)


def attend_kernel(odd, query, kv, prev, grads, docs_row, docs_col, *refs):
    if odd:
        out, dq, dkv, dprev, dk, dv = refs
    else:
        out, dq, dkv, dk, dv = refs
    tokens = kv.shape[0]
    half = tokens // 2
    scale = HD ** (-0.5)
    if odd:
        keys = jnp.concatenate([prev[:, :HD], kv[:, :HD]], axis=0)
        values = jnp.concatenate([prev[:, HD:], kv[:, HD:]], axis=0)
        spans = ((0, tokens), (tokens, tokens + half))
        doc_keys = docs_col[...]
        before = half
    else:
        keys, values = kv[:, :HD], kv[:, HD:]
        spans = ((0, half), (0, tokens))
        doc_keys = docs_col[half:, :]
        before = 0
    dk[...] = jnp.zeros_like(dk)
    dv[...] = jnp.zeros_like(dv)
    for part, (low, high) in enumerate(spans):
        rows = slice(part * half, (part + 1) * half)
        key_at = lax.broadcasted_iota(jnp.int32, (high - low, half), 0) + (low - before)
        query_at = lax.broadcasted_iota(jnp.int32, (high - low, half), 1) + part * half
        allowed = (doc_keys[low:high, :] == docs_row[:, rows]) & (key_at <= query_at)
        key, value = keys[low:high], values[low:high]
        for h in range(dq.shape[1] // HD):
            source = slice((2 * h + odd) * HD, (2 * h + odd + 1) * HD)
            target = slice(h * HD, (h + 1) * HD)
            row_query, cot = query[rows, source], grads[rows, source]
            scores = (
                lax.dot_general(
                    key, row_query, (((1,), (1,)), ((), ())), preferred_element_type=F32
                )
                * scale
            )
            scores = jnp.where(allowed, scores, NEG_FILL)
            expo = jnp.exp(scores - jnp.max(scores, axis=0, keepdims=True))
            probs = expo * (1.0 / jnp.sum(expo, axis=0, keepdims=True))
            probs_low = probs.astype(BF)
            output = lax.dot_general(
                value, probs_low, (((0,), (0,)), ((), ())), preferred_element_type=F32
            )
            out[rows, target] = output.T.astype(BF)
            dprob = lax.dot_general(
                value, cot, (((1,), (1,)), ((), ())), preferred_element_type=F32
            )
            delta = jnp.sum(probs_low.astype(F32) * dprob, axis=0, keepdims=True)
            dscore = (probs * (dprob - delta)).astype(BF)
            dquery = lax.dot_general(
                key, dscore, (((0,), (0,)), ((), ())), preferred_element_type=F32
            )
            dq[rows, target] = (dquery * scale).T.astype(BF)
            dk[low:high, :] += jnp.dot(dscore, row_query, preferred_element_type=F32)
            dv[low:high, :] += jnp.dot(probs_low, cot, preferred_element_type=F32)
    dkv[:, :HD] = dk[before:, :] * scale
    dkv[:, HD:] = dv[before:, :]
    if odd:
        dprev[:, :HD] = (dk[:before, :] * scale).astype(BF)
        dprev[:, HD:] = dv[:before, :].astype(BF)


def attend(odd, query, kv, prev, grads, docs_row, docs_col):
    tokens, columns = grads.shape
    half = tokens // 2
    span = tokens + half if odd else tokens
    outs = [
        jax.ShapeDtypeStruct((tokens, columns // 2), BF),
        jax.ShapeDtypeStruct((tokens, columns // 2), BF),
        jax.ShapeDtypeStruct((tokens, 2 * HD), F32),
    ]
    if odd:
        outs.append(jax.ShapeDtypeStruct((half, 2 * HD), BF))
    return pl.pallas_call(
        functools.partial(attend_kernel, odd),
        in_specs=vmem_specs(6),
        out_specs=vmem_specs(len(outs)),
        out_shape=outs,
        scratch_shapes=[pltpu.VMEM((span, HD), F32)] * 2,
        compiler_params=params(),
        cost_estimate=pl.CostEstimate(
            flops=5 * tokens * tokens * columns,
            bytes_accessed=4 * tokens * columns,
            transcendentals=tokens * tokens * columns // (2 * HD),
        ),
        name="attend",
    )(query, kv, prev, grads, docs_row, docs_col)


def dot_rows(left, right):
    return lax.dot_general(left, right, (((0,), (0,)), ((), ())), preferred_element_type=F32)


def dot_cols(left, right):
    return lax.dot_general(left, right, (((1,), (1,)), ((), ())), preferred_element_type=F32)


def sum_heads(value):
    total = value.astype(F32)
    for step in (1, 2, 3):
        total = total + shift(value, "mp", step).astype(F32)
    return total


def reduce_stage(chunks, whole, move):
    count = whole.shape[0]
    total = jnp.concatenate([whole, chunks[0]], axis=0)
    low = whole.astype(BF)
    for i in (1, 2, 3):
        packed = jnp.concatenate([low, chunks[i].astype(BF)], axis=0)
        total = total + move(packed, REL[i]).astype(F32)
    return total[:count], total[count:]


def per_device(
    hidden,
    gain,
    query_frozen_weight,
    w_key,
    value_frozen_weight,
    a_query,
    query_up_weight,
    a_value,
    value_up_weight,
    doc_ids,
    d_out,
):
    tokens = hidden.shape[1]
    half = tokens // 2
    dp, seq, mp = lax.axis_index("dp"), lax.axis_index("seq"), lax.axis_index("mp")
    pair, high = dp // 4, mp // 2
    own = hidden[0]
    turned = turn(own, 0, 0)
    weights = jnp.concatenate([w_key, value_frozen_weight, query_frozen_weight], axis=1)
    pieces = first_rings(weights)
    a_both = jnp.concatenate([a_query, a_value], axis=1)
    inners = assemble(pieces, a_both)
    turned = tie(turned, corners(inners))
    turned_high = shift(turned, "mp", 2)
    first, second = second_rings(inners)
    turned_high = tie(turned_high, corners(first[1:3] + second[1:3]))
    swapped = shift(jnp.concatenate([turned, turned_high], axis=0), "mp", 1)
    hidden_parts = [turned, turned_high, swapped]
    number, place, number_at = block_places(dp % 4, seq, mp % 2)
    where = jnp.stack([jnp.where(pair == high, 0, 1), pair * 32]).astype(jnp.int32)
    blocks = first + second
    columns = weights.shape[1]
    raw_other, sent, a_rows = project(
        False, columns // 2, number, place, where, hidden_parts, gain, a_both, a_both, blocks
    )
    received = shift(sent, "zl", 1)
    sent_rest = project_rest(columns - columns // 2, raw_other, blocks)
    received_rest = shift(sent_rest, "zl", 1)
    raw_own, kept = project(
        True, columns, number, place, where, hidden_parts, gain, a_rows, sent_rest, blocks
    )
    rank = query_up_weight.shape[0]
    up = jnp.concatenate(
        [
            jnp.concatenate([jnp.zeros((rank, 2 * HD), BF), query_up_weight], axis=1),
            jnp.concatenate(
                [jnp.zeros((rank, HD), BF), value_up_weight, jnp.zeros_like(query_up_weight)], axis=1
            ),
        ],
        axis=0,
    )
    kv, query, low, inverse = combine(gain.shape[0], kept, received, received_rest, up)
    inverse_row = shift(tie(inverse.reshape(-1, 128), kv), "zl", 1)
    prev = lax.ppermute(kv[half:], "seq", [(i, i + 1) for i in range(3)])

    docs = doc_ids[0]
    begin = seq * tokens
    own_docs = lax.dynamic_slice_in_dim(docs, begin, tokens)
    prev_docs = lax.dynamic_slice_in_dim(docs, jnp.maximum(begin - half, 0), half)
    prev_docs = jnp.where(seq > 0, prev_docs, -1)
    ext_docs = jnp.concatenate([prev_docs, own_docs])
    masks = (own_docs[None, :], ext_docs[:, None])
    out_even, dq_even, dkv_even = attend(0, query, kv, kv[half:], d_out[0], *masks)
    dq_even_other = shift(dq_even, "zl", 1)
    out_odd, dq_odd, dkv_odd, dprev = attend(1, query, kv, prev, d_out[0], *masks)
    dq_odd_other = shift(dq_odd, "zl", 1)
    returned = lax.ppermute(dprev, "seq", [(i + 1, i) for i in range(3)])
    dq, dkv, ranks_own = unite(
        False, dq_even, dq_odd, dkv_even, dkv_odd, returned, query_up_weight, value_up_weight
    )
    dkv_other = shift(dkv, "zl", 1)
    dq_other, dkv_other, ranks_other = unite(
        True,
        dq_even_other,
        dq_odd_other,
        dkv_other,
        dkv_other,
        returned,
        query_up_weight,
        value_up_weight,
    )
    output = []
    for h in range(out_even.shape[1] // HD):
        at = slice(h * HD, (h + 1) * HD)
        output += [out_even[:, at], out_odd[:, at]]
    output = jnp.concatenate(output, axis=1)
    inverses = (inverse, tie(inverse_row, dq_other).reshape(-1, 1))
    rank_rows = sum_heads(jnp.concatenate([ranks_own, ranks_other], axis=0))
    rank_rows = (rank_rows * jnp.concatenate(inverses, axis=0)).astype(BF)

    up_rows = ADAPTER_SCALE * jnp.concatenate(
        [dot_rows(low[:, rank:], dkv[:, HD:]), dot_rows(low[:, :rank], dq)], axis=1
    )
    up_rows = tie(up_rows, dkv)
    turns = iter((("dp", 1), ("dp", 2), ("seq", 1), ("seq", 2), ("dp", 4)))

    def add_next(rows, *others):
        axis, step = next(turns)
        moved = shift(rows.astype(BF), axis, step)
        if others:
            moved = tie(moved, *others)
        return rows + moved.astype(F32)

    up_rows = add_next(up_rows, dq_other)
    packs = (
        (dkv, dq, ranks_own, inverses[0]),
        (dkv_other, dq_other, ranks_other, inverses[1]),
    )
    gains = gain_part(number_at, packs, (raw_own, raw_other), a_rows, blocks)
    up_rows = add_next(up_rows, gains)

    def row_products(raw, rows):
        width = raw.shape[1]
        mine = lax.dynamic_slice_in_dim(raw, high * (width // 2), width // 2, 1)
        return dot_rows(mine, rows)

    grad_a = row_products(raw_own, rank_rows[:tokens]) + row_products(
        raw_other, rank_rows[tokens:]
    )
    grad_a = grad_a.reshape(16, 2, 64, 2 * rank)
    grad_a = lax.dynamic_index_in_dim(grad_a, mp % 2, 1, keepdims=False)
    grad_a = grad_a.reshape(4, 256, 2 * rank)
    whole, grad_a = reduce_stage(grad_a, gains, lambda v, step: shift_plane(v, 0, step))
    up_rows = add_next(up_rows, whole)
    grad_a = grad_a.reshape(4, 64, 2 * rank)
    whole, grad_a = reduce_stage(grad_a, whole, lambda v, step: shift_plane(v, 1, step))
    up_rows = add_next(up_rows, whole)
    gains = whole.astype(BF)
    gain_sum = jnp.zeros((16, 128), F32)
    for flip_core in range(2):
        send = lax.dynamic_slice_in_dim(gains, (mp % 2 ^ flip_core) * 16, 16, 0)
        for flip_z in range(2):
            gain_sum = gain_sum + turn(send, flip_z, flip_core).astype(F32)
    up_rows = add_next(up_rows)
    gain_sum = gain_sum.reshape(-1)
    gain_own = lax.dynamic_slice_in_dim(gain, mp * gain_sum.shape[0], gain_sum.shape[0])
    return (
        output[None],
        grad_a[:, :rank],
        up_rows[:, HD:],
        grad_a[:, rank:],
        up_rows[:, :HD],
        gain_sum / gain_own,
    )


def solution(mesh):
    return jax.shard_map(
        per_device,
        mesh=mesh,
        in_specs=(
            P("dp", "seq", "mp"),
            P(),
            P(("dp", "seq"), "mp"),
            P(("dp", "seq"), "mp"),
            P(("dp", "seq"), "mp"),
            P(),
            P(None, "mp"),
            P(),
            P(None, "mp"),
            P("dp", None),
            P("dp", "seq", "mp"),
        ),
        out_specs=(
            P("dp", "seq", "mp"),
            P(("dp", "seq", "mp"), None),
            P(None, "mp"),
            P(("dp", "seq", "mp"), None),
            P(None, "mp"),
            P("mp"),
        ),
        check_vma=False,
    )
```

```python
import functools

import jax
import jax.numpy as jnp
from jax import lax
from jax.experimental import pallas as pl
from jax.experimental.pallas import tpu as pltpu
from jax.sharding import PartitionSpec as P

HD = 128
EPS = 1e-05
ADAPTER_SCALE = 0.25
NEG_FILL = -1e30
BF = jnp.bfloat16
F32 = jnp.float32
VMEM_LIMIT = 56 * 1024 * 1024
VMEM_SMALL = 24 * 1024 * 1024
REL = (0, -1, 1, 2)
ROWS = 512


def shift(value, axis, step):
    if axis == "x":
        route = [(z * 4 + i, z * 4 + (i + step) % 4) for z in range(2) for i in range(4)]
        return lax.ppermute(value, "dp", route)
    if axis == "dp":
        return lax.ppermute(value, "dp", [(i, i ^ step) for i in range(8)])
    if axis == "zl":
        return lax.ppermute(value, "dp", [(i, (i + 4) % 8) for i in range(8)])
    if axis == "seq":
        return lax.ppermute(value, "seq", [(i, i ^ step) for i in range(4)])
    if axis == "y":
        return lax.ppermute(value, "seq", [(i, (i + step) % 4) for i in range(4)])
    return lax.ppermute(value, "mp", [(i, i ^ step) for i in range(4)])


def shift_plane(value, stage, step):
    route = []
    for z in range(2):
        for x in range(4):
            for y in range(4):
                for m in range(4):
                    to_x, to_y = x, y
                    if (m < 2) == (stage == 0):
                        to_y = (y + step) % 4
                    else:
                        to_x = (x + step) % 4
                    route.append(
                        (((z * 4 + x) * 4 + y) * 4 + m, ((z * 4 + to_x) * 4 + to_y) * 4 + m)
                    )
    return lax.ppermute(value, ("dp", "seq", "mp"), route)


def params(limit=VMEM_SMALL):
    return pltpu.CompilerParams(vmem_limit_bytes=limit)


def any_specs(count):
    return [pl.BlockSpec(memory_space=pl.ANY)] * count


def vmem_specs(count):
    return [pl.BlockSpec(memory_space=pltpu.VMEM)] * count


def assemble_kernel(*refs):
    pieces, outs = refs[:8], refs[-2:]
    rows = pieces[0].shape[0]
    for k, piece in enumerate(pieces):
        outs[k // 4][k % 4 * rows : (k % 4 + 1) * rows, :] = piece[...]


def assemble(pieces, *others):
    rows, columns = pieces[0].shape
    return pl.pallas_call(
        assemble_kernel,
        in_specs=vmem_specs(8) + any_specs(len(others)),
        out_specs=vmem_specs(2),
        out_shape=[jax.ShapeDtypeStruct((4 * rows, columns), BF)] * 2,
        compiler_params=params(),
        cost_estimate=pl.CostEstimate(
            flops=0, bytes_accessed=32 * rows * columns, transcendentals=0
        ),
        name="assemble",
    )(*pieces, *others)


def first_rings(shard):
    half = shard.shape[0] // 2
    pieces = []
    for part, axis in ((shard[:half], "x"), (shard[half:], "y")):
        pieces += [part] + [shift(part, axis, -step) for step in REL[1:]]
    return pieces


def second_rings(inners):
    blocks = []
    for inner, axis in zip(inners, ("y", "x")):
        before, after = shift(inner, axis, 1), shift(inner, axis, -1)
        blocks.append(
            [inner, before, after]
            + [shift(before[: ROWS // 2], axis, 1), shift(after[ROWS // 2 :], axis, -1)]
        )
    return blocks


def tie_kernel(*refs):
    del refs


def tie(value, *others):
    return pl.pallas_call(
        tie_kernel,
        in_specs=any_specs(1 + len(others)),
        out_specs=any_specs(1)[0],
        out_shape=jax.ShapeDtypeStruct(value.shape, value.dtype),
        input_output_aliases={0: 0},
        compiler_params=params(VMEM_LIMIT),
        name="tie",
    )(value, *others)


def corners(values):
    return jnp.concatenate([value[:16, :128] for value in values], axis=0)


def turn(value, flip_z, flip_core, stay=True):
    route = []
    for zl in range(2):
        for x in range(4):
            for zh in range(2):
                for c in range(2):
                    target = ((zh ^ flip_z) * 4 + x) * 4 + zl * 2 + (c ^ flip_core)
                    source = (zl * 4 + x) * 4 + zh * 2 + c
                    if stay or source != target:
                        route.append((source, target))
    return lax.ppermute(value, ("dp", "mp"), route)


def block_places(x, y, core):
    at = jnp.arange(32, dtype=jnp.int32)
    number = ((at // 16) ^ core) * 16 + at % 16
    order, shard = number % 2, number // 2
    inverse = jnp.array([0, 2, 3, 1], jnp.int32)
    by_x = inverse[(shard // 4 - x) % 4]
    by_y = inverse[(shard % 4 - y) % 4]
    outer = jnp.where(order == 0, by_y, by_x)
    inner = jnp.where(order == 0, by_x, by_y)
    place = order * 16 + outer * 4 + inner
    number_at = jnp.sum(jnp.where(place[None, :] == at[:, None], number[None, :], 0), axis=1)
    return number, place, number_at.astype(jnp.int32)


def fetch(sources, held, sems):
    copies = []
    begin = 0
    for k, source in enumerate(sources):
        rows = source.shape[0]
        copies.append(
            pltpu.make_async_copy(source, held.at[pl.ds(begin, rows)], sems.at[k])
        )
        begin += rows
    for copy in copies:
        copy.start()
    return copies


TILE = 256


def project_kernel(own, number, place, where, p0, p1, swapped, gain, a_both, other, *refs):
    del other
    if own:
        sources, (raw, out, taken, held, square, sems, take_sems) = refs[:-7], refs[-7:]
        a_rows = a_both
    else:
        sources, (raw, out, a_rows, taken, held, square, sems, take_sems) = refs[:-8], refs[-8:]

    tokens = p0.shape[0]

    def take(parts):
        return [pltpu.make_async_copy(p, taken.at[k], take_sems.at[k]) for k, p in enumerate(parts)]

    @pl.when(where[0] == (0 if own else 1))
    def _():
        for copy in take((p0, swapped.at[pl.ds(0, tokens)])):
            copy.start()

    @pl.when(where[0] != (0 if own else 1))
    def _():
        for copy in take((p1, swapped.at[pl.ds(tokens, tokens)])):
            copy.start()

    copies = fetch([source.at[:, pl.ds(0, held.shape[1])] for source in sources], held, sems)
    for copy in take((p0, swapped.at[pl.ds(0, tokens)])):
        copy.wait()
    per = taken.shape[2] // 128
    square[...] = jnp.zeros_like(square)
    for r in range(2):

        @pl.loop(0, per)
        def _(i):
            block = where[1] + number[r * per + i]
            target = pl.ds(pl.multiple_of(place[r * per + i] * 128, 128), 128)
            value = taken[r, :, pl.ds(pl.multiple_of(i * 128, 128), 128)].astype(F32)
            square[...] += value * value
            raw[:, target] = (value * gain[pl.ds(block, 1), :]).astype(BF)
            if not own:
                source = pl.ds(pl.multiple_of(block * 128, 128), 128)
                a_rows[target, :] = a_both[source, :]

    columns = held.shape[1]
    tile = TILE if columns % TILE == 0 else 128
    low = jnp.dot(raw[...], a_rows[...], preferred_element_type=F32)
    out[:, columns : columns + 128] = low.astype(out.dtype)
    total = jnp.broadcast_to(jnp.sum(square[...], axis=1, keepdims=True), square.shape)
    if not own:
        lead = total.astype(BF)
        lane = lax.broadcasted_iota(jnp.int32, square.shape, 1)
        total = jnp.where(lane == 0, lead.astype(F32), total - lead.astype(F32))
    out[:, columns + 128 :] = total.astype(out.dtype)
    for copy in copies:
        copy.wait()

    @pl.loop(0, columns // tile)
    def _(n):
        at = pl.ds(pl.multiple_of(n * tile, tile), tile)
        total = jnp.dot(raw[...], held[:, at], preferred_element_type=F32)
        out[:, at] = total.astype(out.dtype)


def project(own, columns, number, place, where, parts, gain, a_both, other, blocks):
    tokens, quarter = parts[0].shape
    count = len(blocks)
    outs = [
        jax.ShapeDtypeStruct((tokens, 2 * quarter), BF),
        jax.ShapeDtypeStruct((tokens, columns + 256), F32 if own else BF),
    ]
    if not own:
        outs.append(jax.ShapeDtypeStruct((2 * quarter, 128), BF))
    return pl.pallas_call(
        functools.partial(project_kernel, own),
        in_specs=[pl.BlockSpec(memory_space=pltpu.SMEM)] * 3
        + any_specs(3)
        + vmem_specs(2)
        + any_specs(1 + count),
        out_specs=vmem_specs(len(outs)),
        out_shape=outs,
        scratch_shapes=[
            pltpu.VMEM((2, tokens, quarter), BF),
            pltpu.VMEM((2 * quarter, columns), BF),
            pltpu.VMEM((tokens, 128), F32),
            pltpu.SemaphoreType.DMA((count,)),
            pltpu.SemaphoreType.DMA((2,)),
        ],
        compiler_params=params(VMEM_LIMIT),
        cost_estimate=pl.CostEstimate(
            flops=4 * tokens * quarter * columns,
            bytes_accessed=4 * quarter * (2 * tokens + columns),
            transcendentals=0,
        ),
        name="project",
    )(number, place, where, *parts, gain.reshape(-1, 128), a_both, other, *blocks)


def project_rest_kernel(raw, *refs):
    sources, (out, held, sems) = refs[:-3], refs[-3:]
    columns = held.shape[1]
    begin = sources[0].shape[1] - columns
    copies = fetch([source.at[:, pl.ds(begin, columns)] for source in sources], held, sems)
    for copy in copies:
        copy.wait()

    @pl.loop(0, columns // TILE)
    def _(n):
        at = pl.ds(pl.multiple_of(n * TILE, TILE), TILE)
        out[:, at] = jnp.dot(raw[...], held[:, at], preferred_element_type=F32).astype(BF)


def project_rest(columns, raw, blocks):
    tokens, width = raw.shape
    count = len(blocks)
    return pl.pallas_call(
        project_rest_kernel,
        in_specs=vmem_specs(1) + any_specs(count),
        out_specs=vmem_specs(1)[0],
        out_shape=jax.ShapeDtypeStruct((tokens, columns), BF),
        scratch_shapes=[pltpu.VMEM((width, columns), BF), pltpu.SemaphoreType.DMA((count,))],
        compiler_params=params(VMEM_LIMIT),
        cost_estimate=pl.CostEstimate(
            flops=2 * tokens * width * columns,
            bytes_accessed=2 * width * (tokens + columns),
            transcendentals=0,
        ),
        name="project_rest",
    )(raw, *blocks)


def combine_kernel(features, kept, received, rest, up, kv, query, low, inverse):
    columns = kv.shape[1] + query.shape[1]
    last = columns + 128
    begin = columns - rest.shape[1]
    lead = begin + 128
    square = kept[:, last : last + 1] + received[:, lead : lead + 1].astype(F32)
    square += received[:, lead + 1 : lead + 2].astype(F32)
    inv = lax.rsqrt(square * (1.0 / features) + EPS)
    inverse[...] = inv
    low_sum = kept[:, columns:last] + received[:, begin:lead].astype(F32)
    low_sum = (low_sum * inv).astype(BF)
    low[...] = low_sum
    both = jnp.concatenate([received[:, :begin], rest[...]], axis=1)
    total = (kept[:, :columns] + both.astype(F32)) * inv
    total += ADAPTER_SCALE * jnp.dot(low_sum, up[...], preferred_element_type=F32)
    kv[...] = total[:, : 2 * HD].astype(BF)
    query[...] = total[:, 2 * HD :].astype(BF)


def combine(features, kept, received, rest, up):
    tokens = kept.shape[0]
    columns = up.shape[1]
    return pl.pallas_call(
        functools.partial(combine_kernel, features),
        in_specs=vmem_specs(4),
        out_specs=vmem_specs(4),
        out_shape=[
            jax.ShapeDtypeStruct((tokens, 2 * HD), BF),
            jax.ShapeDtypeStruct((tokens, columns - 2 * HD), BF),
            jax.ShapeDtypeStruct((tokens, 128), BF),
            jax.ShapeDtypeStruct((tokens, 1), F32),
        ],
        compiler_params=params(),
        cost_estimate=pl.CostEstimate(
            flops=2 * tokens * 128 * columns,
            bytes_accessed=8 * tokens * columns,
            transcendentals=0,
        ),
        name="combine",
    )(kept, received, rest, up)


def gain_kernel(count, numbers, *refs):
    packs, inverse, a_rows, raws = (refs[:3], refs[3:6]), refs[6], refs[7], refs[8:10]
    sources, rest = refs[10 : 10 + count], refs[10 + count :]
    out, held, rows, grads, inv, sems, row_sems = rest
    tokens = raws[0].shape[0]
    columns = held.shape[1]
    spans = []
    for source in sources:
        begin = spans[-1][1] if spans else 0
        spans.append((begin, begin + source.shape[0]))
    copies = fetch(sources, held, sems)
    row_copies = []
    for k, (begin, end) in enumerate(spans):
        at = pl.ds(begin, end - begin)
        for pack in range(2):
            copy = pltpu.make_async_copy(
                raws[pack].at[:, at], rows.at[pl.ds(pack * tokens, tokens), at], row_sems.at[pack, k]
            )
            copy.start()
            row_copies.append(copy)
    for pack, (dkv, dq, ranks) in enumerate(packs):
        at = slice(pack * tokens, (pack + 1) * tokens)
        grads[at, : 2 * HD] = dkv[...]
        grads[at, 2 * HD : columns] = dq[...]
        grads[at, columns:] = ranks[...]
    inv[...] = jnp.broadcast_to(inverse[...], inv.shape)
    nt = (((1,), (1,)), ((), ()))
    for k, (begin, end) in enumerate(spans):
        at = slice(begin, end)
        copies[k].wait()
        row_copies[2 * k].wait()
        row_copies[2 * k + 1].wait()
        term = lax.dot_general(grads[:, :columns], held[at, :], nt, preferred_element_type=F32)
        term += lax.dot_general(grads[:, columns:], a_rows[at, :], nt, preferred_element_type=F32)
        term *= inv[:, : end - begin] * rows[:, at].astype(F32)
        sums = jnp.sum(term, axis=0, keepdims=True)
        for s in range((end - begin) // 128):
            out[pl.ds(numbers[begin // 128 + s], 1), :] = sums[:, s * 128 : (s + 1) * 128]


def gain_part(numbers, packs, inverse, raws, a_rows, blocks):
    tokens, width = raws[0].shape
    columns = blocks[0].shape[1]
    count = len(blocks)
    return pl.pallas_call(
        functools.partial(gain_kernel, count),
        in_specs=[pl.BlockSpec(memory_space=pltpu.SMEM)]
        + vmem_specs(8)
        + any_specs(2 + count),
        out_specs=vmem_specs(1)[0],
        out_shape=jax.ShapeDtypeStruct((width // 128, 128), F32),
        scratch_shapes=[
            pltpu.VMEM((width, columns), BF),
            pltpu.VMEM((2 * tokens, width), BF),
            pltpu.VMEM((2 * tokens, columns + 128), BF),
            pltpu.VMEM((2 * tokens, ROWS), F32),
            pltpu.SemaphoreType.DMA((count,)),
            pltpu.SemaphoreType.DMA((2, count)),
        ],
        compiler_params=params(VMEM_LIMIT),
        cost_estimate=pl.CostEstimate(
            flops=4 * tokens * width * columns,
            bytes_accessed=2 * width * (2 * tokens + columns),
            transcendentals=0,
        ),
        name="gain_part",
    )(numbers, *packs[0], *packs[1], inverse, a_rows, *raws, *blocks)


def unite_kernel(partner, dq0, dq1, dkv0, dkv1, returned, up_query, up_value, dq, dkv, ranks):
    rank = up_query.shape[0]
    half = returned.shape[0]
    for h in range(dq.shape[1] // HD):
        source = (dq0, dq1)[h % 2]
        dq[:, h * HD : (h + 1) * HD] = source[:, h // 2 * HD : (h // 2 + 1) * HD]
    if partner:
        dkv[...] = dkv0[...]
    else:
        dkv[:half, :] = (dkv0[:half, :] + dkv1[:half, :]).astype(BF)
        dkv[half:, :] = (dkv0[half:, :] + dkv1[half:, :] + returned[...].astype(F32)).astype(BF)
    nt = (((1,), (1,)), ((), ()))
    of_query = lax.dot_general(dq[...], up_query[...], nt, preferred_element_type=F32)
    of_value = lax.dot_general(dkv[:, HD:], up_value[...], nt, preferred_element_type=F32)
    ranks[:, :rank] = (ADAPTER_SCALE * of_query).astype(BF)
    ranks[:, rank:] = (ADAPTER_SCALE * of_value).astype(BF)


def unite(partner, dq0, dq1, dkv0, dkv1, returned, up_query, up_value):
    tokens, columns = dq0.shape
    return pl.pallas_call(
        functools.partial(unite_kernel, partner),
        in_specs=vmem_specs(7),
        out_specs=vmem_specs(3),
        out_shape=[
            jax.ShapeDtypeStruct((tokens, 2 * columns), BF),
            jax.ShapeDtypeStruct((tokens, 2 * HD), BF),
            jax.ShapeDtypeStruct((tokens, 128), BF),
        ],
        compiler_params=params(),
        cost_estimate=pl.CostEstimate(
            flops=4 * tokens * columns * 64, bytes_accessed=8 * tokens * columns, transcendentals=0
        ),
        name="unite",
    )(dq0, dq1, dkv0, dkv1, returned, up_query, up_value)


def attend_kernel(odd, query, kv, prev, grads, docs_row, docs_col, *refs):
    if odd:
        out, dq, dkv, dprev, dk, dv = refs
    else:
        out, dq, dkv, dk, dv = refs
    tokens = kv.shape[0]
    half = tokens // 2
    scale = HD ** (-0.5)
    if odd:
        keys = jnp.concatenate([prev[:, :HD], kv[:, :HD]], axis=0)
        values = jnp.concatenate([prev[:, HD:], kv[:, HD:]], axis=0)
        spans = ((0, tokens), (tokens, tokens + half))
        doc_keys = docs_col[...]
        before = half
    else:
        keys, values = kv[:, :HD], kv[:, HD:]
        spans = ((0, half), (0, tokens))
        doc_keys = docs_col[half:, :]
        before = 0
    dk[...] = jnp.zeros_like(dk)
    dv[...] = jnp.zeros_like(dv)
    for part, (low, high) in enumerate(spans):
        rows = slice(part * half, (part + 1) * half)
        key_at = lax.broadcasted_iota(jnp.int32, (high - low, half), 0) + (low - before)
        query_at = lax.broadcasted_iota(jnp.int32, (high - low, half), 1) + part * half
        allowed = (doc_keys[low:high, :] == docs_row[:, rows]) & (key_at <= query_at)
        key, value = keys[low:high], values[low:high]
        for h in range(dq.shape[1] // HD):
            source = slice((2 * h + odd) * HD, (2 * h + odd + 1) * HD)
            target = slice(h * HD, (h + 1) * HD)
            row_query, cot = query[rows, source], grads[rows, source]
            scores = (
                lax.dot_general(
                    key, row_query, (((1,), (1,)), ((), ())), preferred_element_type=F32
                )
                * scale
            )
            scores = jnp.where(allowed, scores, NEG_FILL)
            expo = jnp.exp(scores - jnp.max(scores, axis=0, keepdims=True))
            probs = expo * (1.0 / jnp.sum(expo, axis=0, keepdims=True))
            probs_low = probs.astype(BF)
            output = lax.dot_general(
                value, probs_low, (((0,), (0,)), ((), ())), preferred_element_type=F32
            )
            out[rows, target] = output.T.astype(BF)
            dprob = lax.dot_general(
                value, cot, (((1,), (1,)), ((), ())), preferred_element_type=F32
            )
            delta = jnp.sum(probs_low.astype(F32) * dprob, axis=0, keepdims=True)
            dscore = (probs * (dprob - delta)).astype(BF)
            dquery = lax.dot_general(
                key, dscore, (((0,), (0,)), ((), ())), preferred_element_type=F32
            )
            dq[rows, target] = (dquery * scale).T.astype(BF)
            dk[low:high, :] += jnp.dot(dscore, row_query, preferred_element_type=F32)
            dv[low:high, :] += jnp.dot(probs_low, cot, preferred_element_type=F32)
    dkv[:, :HD] = dk[before:, :] * scale
    dkv[:, HD:] = dv[before:, :]
    if odd:
        dprev[:, :HD] = (dk[:before, :] * scale).astype(BF)
        dprev[:, HD:] = dv[:before, :].astype(BF)


def attend(odd, query, kv, prev, grads, docs_row, docs_col):
    tokens, columns = grads.shape
    half = tokens // 2
    span = tokens + half if odd else tokens
    outs = [
        jax.ShapeDtypeStruct((tokens, columns // 2), BF),
        jax.ShapeDtypeStruct((tokens, columns // 2), BF),
        jax.ShapeDtypeStruct((tokens, 2 * HD), F32),
    ]
    if odd:
        outs.append(jax.ShapeDtypeStruct((half, 2 * HD), BF))
    return pl.pallas_call(
        functools.partial(attend_kernel, odd),
        in_specs=vmem_specs(6),
        out_specs=vmem_specs(len(outs)),
        out_shape=outs,
        scratch_shapes=[pltpu.VMEM((span, HD), F32)] * 2,
        compiler_params=params(),
        cost_estimate=pl.CostEstimate(
            flops=5 * tokens * tokens * columns,
            bytes_accessed=4 * tokens * columns,
            transcendentals=tokens * tokens * columns // (2 * HD),
        ),
        name="attend",
    )(query, kv, prev, grads, docs_row, docs_col)


def dot_rows(left, right):
    return lax.dot_general(left, right, (((0,), (0,)), ((), ())), preferred_element_type=F32)


def dot_cols(left, right):
    return lax.dot_general(left, right, (((1,), (1,)), ((), ())), preferred_element_type=F32)


def sum_heads(value):
    total = value.astype(F32)
    for step in (1, 2, 3):
        total = total + shift(value, "mp", step).astype(F32)
    return total


def reduce_stage(chunks, whole, move):
    count = whole.shape[0]
    total = jnp.concatenate([whole, chunks[0]], axis=0)
    low = whole.astype(BF)
    for i in (1, 2, 3):
        packed = jnp.concatenate([low, chunks[i].astype(BF)], axis=0)
        total = total + move(packed, REL[i]).astype(F32)
    return total[:count], total[count:]


def per_device(
    hidden,
    gain,
    query_frozen_weight,
    w_key,
    value_frozen_weight,
    a_query,
    query_up_weight,
    a_value,
    value_up_weight,
    doc_ids,
    d_out,
):
    tokens = hidden.shape[1]
    half = tokens // 2
    dp, seq, mp = lax.axis_index("dp"), lax.axis_index("seq"), lax.axis_index("mp")
    pair, high = dp // 4, mp // 2
    own = hidden[0]
    turned = turn(own, 0, 0, stay=False)
    weights = jnp.concatenate([w_key, value_frozen_weight, query_frozen_weight], axis=1)
    pieces = first_rings(weights)
    a_both = jnp.concatenate([a_query, a_value], axis=1)
    inners = assemble(pieces, a_both)
    turned = jnp.where(pair == high, own, tie(turned, corners(inners)))
    turned_high = shift(turned, "mp", 2)
    first, second = second_rings(inners)
    turned_high = tie(turned_high, corners(first[1:3] + second[1:3]))
    swapped = shift(jnp.concatenate([turned, turned_high], axis=0), "mp", 1)
    hidden_parts = [turned, turned_high, swapped]
    number, place, number_at = block_places(dp % 4, seq, mp % 2)
    where = jnp.stack([jnp.where(pair == high, 0, 1), pair * 32]).astype(jnp.int32)
    blocks = first + second
    columns = weights.shape[1]
    lead = 3 * columns // 5
    raw_other, sent, a_rows = project(
        False, lead, number, place, where, hidden_parts, gain, a_both, a_both, blocks
    )
    received = shift(sent, "zl", 1)
    sent_rest = project_rest(columns - lead, raw_other, blocks)
    received_rest = shift(sent_rest, "zl", 1)
    raw_own, kept = project(
        True, columns, number, place, where, hidden_parts, gain, a_rows, sent_rest, blocks
    )
    rank = query_up_weight.shape[0]
    up = jnp.concatenate(
        [
            jnp.concatenate([jnp.zeros((rank, 2 * HD), BF), query_up_weight], axis=1),
            jnp.concatenate(
                [jnp.zeros((rank, HD), BF), value_up_weight, jnp.zeros_like(query_up_weight)], axis=1
            ),
        ],
        axis=0,
    )
    kv, query, low, inverse = combine(gain.shape[0], kept, received, received_rest, up)
    inverse_row = shift(tie(inverse.reshape(-1, 128), kv), "zl", 1)
    prev = lax.ppermute(kv[half:], "seq", [(i, i + 1) for i in range(3)])

    docs = doc_ids[0]
    begin = seq * tokens
    own_docs = lax.dynamic_slice_in_dim(docs, begin, tokens)
    prev_docs = lax.dynamic_slice_in_dim(docs, jnp.maximum(begin - half, 0), half)
    prev_docs = jnp.where(seq > 0, prev_docs, -1)
    ext_docs = jnp.concatenate([prev_docs, own_docs])
    masks = (own_docs[None, :], ext_docs[:, None])
    out_even, dq_even, dkv_even = attend(0, query, kv, kv[half:], d_out[0], *masks)
    dq_even_other = shift(dq_even, "zl", 1)
    out_odd, dq_odd, dkv_odd, dprev = attend(1, query, kv, prev, d_out[0], *masks)
    dq_odd_other = shift(dq_odd, "zl", 1)
    returned = lax.ppermute(dprev, "seq", [(i + 1, i) for i in range(3)])
    dq, dkv, ranks_own = unite(
        False, dq_even, dq_odd, dkv_even, dkv_odd, returned, query_up_weight, value_up_weight
    )
    dkv_other = shift(dkv, "zl", 1)
    dq_other, dkv_other, ranks_other = unite(
        True,
        dq_even_other,
        dq_odd_other,
        dkv_other,
        dkv_other,
        returned,
        query_up_weight,
        value_up_weight,
    )
    output = []
    for h in range(out_even.shape[1] // HD):
        at = slice(h * HD, (h + 1) * HD)
        output += [out_even[:, at], out_odd[:, at]]
    output = jnp.concatenate(output, axis=1)
    inverses = (inverse, tie(inverse_row, dq_other).reshape(-1, 1))
    rank_rows = sum_heads(jnp.concatenate([ranks_own, ranks_other], axis=0))
    rank_rows = (rank_rows * jnp.concatenate(inverses, axis=0)).astype(BF)

    up_rows = ADAPTER_SCALE * jnp.concatenate(
        [dot_rows(low[:, rank:], dkv[:, HD:]), dot_rows(low[:, :rank], dq)], axis=1
    )
    up_rows = tie(up_rows, dkv)
    turns = iter((("dp", 1), ("dp", 2), ("seq", 1), ("seq", 2), ("dp", 4)))

    def add_next(rows, *others):
        axis, step = next(turns)
        moved = shift(rows.astype(BF), axis, step)
        if others:
            moved = tie(moved, *others)
        return rows + moved.astype(F32)

    up_rows = add_next(up_rows, dq_other)
    packs = ((dkv, dq, ranks_own), (dkv_other, dq_other, ranks_other))
    gains = gain_part(
        number_at, packs, jnp.concatenate(inverses, axis=0), (raw_own, raw_other), a_rows, blocks
    )
    up_rows = add_next(up_rows, gains)

    def row_products(raw, rows):
        width = raw.shape[1]
        mine = lax.dynamic_slice_in_dim(raw, high * (width // 2), width // 2, 1)
        return dot_rows(mine, rows)

    grad_a = row_products(raw_own, rank_rows[:tokens]) + row_products(
        raw_other, rank_rows[tokens:]
    )
    grad_a = grad_a.reshape(16, 2, 64, 2 * rank)
    grad_a = lax.dynamic_index_in_dim(grad_a, mp % 2, 1, keepdims=False)
    grad_a = grad_a.reshape(4, 256, 2 * rank)
    whole, grad_a = reduce_stage(grad_a, gains, lambda v, step: shift_plane(v, 0, step))
    up_rows = add_next(up_rows, whole)
    grad_a = grad_a.reshape(4, 64, 2 * rank)
    whole, grad_a = reduce_stage(grad_a, whole, lambda v, step: shift_plane(v, 1, step))
    up_rows = add_next(up_rows, whole)
    gains = whole.astype(BF)
    gain_sum = jnp.zeros((16, 128), F32)
    for flip_core in range(2):
        send = lax.dynamic_slice_in_dim(gains, (mp % 2 ^ flip_core) * 16, 16, 0)
        for flip_z in range(2):
            gain_sum = gain_sum + turn(send, flip_z, flip_core).astype(F32)
    up_rows = add_next(up_rows)
    gain_sum = gain_sum.reshape(-1)
    gain_own = lax.dynamic_slice_in_dim(gain, mp * gain_sum.shape[0], gain_sum.shape[0])
    return (
        output[None],
        grad_a[:, :rank],
        up_rows[:, HD:],
        grad_a[:, rank:],
        up_rows[:, :HD],
        gain_sum / gain_own,
    )


def solution(mesh):
    return jax.shard_map(
        per_device,
        mesh=mesh,
        in_specs=(
            P("dp", "seq", "mp"),
            P(),
            P(("dp", "seq"), "mp"),
            P(("dp", "seq"), "mp"),
            P(("dp", "seq"), "mp"),
            P(),
            P(None, "mp"),
            P(),
            P(None, "mp"),
            P("dp", None),
            P("dp", "seq", "mp"),
        ),
        out_specs=(
            P("dp", "seq", "mp"),
            P(("dp", "seq", "mp"), None),
            P(None, "mp"),
            P(("dp", "seq", "mp"), None),
            P(None, "mp"),
            P("mp"),
        ),
        check_vma=False,
    )
```

```python
import functools

import jax
import jax.numpy as jnp
from jax import lax
from jax.experimental import pallas as pl
from jax.experimental.pallas import tpu as pltpu
from jax.sharding import PartitionSpec as P

HD = 128
EPS = 1e-05
ADAPTER_SCALE = 0.25
NEG_FILL = -1e30
BF = jnp.bfloat16
F32 = jnp.float32
VMEM_LIMIT = 56 * 1024 * 1024
VMEM_SMALL = 24 * 1024 * 1024
REL = (0, -1, 1, 2)
ROWS = 512


def shift(value, axis, step):
    if axis == "x":
        route = [(z * 4 + i, z * 4 + (i + step) % 4) for z in range(2) for i in range(4)]
        return lax.ppermute(value, "dp", route)
    if axis == "dp":
        return lax.ppermute(value, "dp", [(i, i ^ step) for i in range(8)])
    if axis == "zl":
        return lax.ppermute(value, "dp", [(i, (i + 4) % 8) for i in range(8)])
    if axis == "seq":
        return lax.ppermute(value, "seq", [(i, i ^ step) for i in range(4)])
    if axis == "y":
        return lax.ppermute(value, "seq", [(i, (i + step) % 4) for i in range(4)])
    return lax.ppermute(value, "mp", [(i, i ^ step) for i in range(4)])


def shift_plane(value, stage, step):
    route = []
    for z in range(2):
        for x in range(4):
            for y in range(4):
                for m in range(4):
                    to_x, to_y = x, y
                    if (m < 2) == (stage == 0):
                        to_y = (y + step) % 4
                    else:
                        to_x = (x + step) % 4
                    route.append(
                        (((z * 4 + x) * 4 + y) * 4 + m, ((z * 4 + to_x) * 4 + to_y) * 4 + m)
                    )
    return lax.ppermute(value, ("dp", "seq", "mp"), route)


def params(limit=VMEM_SMALL):
    return pltpu.CompilerParams(vmem_limit_bytes=limit)


def any_specs(count):
    return [pl.BlockSpec(memory_space=pl.ANY)] * count


def vmem_specs(count):
    return [pl.BlockSpec(memory_space=pltpu.VMEM)] * count


def assemble_kernel(*refs):
    pieces, outs = refs[:8], refs[-2:]
    rows = pieces[0].shape[0]
    for k, piece in enumerate(pieces):
        outs[k // 4][k % 4 * rows : (k % 4 + 1) * rows, :] = piece[...]


def assemble(pieces, *others):
    rows, columns = pieces[0].shape
    return pl.pallas_call(
        assemble_kernel,
        in_specs=vmem_specs(8) + any_specs(len(others)),
        out_specs=vmem_specs(2),
        out_shape=[jax.ShapeDtypeStruct((4 * rows, columns), BF)] * 2,
        compiler_params=params(VMEM_LIMIT),
        cost_estimate=pl.CostEstimate(
            flops=0, bytes_accessed=32 * rows * columns, transcendentals=0
        ),
        name="assemble",
    )(*pieces, *others)


def first_rings(shard):
    half = shard.shape[0] // 2
    pieces = []
    for part, axis in ((shard[:half], "x"), (shard[half:], "y")):
        pieces += [part] + [shift(part, axis, -step) for step in REL[1:]]
    return pieces


def second_rings(inners):
    blocks = []
    for inner, axis in zip(inners, ("y", "x")):
        before, after = shift(inner, axis, 1), shift(inner, axis, -1)
        blocks.append(
            [inner, before, after]
            + [shift(before[: ROWS // 2], axis, 1), shift(after[ROWS // 2 :], axis, -1)]
        )
    return blocks


def tie_kernel(*refs):
    del refs


def tie(value, *others):
    return pl.pallas_call(
        tie_kernel,
        in_specs=any_specs(1 + len(others)),
        out_specs=any_specs(1)[0],
        out_shape=jax.ShapeDtypeStruct(value.shape, value.dtype),
        input_output_aliases={0: 0},
        compiler_params=params(VMEM_LIMIT),
        name="tie",
    )(value, *others)


def corners(values):
    return jnp.concatenate([value[:16, :128] for value in values], axis=0)


def turn(value, flip_z, flip_core, stay=True):
    route = []
    for zl in range(2):
        for x in range(4):
            for zh in range(2):
                for c in range(2):
                    target = ((zh ^ flip_z) * 4 + x) * 4 + zl * 2 + (c ^ flip_core)
                    source = (zl * 4 + x) * 4 + zh * 2 + c
                    if stay or source != target:
                        route.append((source, target))
    return lax.ppermute(value, ("dp", "mp"), route)


def block_places(x, y, core):
    at = jnp.arange(32, dtype=jnp.int32)
    number = ((at // 16) ^ core) * 16 + at % 16
    order, shard = number % 2, number // 2
    inverse = jnp.array([0, 2, 3, 1], jnp.int32)
    by_x = inverse[(shard // 4 - x) % 4]
    by_y = inverse[(shard % 4 - y) % 4]
    outer = jnp.where(order == 0, by_y, by_x)
    inner = jnp.where(order == 0, by_x, by_y)
    place = order * 16 + outer * 4 + inner
    number_at = jnp.sum(jnp.where(place[None, :] == at[:, None], number[None, :], 0), axis=1)
    return number, place, number_at.astype(jnp.int32)


def fetch(sources, held, sems):
    copies = []
    begin = 0
    for k, source in enumerate(sources):
        rows = source.shape[0]
        copies.append(
            pltpu.make_async_copy(source, held.at[pl.ds(begin, rows)], sems.at[k])
        )
        begin += rows
    for copy in copies:
        copy.start()
    return copies


TILE = 256


def project_kernel(own, number, place, where, p0, p1, swapped, gain, a_both, other, *refs):
    del other
    if own:
        sources, (raw, out, taken, held, square, sems, take_sems) = refs[:-7], refs[-7:]
        a_rows = a_both
    else:
        sources, (raw, out, a_rows, taken, held, square, sems, take_sems) = refs[:-8], refs[-8:]

    tokens = p0.shape[0]

    def take(parts):
        return [pltpu.make_async_copy(p, taken.at[k], take_sems.at[k]) for k, p in enumerate(parts)]

    @pl.when(where[0] == (0 if own else 1))
    def _():
        for copy in take((p0, swapped.at[pl.ds(0, tokens)])):
            copy.start()

    @pl.when(where[0] != (0 if own else 1))
    def _():
        for copy in take((p1, swapped.at[pl.ds(tokens, tokens)])):
            copy.start()

    copies = fetch([source.at[:, pl.ds(0, held.shape[1])] for source in sources], held, sems)
    for copy in take((p0, swapped.at[pl.ds(0, tokens)])):
        copy.wait()
    per = taken.shape[2] // 128
    square[...] = jnp.zeros_like(square)
    for r in range(2):

        @pl.loop(0, per)
        def _(i):
            block = where[1] + number[r * per + i]
            target = pl.ds(pl.multiple_of(place[r * per + i] * 128, 128), 128)
            value = taken[r, :, pl.ds(pl.multiple_of(i * 128, 128), 128)].astype(F32)
            square[...] += value * value
            raw[:, target] = (value * gain[pl.ds(block, 1), :]).astype(BF)
            if not own:
                source = pl.ds(pl.multiple_of(block * 128, 128), 128)
                a_rows[target, :] = a_both[source, :]

    columns = held.shape[1]
    tile = TILE if columns % TILE == 0 else 128
    low = jnp.dot(raw[...], a_rows[...], preferred_element_type=F32)
    out[:, columns : columns + 128] = low.astype(out.dtype)
    total = jnp.broadcast_to(jnp.sum(square[...], axis=1, keepdims=True), square.shape)
    if not own:
        lead = total.astype(BF)
        lane = lax.broadcasted_iota(jnp.int32, square.shape, 1)
        total = jnp.where(lane == 0, lead.astype(F32), total - lead.astype(F32))
    out[:, columns + 128 :] = total.astype(out.dtype)
    for copy in copies:
        copy.wait()

    @pl.loop(0, columns // tile)
    def _(n):
        at = pl.ds(pl.multiple_of(n * tile, tile), tile)
        total = jnp.dot(raw[...], held[:, at], preferred_element_type=F32)
        out[:, at] = total.astype(out.dtype)


def project(own, columns, number, place, where, parts, gain, a_both, other, blocks):
    tokens, quarter = parts[0].shape
    count = len(blocks)
    outs = [
        jax.ShapeDtypeStruct((tokens, 2 * quarter), BF),
        jax.ShapeDtypeStruct((tokens, columns + 256), F32 if own else BF),
    ]
    if not own:
        outs.append(jax.ShapeDtypeStruct((2 * quarter, 128), BF))
    return pl.pallas_call(
        functools.partial(project_kernel, own),
        in_specs=[pl.BlockSpec(memory_space=pltpu.SMEM)] * 3
        + any_specs(3)
        + vmem_specs(2)
        + any_specs(1 + count),
        out_specs=vmem_specs(len(outs)),
        out_shape=outs,
        scratch_shapes=[
            pltpu.VMEM((2, tokens, quarter), BF),
            pltpu.VMEM((2 * quarter, columns), BF),
            pltpu.VMEM((tokens, 128), F32),
            pltpu.SemaphoreType.DMA((count,)),
            pltpu.SemaphoreType.DMA((2,)),
        ],
        compiler_params=params(VMEM_LIMIT),
        cost_estimate=pl.CostEstimate(
            flops=4 * tokens * quarter * columns,
            bytes_accessed=4 * quarter * (2 * tokens + columns),
            transcendentals=0,
        ),
        name="project",
    )(number, place, where, *parts, gain.reshape(-1, 128), a_both, other, *blocks)


def project_rest_kernel(raw, *refs):
    sources, (out, held, sems) = refs[:-3], refs[-3:]
    columns = held.shape[1]
    begin = sources[0].shape[1] - columns
    copies = fetch([source.at[:, pl.ds(begin, columns)] for source in sources], held, sems)
    for copy in copies:
        copy.wait()

    @pl.loop(0, columns // TILE)
    def _(n):
        at = pl.ds(pl.multiple_of(n * TILE, TILE), TILE)
        out[:, at] = jnp.dot(raw[...], held[:, at], preferred_element_type=F32).astype(BF)


def project_rest(columns, raw, blocks):
    tokens, width = raw.shape
    count = len(blocks)
    return pl.pallas_call(
        project_rest_kernel,
        in_specs=vmem_specs(1) + any_specs(count),
        out_specs=vmem_specs(1)[0],
        out_shape=jax.ShapeDtypeStruct((tokens, columns), BF),
        scratch_shapes=[pltpu.VMEM((width, columns), BF), pltpu.SemaphoreType.DMA((count,))],
        compiler_params=params(VMEM_LIMIT),
        cost_estimate=pl.CostEstimate(
            flops=2 * tokens * width * columns,
            bytes_accessed=2 * width * (tokens + columns),
            transcendentals=0,
        ),
        name="project_rest",
    )(raw, *blocks)


def combine_kernel(features, kept, received, rest, up, kv, query, low, inverse):
    columns = kv.shape[1] + query.shape[1]
    last = columns + 128
    begin = columns - rest.shape[1]
    lead = begin + 128
    square = kept[:, last : last + 1] + received[:, lead : lead + 1].astype(F32)
    square += received[:, lead + 1 : lead + 2].astype(F32)
    inv = lax.rsqrt(square * (1.0 / features) + EPS)
    inverse[...] = inv
    low_sum = kept[:, columns:last] + received[:, begin:lead].astype(F32)
    low_sum = (low_sum * inv).astype(BF)
    low[...] = low_sum
    both = jnp.concatenate([received[:, :begin], rest[...]], axis=1)
    total = (kept[:, :columns] + both.astype(F32)) * inv
    total += ADAPTER_SCALE * jnp.dot(low_sum, up[...], preferred_element_type=F32)
    kv[...] = total[:, : 2 * HD].astype(BF)
    query[...] = total[:, 2 * HD :].astype(BF)


def combine(features, kept, received, rest, up):
    tokens = kept.shape[0]
    columns = up.shape[1]
    return pl.pallas_call(
        functools.partial(combine_kernel, features),
        in_specs=vmem_specs(4),
        out_specs=vmem_specs(4),
        out_shape=[
            jax.ShapeDtypeStruct((tokens, 2 * HD), BF),
            jax.ShapeDtypeStruct((tokens, columns - 2 * HD), BF),
            jax.ShapeDtypeStruct((tokens, 128), BF),
            jax.ShapeDtypeStruct((tokens, 1), F32),
        ],
        compiler_params=params(),
        cost_estimate=pl.CostEstimate(
            flops=2 * tokens * 128 * columns,
            bytes_accessed=8 * tokens * columns,
            transcendentals=0,
        ),
        name="combine",
    )(kept, received, rest, up)


def gain_kernel(count, numbers, *refs):
    packs, inverse, a_rows, raws = (refs[:3], refs[3:6]), refs[6], refs[7], refs[8:10]
    sources, rest = refs[10 : 10 + count], refs[10 + count :]
    out, held, rows, grads, inv, sems, row_sems = rest
    tokens = raws[0].shape[0]
    columns = held.shape[1]
    spans = []
    for source in sources:
        begin = spans[-1][1] if spans else 0
        spans.append((begin, begin + source.shape[0]))
    copies = fetch(sources, held, sems)
    row_copies = []
    for k, (begin, end) in enumerate(spans):
        at = pl.ds(begin, end - begin)
        for pack in range(2):
            copy = pltpu.make_async_copy(
                raws[pack].at[:, at], rows.at[pl.ds(pack * tokens, tokens), at], row_sems.at[pack, k]
            )
            copy.start()
            row_copies.append(copy)
    for pack, (dkv, dq, ranks) in enumerate(packs):
        at = slice(pack * tokens, (pack + 1) * tokens)
        grads[at, : 2 * HD] = dkv[...]
        grads[at, 2 * HD : columns] = dq[...]
        grads[at, columns:] = ranks[...]
    inv[...] = jnp.broadcast_to(inverse[...], inv.shape)
    nt = (((1,), (1,)), ((), ()))
    for k, (begin, end) in enumerate(spans):
        at = slice(begin, end)
        copies[k].wait()
        row_copies[2 * k].wait()
        row_copies[2 * k + 1].wait()
        term = lax.dot_general(grads[:, :columns], held[at, :], nt, preferred_element_type=F32)
        term += lax.dot_general(grads[:, columns:], a_rows[at, :], nt, preferred_element_type=F32)
        term *= inv[:, : end - begin] * rows[:, at].astype(F32)
        sums = jnp.sum(term, axis=0, keepdims=True)
        for s in range((end - begin) // 128):
            out[pl.ds(numbers[begin // 128 + s], 1), :] = sums[:, s * 128 : (s + 1) * 128]


def gain_part(numbers, packs, inverse, raws, a_rows, blocks):
    tokens, width = raws[0].shape
    columns = blocks[0].shape[1]
    count = len(blocks)
    return pl.pallas_call(
        functools.partial(gain_kernel, count),
        in_specs=[pl.BlockSpec(memory_space=pltpu.SMEM)]
        + vmem_specs(8)
        + any_specs(2 + count),
        out_specs=vmem_specs(1)[0],
        out_shape=jax.ShapeDtypeStruct((width // 128, 128), F32),
        scratch_shapes=[
            pltpu.VMEM((width, columns), BF),
            pltpu.VMEM((2 * tokens, width), BF),
            pltpu.VMEM((2 * tokens, columns + 128), BF),
            pltpu.VMEM((2 * tokens, ROWS), F32),
            pltpu.SemaphoreType.DMA((count,)),
            pltpu.SemaphoreType.DMA((2, count)),
        ],
        compiler_params=params(VMEM_LIMIT),
        cost_estimate=pl.CostEstimate(
            flops=4 * tokens * width * columns,
            bytes_accessed=2 * width * (2 * tokens + columns),
            transcendentals=0,
        ),
        name="gain_part",
    )(numbers, *packs[0], *packs[1], inverse, a_rows, *raws, *blocks)


def unite_kernel(partner, dq0, dq1, dkv0, dkv1, returned, up_query, up_value, dq, dkv, ranks):
    rank = up_query.shape[0]
    half = returned.shape[0]
    for h in range(dq.shape[1] // HD):
        source = (dq0, dq1)[h % 2]
        dq[:, h * HD : (h + 1) * HD] = source[:, h // 2 * HD : (h // 2 + 1) * HD]
    if partner:
        dkv[...] = dkv0[...]
    else:
        dkv[:half, :] = (dkv0[:half, :] + dkv1[:half, :]).astype(BF)
        dkv[half:, :] = (dkv0[half:, :] + dkv1[half:, :] + returned[...].astype(F32)).astype(BF)
    nt = (((1,), (1,)), ((), ()))
    of_query = lax.dot_general(dq[...], up_query[...], nt, preferred_element_type=F32)
    of_value = lax.dot_general(dkv[:, HD:], up_value[...], nt, preferred_element_type=F32)
    ranks[:, :rank] = (ADAPTER_SCALE * of_query).astype(BF)
    ranks[:, rank:] = (ADAPTER_SCALE * of_value).astype(BF)


def unite(partner, dq0, dq1, dkv0, dkv1, returned, up_query, up_value):
    tokens, columns = dq0.shape
    return pl.pallas_call(
        functools.partial(unite_kernel, partner),
        in_specs=vmem_specs(7),
        out_specs=vmem_specs(3),
        out_shape=[
            jax.ShapeDtypeStruct((tokens, 2 * columns), BF),
            jax.ShapeDtypeStruct((tokens, 2 * HD), BF),
            jax.ShapeDtypeStruct((tokens, 128), BF),
        ],
        compiler_params=params(),
        cost_estimate=pl.CostEstimate(
            flops=4 * tokens * columns * 64, bytes_accessed=8 * tokens * columns, transcendentals=0
        ),
        name="unite",
    )(dq0, dq1, dkv0, dkv1, returned, up_query, up_value)


def attend_kernel(odd, query, kv, prev, grads, docs_row, docs_col, *refs):
    if odd:
        out, dq, dkv, dprev, dk, dv = refs
    else:
        out, dq, dkv, dk, dv = refs
    tokens = kv.shape[0]
    half = tokens // 2
    scale = HD ** (-0.5)
    if odd:
        keys = jnp.concatenate([prev[:, :HD], kv[:, :HD]], axis=0)
        values = jnp.concatenate([prev[:, HD:], kv[:, HD:]], axis=0)
        spans = ((0, tokens), (tokens, tokens + half))
        doc_keys = docs_col[...]
        before = half
    else:
        keys, values = kv[:, :HD], kv[:, HD:]
        spans = ((0, half), (0, tokens))
        doc_keys = docs_col[half:, :]
        before = 0
    dk[...] = jnp.zeros_like(dk)
    dv[...] = jnp.zeros_like(dv)
    for part, (low, high) in enumerate(spans):
        rows = slice(part * half, (part + 1) * half)
        key_at = lax.broadcasted_iota(jnp.int32, (high - low, half), 0) + (low - before)
        query_at = lax.broadcasted_iota(jnp.int32, (high - low, half), 1) + part * half
        allowed = (doc_keys[low:high, :] == docs_row[:, rows]) & (key_at <= query_at)
        key, value = keys[low:high], values[low:high]
        for h in range(dq.shape[1] // HD):
            source = slice((2 * h + odd) * HD, (2 * h + odd + 1) * HD)
            target = slice(h * HD, (h + 1) * HD)
            row_query, cot = query[rows, source], grads[rows, source]
            scores = (
                lax.dot_general(
                    key, row_query, (((1,), (1,)), ((), ())), preferred_element_type=F32
                )
                * scale
            )
            scores = jnp.where(allowed, scores, NEG_FILL)
            expo = jnp.exp(scores - jnp.max(scores, axis=0, keepdims=True))
            probs = expo * (1.0 / jnp.sum(expo, axis=0, keepdims=True))
            probs_low = probs.astype(BF)
            output = lax.dot_general(
                value, probs_low, (((0,), (0,)), ((), ())), preferred_element_type=F32
            )
            out[rows, target] = output.T.astype(BF)
            dprob = lax.dot_general(
                value, cot, (((1,), (1,)), ((), ())), preferred_element_type=F32
            )
            delta = jnp.sum(probs_low.astype(F32) * dprob, axis=0, keepdims=True)
            dscore = (probs * (dprob - delta)).astype(BF)
            dquery = lax.dot_general(
                key, dscore, (((0,), (0,)), ((), ())), preferred_element_type=F32
            )
            dq[rows, target] = (dquery * scale).T.astype(BF)
            dk[low:high, :] += jnp.dot(dscore, row_query, preferred_element_type=F32)
            dv[low:high, :] += jnp.dot(probs_low, cot, preferred_element_type=F32)
    dkv[:, :HD] = dk[before:, :] * scale
    dkv[:, HD:] = dv[before:, :]
    if odd:
        dprev[:, :HD] = (dk[:before, :] * scale).astype(BF)
        dprev[:, HD:] = dv[:before, :].astype(BF)


def attend(odd, query, kv, prev, grads, docs_row, docs_col):
    tokens, columns = grads.shape
    half = tokens // 2
    span = tokens + half if odd else tokens
    outs = [
        jax.ShapeDtypeStruct((tokens, columns // 2), BF),
        jax.ShapeDtypeStruct((tokens, columns // 2), BF),
        jax.ShapeDtypeStruct((tokens, 2 * HD), F32),
    ]
    if odd:
        outs.append(jax.ShapeDtypeStruct((half, 2 * HD), BF))
    return pl.pallas_call(
        functools.partial(attend_kernel, odd),
        in_specs=vmem_specs(6),
        out_specs=vmem_specs(len(outs)),
        out_shape=outs,
        scratch_shapes=[pltpu.VMEM((span, HD), F32)] * 2,
        compiler_params=params(),
        cost_estimate=pl.CostEstimate(
            flops=5 * tokens * tokens * columns,
            bytes_accessed=4 * tokens * columns,
            transcendentals=tokens * tokens * columns // (2 * HD),
        ),
        name="attend",
    )(query, kv, prev, grads, docs_row, docs_col)


def dot_rows(left, right):
    return lax.dot_general(left, right, (((0,), (0,)), ((), ())), preferred_element_type=F32)


def dot_cols(left, right):
    return lax.dot_general(left, right, (((1,), (1,)), ((), ())), preferred_element_type=F32)


def sum_heads(value):
    total = value.astype(F32)
    for step in (1, 2, 3):
        total = total + shift(value, "mp", step).astype(F32)
    return total


def reduce_stage(chunks, whole, move):
    count = whole.shape[0]
    total = jnp.concatenate([whole, chunks[0]], axis=0)
    low = whole.astype(BF)
    for i in (1, 2, 3):
        packed = jnp.concatenate([low, chunks[i].astype(BF)], axis=0)
        total = total + move(packed, REL[i]).astype(F32)
    return total[:count], total[count:]


def per_device(
    hidden,
    gain,
    query_frozen_weight,
    w_key,
    value_frozen_weight,
    a_query,
    query_up_weight,
    a_value,
    value_up_weight,
    doc_ids,
    d_out,
):
    tokens = hidden.shape[1]
    half = tokens // 2
    dp, seq, mp = lax.axis_index("dp"), lax.axis_index("seq"), lax.axis_index("mp")
    pair, high = dp // 4, mp // 2
    own = hidden[0]
    turned = turn(own, 0, 0, stay=False)
    weights = jnp.concatenate([w_key, value_frozen_weight, query_frozen_weight], axis=1)
    pieces = first_rings(weights)
    a_both = jnp.concatenate([a_query, a_value], axis=1)
    inners = assemble(pieces, a_both)
    turned = jnp.where(pair == high, own, tie(turned, corners(inners)))
    turned_high = shift(turned, "mp", 2)
    first, second = second_rings(inners)
    turned_high = tie(turned_high, corners(first[1:3] + second[1:3]))
    swapped = shift(jnp.concatenate([turned, turned_high], axis=0), "mp", 1)
    hidden_parts = [turned, turned_high, swapped]
    number, place, number_at = block_places(dp % 4, seq, mp % 2)
    where = jnp.stack([jnp.where(pair == high, 0, 1), pair * 32]).astype(jnp.int32)
    blocks = first + second
    columns = weights.shape[1]
    lead = 3 * columns // 5
    raw_other, sent, a_rows = project(
        False, lead, number, place, where, hidden_parts, gain, a_both, a_both, blocks
    )
    received = shift(sent, "zl", 1)
    sent_rest = project_rest(columns - lead, raw_other, blocks)
    received_rest = shift(sent_rest, "zl", 1)
    raw_own, kept = project(
        True, columns, number, place, where, hidden_parts, gain, a_rows, sent_rest, blocks
    )
    rank = query_up_weight.shape[0]
    up = jnp.concatenate(
        [
            jnp.concatenate([jnp.zeros((rank, 2 * HD), BF), query_up_weight], axis=1),
            jnp.concatenate(
                [jnp.zeros((rank, HD), BF), value_up_weight, jnp.zeros_like(query_up_weight)], axis=1
            ),
        ],
        axis=0,
    )
    kv, query, low, inverse = combine(gain.shape[0], kept, received, received_rest, up)
    inverse_row = shift(tie(inverse.reshape(-1, 128), kv), "zl", 1)
    prev = lax.ppermute(kv[half:], "seq", [(i, i + 1) for i in range(3)])

    docs = doc_ids[0]
    begin = seq * tokens
    own_docs = lax.dynamic_slice_in_dim(docs, begin, tokens)
    prev_docs = lax.dynamic_slice_in_dim(docs, jnp.maximum(begin - half, 0), half)
    prev_docs = jnp.where(seq > 0, prev_docs, -1)
    ext_docs = jnp.concatenate([prev_docs, own_docs])
    masks = (own_docs[None, :], ext_docs[:, None])
    out_even, dq_even, dkv_even = attend(0, query, kv, kv[half:], d_out[0], *masks)
    dq_even_other = shift(dq_even, "zl", 1)
    out_odd, dq_odd, dkv_odd, dprev = attend(1, query, kv, prev, d_out[0], *masks)
    dq_odd_other = shift(dq_odd, "zl", 1)
    returned = lax.ppermute(dprev, "seq", [(i + 1, i) for i in range(3)])
    dq, dkv, ranks_own = unite(
        False, dq_even, dq_odd, dkv_even, dkv_odd, returned, query_up_weight, value_up_weight
    )
    dkv_moved = shift(dkv, "zl", 1)
    dq_other, dkv_other, ranks_other = unite(
        True,
        dq_even_other,
        dq_odd_other,
        dkv_moved,
        dkv_moved,
        returned,
        query_up_weight,
        value_up_weight,
    )
    output = []
    for h in range(out_even.shape[1] // HD):
        at = slice(h * HD, (h + 1) * HD)
        output += [out_even[:, at], out_odd[:, at]]
    output = jnp.concatenate(output, axis=1)
    inverses = (inverse, tie(inverse_row, dq_other).reshape(-1, 1))
    rank_rows = sum_heads(jnp.concatenate([ranks_own, ranks_other], axis=0))
    rank_rows = (rank_rows * jnp.concatenate(inverses, axis=0)).astype(BF)

    up_rows = ADAPTER_SCALE * jnp.concatenate(
        [dot_rows(low[:, rank:], dkv[:, HD:]), dot_rows(low[:, :rank], dq)], axis=1
    )
    up_rows = tie(up_rows, dkv)
    turns = iter((("dp", 1), ("dp", 2), ("seq", 1), ("seq", 2), ("dp", 4)))

    def add_next(rows, *others):
        axis, step = next(turns)
        moved = shift(rows.astype(BF), axis, step)
        if others:
            moved = tie(moved, *others)
        return rows + moved.astype(F32)

    up_rows = add_next(up_rows, corners([dkv_moved]))
    up_rows = add_next(up_rows, dq_other)
    packs = ((dkv, dq, ranks_own), (dkv_other, dq_other, ranks_other))
    gains = gain_part(
        number_at, packs, jnp.concatenate(inverses, axis=0), (raw_own, raw_other), a_rows, blocks
    )
    up_rows = add_next(up_rows, gains)

    def row_products(raw, rows):
        width = raw.shape[1]
        mine = lax.dynamic_slice_in_dim(raw, high * (width // 2), width // 2, 1)
        return dot_rows(mine, rows)

    grad_a = row_products(raw_own, rank_rows[:tokens]) + row_products(
        raw_other, rank_rows[tokens:]
    )
    grad_a = grad_a.reshape(16, 2, 64, 2 * rank)
    grad_a = lax.dynamic_index_in_dim(grad_a, mp % 2, 1, keepdims=False)
    grad_a = grad_a.reshape(4, 256, 2 * rank)
    whole, grad_a = reduce_stage(grad_a, gains, lambda v, step: shift_plane(v, 0, step))
    up_rows = add_next(up_rows, whole)
    grad_a = grad_a.reshape(4, 64, 2 * rank)
    whole, grad_a = reduce_stage(grad_a, whole, lambda v, step: shift_plane(v, 1, step))
    up_rows = add_next(up_rows, whole)
    gains = whole.astype(BF)
    gain_sum = jnp.zeros((16, 128), F32)
    for flip_core in range(2):
        send = lax.dynamic_slice_in_dim(gains, (mp % 2 ^ flip_core) * 16, 16, 0)
        for flip_z in range(2):
            gain_sum = gain_sum + turn(send, flip_z, flip_core).astype(F32)
    gain_sum = gain_sum.reshape(-1)
    gain_own = lax.dynamic_slice_in_dim(gain, mp * gain_sum.shape[0], gain_sum.shape[0])
    return (
        output[None],
        grad_a[:, :rank],
        up_rows[:, HD:],
        grad_a[:, rank:],
        up_rows[:, :HD],
        gain_sum / gain_own,
    )


def solution(mesh):
    return jax.shard_map(
        per_device,
        mesh=mesh,
        in_specs=(
            P("dp", "seq", "mp"),
            P(),
            P(("dp", "seq"), "mp"),
            P(("dp", "seq"), "mp"),
            P(("dp", "seq"), "mp"),
            P(),
            P(None, "mp"),
            P(),
            P(None, "mp"),
            P("dp", None),
            P("dp", "seq", "mp"),
        ),
        out_specs=(
            P("dp", "seq", "mp"),
            P(("dp", "seq", "mp"), None),
            P(None, "mp"),
            P(("dp", "seq", "mp"), None),
            P(None, "mp"),
            P("mp"),
        ),
        check_vma=False,
    )
```
